32 devices in a mesh: grp: 8 (over z, x), tp: 4 (over y, core).
Axes of the slice: x: 2, y: 2, z: 4, core: 2. Of those that a mesh axis runs over, the one named last changes fastest.
Arguments:
- latents: bfloat16 [128, 128, 1024], P('grp', None, 'tp'), may hold values from -6 to 6
- skip_latents: bfloat16 [128, 128, 1024], P('grp', None, 'tp'), may hold values from -24 to 24
- points: bfloat16 [16384, 1024], P('grp'), may hold values from -6 to 6
- neighbours: int32 [128, 4], P('grp'), may hold values from 0 to 127, as said below
- block_lengths: int32 [128], replicated, may hold values from 32 to 128
- latent_embed: float32 [128, 1024], P(None, 'tp'), may hold values from -4 to 4
- gain_cross: float32 [1024], replicated, may hold values from 0.2 to 3
- query_cross: bfloat16 [1024, 1024], P(None, 'tp'), may hold values from -0.1875 to 0.1875
- key_cross: bfloat16 [1024, 1024], P(None, 'tp'), may hold values from -0.1875 to 0.1875
- value_cross: bfloat16 [1024, 1024], P(None, 'tp'), may hold values from -0.1875 to 0.1875
- output_cross: bfloat16 [1024, 1024], P('tp'), may hold values from -0.75 to 0.75
- bias_cross: float32 [1024], P('tp'), may hold values from -2 to 2
- gain_self: float32 [1024], replicated, may hold values from 0.2 to 3
- query_self: bfloat16 [1024, 1024], P(None, 'tp'), may hold values from -0.1875 to 0.1875
- key_self: bfloat16 [1024, 1024], P(None, 'tp'), may hold values from -0.1875 to 0.1875
- value_self: bfloat16 [1024, 1024], P(None, 'tp'), may hold values from -0.1875 to 0.1875
- output_self: bfloat16 [1024, 1024], P('tp'), may hold values from -0.75 to 0.75
- bias_self: float32 [1024], P('tp'), may hold values from -2 to 2
- gain_mlp: float32 [1024], replicated, may hold values from 0.2 to 3
- hidden_weight: bfloat16 [1024, 4096], P(None, 'tp'), may hold values from -0.1875 to 0.1875
- hidden_bias: float32 [4096], P('tp'), may hold values from -3 to 3
- output_weight: bfloat16 [4096, 1024], P('tp'), may hold values from -0.09375 to 0.09375
- output_bias: float32 [1024], P('tp'), may hold values from -2 to 2
- cotangent: bfloat16 [128, 128, 1024], P('grp', None, 'tp'), may hold values from -6 to 6
Outputs:
- block_out: float32 [128, 128, 1024], P('grp', None, 'tp')
- group_norms: float32 [128], replicated
- latents_grad: float32 [128, 128, 1024], P('grp', None, 'tp')
- embed_grad: float32 [128, 1024], P(None, 'tp')
- gain_cross_grad: float32 [1024], P('tp')
- query_cross_grad: float32 [1024, 1024], P(None, 'tp')
- key_cross_grad: float32 [1024, 1024], P(None, 'tp')
- value_cross_grad: float32 [1024, 1024], P(None, 'tp')
- output_cross_grad: float32 [1024, 1024], P('tp')
- bias_cross_grad: float32 [1024], P('tp')
- gain_self_grad: float32 [1024], P('tp')
- query_self_grad: float32 [1024, 1024], P(None, 'tp')
- key_self_grad: float32 [1024, 1024], P(None, 'tp')
- value_self_grad: float32 [1024, 1024], P(None, 'tp')
- output_self_grad: float32 [1024, 1024], P('tp')
- bias_self_grad: float32 [1024], P('tp')
- gain_mlp_grad: float32 [1024], P('tp')
- hidden_weight_grad: float32 [1024, 4096], P(None, 'tp')
- hidden_bias_grad: float32 [4096], P('tp')
- output_weight_grad: float32 [4096, 1024], P('tp')
- output_bias_grad: float32 [1024], P('tp')
The draws below stay inside these ranges and needn't reach their ends.
Inputs may be any that keep to these rules, and one draw needn't show every extreme that they name: The neighbours of group g lie among the 16 blocks that start at block (g // 16) * 16 - 16 // 2, counted cyclically modulo 128; the first of them lies among the first 8 of these.
All inputs are finite; a program needn't handle non-finite values.
Results may differ from the reference program's by a relative error of at most 0.025.
Values may be sent and summed in bfloat16 or wider, within the bound.
No kernel may reach another device: no remote copies, remote signals or barrier semaphores. Data moves between devices by JAX's collectives and lax.ppermute only.
A program may use at most 192 MiB of HBM per device.

```python
import jax
import jax.numpy as jnp
from jax import lax

D = 1024
H = 8
HD = 128
FF = 4096
LAT = 128
PB = 128
NB = 4
GRP_DEV = 16
BPD = 16
GROUPS = 128
BLOCKS = 128


def draw_neighbours(key, part):
    key = jax.random.fold_in(key, 5)
    first_key, rest_key = jax.random.split(key)
    first_offset = jax.random.randint(first_key, (GROUPS, 1), 0, BPD // 2)
    rest_offsets = jax.random.randint(rest_key, (GROUPS, NB - 1), 0, BPD)
    offsets = jnp.concatenate([first_offset, rest_offsets], axis=1)
    owners = jnp.arange(GROUPS, dtype=jnp.int32) // GRP_DEV
    first_block = owners * BPD - BPD // 2
    return ((first_block[:, None] + offsets) % BLOCKS).astype(jnp.int32)


def rising_rows(key, start, stop):
    place = jnp.arange(LAT, dtype=jnp.float32) / (LAT - 1)
    return (start + (stop - start) * place)[:, None, None]


def draw_skip_latents(key, part):
    key = jax.random.fold_in(key, 11)
    noise = jax.random.normal(key, (LAT, GROUPS, D), jnp.float32)
    values = jnp.clip(noise, -6.0, 6.0) * rising_rows(key, 0.5, 4.0)
    return jnp.clip(values, -24.0, 24.0).astype(jnp.bfloat16)


def rising_gain(key, start, stop):
    place = jnp.arange(D, dtype=jnp.float32) / (D - 1)
    profile = jnp.exp(jnp.log(start) + (jnp.log(stop) - jnp.log(start)) * place)
    rough = jax.random.uniform(key, (D,), jnp.float32, 0.8, 1.2)
    return profile * rough


def draw_gain_cross(key, part):
    key = jax.random.fold_in(key, 21)
    return rising_gain(key, 0.4, 2.4)


def draw_gain_self(key, part):
    key = jax.random.fold_in(key, 22)
    return rising_gain(key, 0.4, 2.4)


def draw_gain_mlp(key, part):
    key = jax.random.fold_in(key, 23)
    return rising_gain(key, 0.4, 2.4)


def set_ends(drawn, own_key, smallest, top_value):
    longest = drawn.shape.index(max(drawn.shape))
    spots = []
    for shift in (0, 1):
        where = [jax.random.randint(jax.random.fold_in(own_key, axis), (), 0, length) for axis, length in enumerate(drawn.shape)]
        where[longest] = (where[longest] + shift) % drawn.shape[longest]
        spots.append(tuple(where))
    return drawn.at[spots[0]].set(smallest).at[spots[1]].set(top_value)


def level_of(key, extent, cuts, low, top_value):
    level, own = 1.0, jax.random.fold_in(key, 6)
    for dim, parts in cuts:
        draws = jnp.exp(jax.random.uniform(jax.random.fold_in(own, dim), (parts,), jnp.float32, low / len(cuts), top_value / len(cuts)))
        level = level * jnp.repeat(draws, extent[dim] // parts).reshape([-1 if axis == dim else 1 for axis in range(len(extent))])
    return level


def gaussian(rng, extent, scale, limit, cuts=(), kind=jnp.bfloat16):
    drawn = jax.random.normal(rng, extent, jnp.float32) * scale
    if len(cuts) > 0:
        drawn = level_of(rng, extent, cuts, -0.22, 0.18) * drawn
    return jnp.clip(drawn, min=-limit, max=limit).astype(kind)


def setup_inputs(seed: int = 0) -> dict:
    key_list = jax.random.split(jax.random.key(seed), 25)
    return {
        "latents": gaussian(key_list[0], (LAT, GROUPS, D), 1.0, 6.0, ((0, 8), (2, 4))),
        "skip_latents": draw_skip_latents(jax.random.fold_in(key_list[24], 71), 0),
        "points": gaussian(key_list[2], (BLOCKS * PB, D), 1.0, 6.0, ((0, 8),)),
        "neighbours": draw_neighbours(jax.random.fold_in(key_list[24], 71), 0),
        "block_lengths": set_ends(jax.random.randint(key_list[4], (BLOCKS,), PB // 4, PB + 1), jax.random.fold_in(key_list[4], 1), PB // 4, PB).astype(jnp.int32),
        "latent_embed": gaussian(key_list[5], (LAT, D), 0.5, 4.0, ((1, 4),), jnp.float32),
        "gain_cross": draw_gain_cross(jax.random.fold_in(key_list[24], 71), 0),
        "query_cross": gaussian(key_list[7], (D, D), D ** -0.5, 0.1875, ((1, 4),)),
        "key_cross": gaussian(key_list[8], (D, D), D ** -0.5, 0.1875, ((1, 4),)),
        "value_cross": gaussian(key_list[9], (D, D), D ** -0.5, 0.1875, ((1, 4),)),
        "output_cross": gaussian(key_list[10], (D, D), (D // 16) ** -0.5, 0.75, ((0, 4),)),
        "bias_cross": gaussian(key_list[11], (D,), 0.3, 2.0, ((0, 4),), jnp.float32),
        "gain_self": draw_gain_self(jax.random.fold_in(key_list[24], 71), 0),
        "query_self": gaussian(key_list[13], (D, D), D ** -0.5, 0.1875, ((1, 4),)),
        "key_self": gaussian(key_list[14], (D, D), D ** -0.5, 0.1875, ((1, 4),)),
        "value_self": gaussian(key_list[15], (D, D), D ** -0.5, 0.1875, ((1, 4),)),
        "output_self": gaussian(key_list[16], (D, D), (D // 16) ** -0.5, 0.75, ((0, 4),)),
        "bias_self": gaussian(key_list[17], (D,), 0.3, 2.0, ((0, 4),), jnp.float32),
        "gain_mlp": draw_gain_mlp(jax.random.fold_in(key_list[24], 71), 0),
        "hidden_weight": gaussian(key_list[19], (D, FF), D ** -0.5, 0.1875, ((1, 4),)),
        "hidden_bias": gaussian(key_list[20], (FF,), 0.5, 3.0, ((0, 4),), jnp.float32),
        "output_weight": gaussian(key_list[21], (FF, D), FF ** -0.5, 0.09375, ((0, 4),)),
        "output_bias": gaussian(key_list[22], (D,), 0.3, 2.0, ((0, 4),), jnp.float32),
        "cotangent": gaussian(key_list[23], (LAT, GROUPS, D), 1.0, 6.0, ((0, 8), (2, 4))),
    }


EPS = 1e-05
NEG = -1e+30
HIGH = lax.Precision.HIGHEST

@jax.custom_vjp
def low(v):
    return lax.optimization_barrier(v.astype(jnp.bfloat16)).astype(jnp.float32)

@jax.custom_vjp
def low_back(v):
    return v

def low_keep(v):
    return (low(v), None)

def low_pass(kept, grad):
    return (grad,)

def back_keep(v):
    return (v, None)

def back_low(kept, grad):
    return (low(grad),)
low.defvjp(low_keep, low_pass)
low_back.defvjp(back_keep, back_low)

def matmul(left, right):
    return jnp.dot(left, right, precision=HIGH)

def layer_norm(value, gain):
    centre = lax.optimization_barrier(jnp.mean(value, axis=-1, keepdims=True))
    spread = lax.optimization_barrier(jnp.mean(jnp.square(value - centre), axis=-1, keepdims=True))
    return (value - centre) * lax.rsqrt(spread + EPS) * gain

def attention(queries, keys, values, live):
    scores = low_back(jnp.einsum('qhd,khd->hqk', queries, keys, precision=HIGH) * HD ** (-0.5))
    scores = jnp.where(live[None, None, :], scores, NEG)
    probs = jax.nn.softmax(scores, axis=-1)
    return low_back(low(jnp.einsum('hqk,khd->qhd', low(probs), values, precision=HIGH)))

def reference(latents, skip_latents, points, neighbours, block_lengths, latent_embed, gain_cross, query_cross, key_cross, value_cross, output_cross, bias_cross, gain_self, query_self, key_self, value_self, output_self, bias_self, gain_mlp, hidden_weight, hidden_bias, output_weight, output_bias, cotangent):
    floats = jnp.float32
    point_rows = points.astype(floats)
    live_points = jnp.arange(PB, dtype=jnp.int32)[None, :] < block_lengths[:, None]
    all_live = jnp.ones((LAT,), dtype=bool)

    def forward(entry, embed, gcross, wqc, wkc, wvc, woc, bcross, gself, wqs, wks, wvs, wos, bself, gmlp, whid, bhid, wout, bout):
        stream = (jnp.transpose(entry, (1, 0, 2)) + embed).reshape(GROUPS * LAT, D)
        normed = low(layer_norm(stream, gcross))
        cross_q = low_back(low(matmul(normed, wqc))).reshape(GROUPS, LAT, H, HD)
        cross_k = low_back(low(matmul(point_rows, wkc))).reshape(BLOCKS, PB, H, HD)
        cross_v = low_back(low(matmul(point_rows, wvc))).reshape(BLOCKS, PB, H, HD)

        def one_group(item):
            group_q, group_ids = item
            group_k = cross_k[group_ids].reshape(NB * PB, H, HD)
            group_v = cross_v[group_ids].reshape(NB * PB, H, HD)
            group_live = live_points[group_ids].reshape(NB * PB)
            return attention(group_q, group_k, group_v, group_live)
        cross_o = lax.map(jax.checkpoint(one_group), (cross_q, neighbours))
        stream = stream + low_back(matmul(cross_o.reshape(GROUPS * LAT, D), woc)) + bcross
        normed = low(layer_norm(stream, gself))
        self_q = low_back(low(matmul(normed, wqs))).reshape(GROUPS, LAT, H, HD)
        self_k = low_back(low(matmul(normed, wks))).reshape(GROUPS, LAT, H, HD)
        self_v = low_back(low(matmul(normed, wvs))).reshape(GROUPS, LAT, H, HD)
        self_o = jax.vmap(attention, in_axes=(0, 0, 0, None))(self_q, self_k, self_v, all_live)
        stream = stream + low_back(matmul(self_o.reshape(GROUPS * LAT, D), wos)) + bself
        normed = low(layer_norm(stream, gmlp))
        before = low_back(matmul(normed, whid) + bhid)
        activation = low(jax.nn.gelu(before))
        stream = stream + low_back(matmul(activation, wout)) + bout
        return jnp.transpose(stream.reshape(GROUPS, LAT, D), (1, 0, 2))
    params = (latents.astype(floats), latent_embed, gain_cross, query_cross.astype(floats), key_cross.astype(floats), value_cross.astype(floats), output_cross.astype(floats), bias_cross, gain_self, query_self.astype(floats), key_self.astype(floats), value_self.astype(floats), output_self.astype(floats), bias_self, gain_mlp, hidden_weight.astype(floats), hidden_bias, output_weight.astype(floats), output_bias)
    core, pullback = jax.vjp(forward, *params)
    block_out = core + skip_latents.astype(floats)
    group_norms = jnp.sqrt(lax.optimization_barrier(jnp.mean(jnp.square(block_out), axis=(0, 2))))
    latents_grad, embed_grad, gain_cross_grad, query_cross_grad, key_cross_grad, value_cross_grad, output_cross_grad, bias_cross_grad, gain_self_grad, query_self_grad, key_self_grad, value_self_grad, output_self_grad, bias_self_grad, gain_mlp_grad, hidden_weight_grad, hidden_bias_grad, output_weight_grad, output_bias_grad = pullback(cotangent.astype(floats))
    return (block_out, group_norms, latents_grad, embed_grad, gain_cross_grad, query_cross_grad, key_cross_grad, value_cross_grad, output_cross_grad, bias_cross_grad, gain_self_grad, query_self_grad, key_self_grad, value_self_grad, output_self_grad, bias_self_grad, gain_mlp_grad, hidden_weight_grad, hidden_bias_grad, output_weight_grad, output_bias_grad)
```

```python
import functools

import jax
import jax.numpy as jnp
from jax import lax
from jax.experimental import pallas as pl
from jax.experimental.pallas import tpu as pltpu
from jax.sharding import PartitionSpec as P

HD = 128
PB = 128
NB = 4
EPS = 1e-05
NEG = -1e30
SCALE = HD ** (-0.5)
BF = jnp.bfloat16
F32 = jnp.float32
VMEM_BYTES = 58 * 2**20

ANY = pl.BlockSpec(memory_space=pl.ANY)
VM = pl.BlockSpec(memory_space=pltpu.VMEM)
SM = pl.BlockSpec(memory_space=pltpu.SMEM)


def shape(dims, kind):
    return jax.ShapeDtypeStruct(dims, kind)


def params():
    return pltpu.CompilerParams(vmem_limit_bytes=VMEM_BYTES)


def nn(left, right):
    return lax.dot_general(left, right, (((1,), (0,)), ((), ())), preferred_element_type=F32)


def nt(left, right):
    return lax.dot_general(left, right, (((1,), (1,)), ((), ())), preferred_element_type=F32)


def tn(left, right):
    return lax.dot_general(left, right, (((0,), (0,)), ((), ())), preferred_element_type=F32)


def rows_at(i, n):
    return pl.ds(pl.multiple_of(i * n, n), n)


def normalise(x):
    d = x - jnp.mean(x, axis=1, keepdims=True)
    r = lax.rsqrt(jnp.mean(d * d, axis=1, keepdims=True) + EPS)
    return d * r, r


def norm_back(u, xhat, r, gain):
    w = u * gain
    a = jnp.mean(w, axis=1, keepdims=True)
    b = jnp.mean(w * xhat, axis=1, keepdims=True)
    return r * (w - a - xhat * b)


def colsum(x):
    return jnp.sum(x, axis=0, keepdims=True)


def begin(copies):
    for c in copies:
        c.start()


def finish(copies):
    for c in copies:
        c.wait()


def row_copies(pieces, buf, sem):
    n = pieces[0].shape[0]
    return [pltpu.make_async_copy(s, buf.at[pl.ds(p * n, n), :], sem) for p, s in enumerate(pieces)]


def col_copies(pieces, buf, sem):
    n = pieces[0].shape[1]
    return [pltpu.make_async_copy(s, buf.at[:, pl.ds(p * n, n)], sem) for p, s in enumerate(pieces)]


def cross_probs(q, ks, lens):
    lane = lax.broadcasted_iota(jnp.int32, (1, PB), 1)
    ss = [jnp.where(lane < n, nt(q, k) * SCALE, NEG) for k, n in zip(ks, lens)]
    top = functools.reduce(jnp.maximum, ss)
    top = jnp.max(top, axis=1, keepdims=True)
    es = [jnp.exp(s - top) for s in ss]
    total = jnp.sum(functools.reduce(jnp.add, es), axis=1, keepdims=True)
    inv = 1.0 / total
    return [e * inv for e in es]


def cross_forward_body(tp, idx, lens, x0, gain_c, gain_s, bias, *refs):
    came, refs = refs[:tp], refs[tp:]
    points, refs = refs[0], refs[1:]
    wkv, wq, wo = refs[:tp], refs[tp : 2 * tp], refs[2 * tp : 3 * tp]
    (kv, q, o, x1, nc, ns, ext_b, wkv_b, wq_b, wo_b, acc, sems) = refs[3 * tp :]
    rows, d = x0.shape
    w = d // tp
    half = ext_b.shape[0] // 2
    ext_c = row_copies(came, ext_b, sems.at[0]) + [
        pltpu.make_async_copy(points.at[pl.ds(0, half), :], ext_b.at[pl.ds(half, half), :], sems.at[0])
    ]
    wkv_c = col_copies(wkv, wkv_b, sems.at[1])
    wq_c = col_copies(wq, wq_b, sems.at[2])
    wo_c = row_copies(wo, wo_b, sems.at[3])
    for c in (wq_c, wkv_c, ext_c, wo_c):
        begin(c)

    @pl.loop(0, rows // PB)
    def _(i):
        s = rows_at(i, PB)
        xhat, _ = normalise(x0[s, :])
        nc[s, :] = (xhat * gain_c[...]).astype(BF)

    finish(wq_c)
    q[...] = nn(nc[...], wq_b[...]).astype(BF)
    finish(wkv_c)
    finish(ext_c)
    span = 512

    @pl.loop(0, ext_b.shape[0] // span)
    def _(i):
        s = rows_at(i, span)
        kv[s, :] = nn(ext_b[s, :], wkv_b[...]).astype(BF)

    @pl.loop(0, rows // PB)
    def _(g):
        s = rows_at(g, PB)
        at = [rows_at(idx[g * NB + n], PB) for n in range(NB)]
        ln = [lens[g * NB + n] for n in range(NB)]
        for p in range(tp):
            for h in range(w // HD):
                c = p * w + h * HD
                k0 = p * 2 * w + h * HD
                ks = [kv[a, k0 : k0 + HD] for a in at]
                vs = [kv[a, k0 + w : k0 + w + HD] for a in at]
                ps = cross_probs(q[s, c : c + HD], ks, ln)
                out = functools.reduce(jnp.add, [nn(pr.astype(BF), v) for pr, v in zip(ps, vs)])
                o[s, c : c + HD] = out.astype(BF)

    finish(wo_c)
    acc[...] = nn(o[...], wo_b[...])

    @pl.loop(0, rows // PB)
    def _(i):
        s = rows_at(i, PB)
        y = x0[s, :] + acc[s, :] + bias[...]
        x1[s, :] = y
        xhat, _ = normalise(y)
        ns[s, :] = (xhat * gain_s[...]).astype(BF)


def cross_forward(idx, lens, x0, gain_c, gain_s, bias, came, points, wkv, wq, wo):
    tp = len(wq)
    rows, d = x0.shape
    w = d // tp
    ext = points.shape[0]
    return pl.pallas_call(
        functools.partial(cross_forward_body, tp),
        out_shape=(
            shape((ext, 2 * d), BF),
            shape((rows, d), BF),
            shape((rows, d), BF),
            shape((rows, d), F32),
            shape((rows, d), BF),
            shape((rows, d), BF),
        ),
        in_specs=[SM, SM] + [VM] * 4 + [ANY] * (4 * tp + 1),
        out_specs=[VM] * 6,
        scratch_shapes=[
            pltpu.VMEM((ext, d), BF),
            pltpu.VMEM((d, 2 * d), BF),
            pltpu.VMEM((d, d), BF),
            pltpu.VMEM((d, d), BF),
            pltpu.VMEM((rows, d), F32),
            pltpu.SemaphoreType.DMA((4,)),
        ],
        compiler_params=params(),
        name="cross_forward",
    )(idx, lens, x0, gain_c, gain_s, bias, *came, points, *wkv, *wq, *wo)


def self_probs(q, k):
    s = nt(q, k) * SCALE
    e = jnp.exp(s - jnp.max(s, axis=1, keepdims=True))
    return e * (1.0 / jnp.sum(e, axis=1, keepdims=True))


def self_forward_body(tp, ns, x1, gain_m, bias, *refs):
    wqkv, wo = refs[:tp], refs[tp : 2 * tp]
    qkv, o, x2, nm, wqkv_b, wo_b, acc, sems = refs[2 * tp :]
    rows, d = x1.shape
    w = d // tp
    wqkv_c = col_copies(wqkv, wqkv_b, sems.at[0])
    wo_c = row_copies(wo, wo_b, sems.at[1])
    begin(wqkv_c)
    begin(wo_c)
    finish(wqkv_c)
    qkv[...] = nn(ns[...], wqkv_b[...]).astype(BF)

    @pl.loop(0, rows // PB)
    def _(g):
        s = rows_at(g, PB)
        for p in range(tp):
            for h in range(w // HD):
                c = p * w + h * HD
                k0 = p * 3 * w + h * HD
                pr = self_probs(qkv[s, k0 : k0 + HD], qkv[s, k0 + w : k0 + w + HD])
                v = qkv[s, k0 + 2 * w : k0 + 2 * w + HD]
                o[s, c : c + HD] = nn(pr.astype(BF), v).astype(BF)

    finish(wo_c)
    acc[...] = nn(o[...], wo_b[...])

    @pl.loop(0, rows // PB)
    def _(i):
        s = rows_at(i, PB)
        y = x1[s, :] + acc[s, :] + bias[...]
        x2[s, :] = y
        xhat, _ = normalise(y)
        nm[s, :] = (xhat * gain_m[...]).astype(BF)


def self_forward(ns, x1, gain_m, bias, wqkv, wo):
    tp = len(wo)
    rows, d = x1.shape
    return pl.pallas_call(
        functools.partial(self_forward_body, tp),
        out_shape=(
            shape((rows, 3 * d), BF),
            shape((rows, d), BF),
            shape((rows, d), F32),
            shape((rows, d), BF),
        ),
        in_specs=[VM] * 4 + [ANY] * (2 * tp),
        out_specs=[VM] * 4,
        scratch_shapes=[
            pltpu.VMEM((d, 3 * d), BF),
            pltpu.VMEM((d, d), BF),
            pltpu.VMEM((rows, d), F32),
            pltpu.SemaphoreType.DMA((2,)),
        ],
        compiler_params=params(),
        name="self_forward",
    )(ns, x1, gain_m, bias, *wqkv, *wo)


ROOT = 0.7978845608028654
CUBE = 0.044715


def feed_body(nm, cot, hb, wh0, wh1, wo0, wo1, act, gb, out, gnm, hbg):
    rows, d = nm.shape
    ff = wh0.shape[1]
    span = min(512, ff)
    for p, (wh, wo) in enumerate(((wh0, wo0), (wh1, wo1))):
        for j in range(ff // span):
            s = slice(j * span, (j + 1) * span)
            x = nn(nm[...], wh[:, s]) + hb[p : p + 1, s]
            ga = nt(cot[...], wo[s, :])
            sq = x * x
            t = jnp.tanh(ROOT * x * (1.0 + CUBE * sq))
            half = 0.5 * (1.0 + t)
            act[p, :, s] = (x * half).astype(BF)
            slope = half + 0.5 * x * (1.0 - t * t) * (ROOT + (3.0 * ROOT * CUBE) * sq)
            g = (ga * slope).astype(BF)
            gb[p, :, s] = g
            hbg[p : p + 1, s] = colsum(g.astype(F32))
    gnm[...] = (nt(gb[0], wh0[...]) + nt(gb[1], wh1[...])).astype(gnm.dtype)
    out[...] = (nn(act[0], wo0[...]) + nn(act[1], wo1[...])).astype(out.dtype)


def feed(nm, cot, hb, wh, wo, kind):
    rows, d = nm.shape
    ff = wh[0].shape[1]
    return pl.pallas_call(
        feed_body,
        out_shape=(
            shape((2, rows, ff), BF),
            shape((2, rows, ff), BF),
            shape((rows, d), kind),
            shape((rows, d), kind),
            shape((2, ff), F32),
        ),
        in_specs=[VM] * 7,
        out_specs=[VM] * 5,
        compiler_params=params(),
        name="feed",
    )(nm, cot, hb, *wh, *wo)


def feed_weights_body(sets, p, *refs):
    acts, cots, nms, gbs = (refs[k * sets : (k + 1) * sets] for k in range(4))
    rest = refs[4 * sets :]
    (came_o, came_h, do, dh) = rest if len(rest) == 4 else (None, None) + tuple(rest)
    tile = 256
    ff, d = do.shape

    @pl.loop(0, ff // tile)
    def _(i):
        s = rows_at(i, tile)
        y = functools.reduce(jnp.add, [tn(a[0, :, s], c[...]) for a, c in zip(acts, cots)])
        if came_o is not None:
            y = y + came_o[s, :].astype(F32)
        do[s, :] = y.astype(BF)

    @pl.loop(0, d // tile)
    def _(i):
        s = rows_at(i, tile)
        y = functools.reduce(jnp.add, [tn(a[:, s], g[0]) for a, g in zip(nms, gbs)])
        if came_h is not None:
            y = y + came_h[s, :].astype(F32)
        dh[s, :] = y.astype(BF)


def feed_weights(p, acts, cots, nms, gbs, came):
    sets = len(acts)
    _, rows, ff = acts[0].shape
    d = cots[0].shape[1]
    one = pl.BlockSpec((1, rows, ff), lambda i: (p, 0, 0))
    whole = pl.BlockSpec((rows, d), lambda i: (0, 0))
    fo = pl.BlockSpec((ff, d), lambda i: (0, 0))
    fh = pl.BlockSpec((d, ff), lambda i: (0, 0))
    return pl.pallas_call(
        functools.partial(feed_weights_body, sets, p),
        grid=(1,),
        out_shape=(shape((ff, d), BF), shape((d, ff), BF)),
        in_specs=[one] * sets + [whole] * sets + [whole] * sets + [one] * sets + ([fo, fh] if came else []),
        out_specs=[fo, fh],
        compiler_params=params(),
        name="feed_weights",
    )(*acts, *cots, *nms, *gbs, *came)


def self_backward_body(tp, others, cot, gnm, x2, x1, gain_m, gain_s, qkv, *refs):
    gots, refs = refs[:others], refs[others:]
    wo, wqkv, refs = refs[:tp], refs[tp : 2 * tp], refs[2 * tp :]
    b2, dqkv, g1, b1, vec, wo_b, wqkv_b, g2, gso, gns, sems = refs
    rows, d = cot.shape
    w = d // tp
    wo_c = row_copies(wo, wo_b, sems.at[0])
    wqkv_c = col_copies(wqkv, wqkv_b, sems.at[1])
    begin(wo_c)
    begin(wqkv_c)
    vec[...] = jnp.zeros_like(vec)

    @pl.loop(0, rows // PB)
    def _(i):
        s = rows_at(i, PB)
        u = functools.reduce(jnp.add, [r[s, :].astype(F32) for r in gots], gnm[s, :])
        xhat, r = normalise(x2[s, :])
        g3 = cot[s, :].astype(F32)
        y = g3 + norm_back(u, xhat, r, gain_m[...])
        g2[s, :] = y
        b2[s, :] = y.astype(BF)
        vec[0:1, :] += colsum(g3)
        vec[1:2, :] += colsum(u * xhat)
        vec[2:3, :] += colsum(y)

    finish(wo_c)
    gso[...] = nt(b2[...], wo_b[...]).astype(BF)

    @pl.loop(0, rows // PB)
    def _(g):
        s = rows_at(g, PB)
        for p in range(tp):
            for h in range(w // HD):
                c = p * w + h * HD
                k0 = p * 3 * w + h * HD
                k1, k2 = k0 + w, k0 + 2 * w
                q, k, v = qkv[s, k0 : k0 + HD], qkv[s, k1 : k1 + HD], qkv[s, k2 : k2 + HD]
                pr = self_probs(q, k)
                do = gso[s, c : c + HD]
                dp = nt(do, v)
                ds = (pr * (dp - jnp.sum(dp * pr, axis=1, keepdims=True))).astype(BF)
                dqkv[s, k0 : k0 + HD] = (nn(ds, k) * SCALE).astype(BF)
                dqkv[s, k1 : k1 + HD] = (tn(ds, q) * SCALE).astype(BF)
                dqkv[s, k2 : k2 + HD] = tn(pr.astype(BF), do).astype(BF)

    finish(wqkv_c)
    gns[...] = nt(dqkv[...], wqkv_b[...])

    @pl.loop(0, rows // PB)
    def _(i):
        s = rows_at(i, PB)
        u = gns[s, :]
        xhat, r = normalise(x1[s, :])
        y = g2[s, :] + norm_back(u, xhat, r, gain_s[...])
        g1[s, :] = y
        b1[s, :] = y.astype(BF)
        vec[3:4, :] += colsum(u * xhat)
        vec[4:5, :] += colsum(y)


def self_backward(cot, gnm, gots, x2, x1, gain_m, gain_s, qkv, wo, wqkv):
    tp = len(wo)
    rows, d = cot.shape
    return pl.pallas_call(
        functools.partial(self_backward_body, tp, len(gots)),
        out_shape=(
            shape((rows, d), BF),
            shape((rows, 3 * d), BF),
            shape((rows, d), F32),
            shape((rows, d), BF),
            shape((8, d), F32),
        ),
        in_specs=[VM] * (7 + len(gots)) + [ANY] * (2 * tp),
        out_specs=[VM] * 5,
        scratch_shapes=[
            pltpu.VMEM((d, d), BF),
            pltpu.VMEM((d, 3 * d), BF),
            pltpu.VMEM((rows, d), F32),
            pltpu.VMEM((rows, d), BF),
            pltpu.VMEM((rows, d), F32),
            pltpu.SemaphoreType.DMA((2,)),
        ],
        compiler_params=params(),
        name="self_backward",
    )(cot, gnm, x2, x1, gain_m, gain_s, qkv, *gots, *wo, *wqkv)


def cross_backward_body(tp, idx, lens, b1, g1, x0, gain_c, q, kv, *refs):
    wo, wq, refs = refs[:tp], refs[tp : 2 * tp], refs[2 * tp :]
    dq, dkv, g0, emb, vec, wo_b, wq_b, gco, gnc, dacc, sems = refs
    rows, d = b1.shape
    w = d // tp
    wo_c = row_copies(wo, wo_b, sems.at[0])
    wq_c = col_copies(wq, wq_b, sems.at[1])
    begin(wo_c)
    begin(wq_c)
    vec[...] = jnp.zeros_like(vec)
    emb[...] = jnp.zeros_like(emb)
    ext = kv.shape[0]

    @pl.loop(0, ext // PB)
    def _(i):
        dacc[rows_at(i, PB), :] = jnp.zeros((PB, dacc.shape[1]), F32)

    finish(wo_c)
    gco[...] = nt(b1[...], wo_b[...]).astype(BF)

    @pl.loop(0, rows // PB)
    def _(g):
        s = rows_at(g, PB)
        at = [rows_at(idx[g * NB + n], PB) for n in range(NB)]
        ln = [lens[g * NB + n] for n in range(NB)]
        for p in range(tp):
            for h in range(w // HD):
                c = p * w + h * HD
                k0 = p * 2 * w + h * HD
                v0 = k0 + w
                ks = [kv[a, k0 : k0 + HD] for a in at]
                vs = [kv[a, v0 : v0 + HD] for a in at]
                qh = q[s, c : c + HD]
                do = gco[s, c : c + HD]
                ps = cross_probs(qh, ks, ln)
                dps = [nt(do, v) for v in vs]
                mixed = functools.reduce(jnp.add, [a * b for a, b in zip(ps, dps)])
                mixed = jnp.sum(mixed, axis=1, keepdims=True)
                dss = [(a * (b - mixed)).astype(BF) for a, b in zip(ps, dps)]
                dqh = functools.reduce(jnp.add, [nn(ds, k) for ds, k in zip(dss, ks)])
                dq[s, c : c + HD] = (dqh * SCALE).astype(BF)
                for a, ds, pr in zip(at, dss, ps):
                    dacc[a, k0 : k0 + HD] += tn(ds, qh) * SCALE
                    dacc[a, v0 : v0 + HD] += tn(pr.astype(BF), do)

    @pl.loop(0, ext // PB)
    def _(i):
        s = rows_at(i, PB)
        dkv[s, :] = dacc[s, :].astype(BF)

    finish(wq_c)
    gnc[...] = nt(dq[...], wq_b[...])

    @pl.loop(0, rows // PB)
    def _(i):
        s = rows_at(i, PB)
        u = gnc[s, :]
        xhat, r = normalise(x0[s, :])
        y = g1[s, :] + norm_back(u, xhat, r, gain_c[...])
        g0[s, :] = y.astype(BF)
        emb[...] += y
        vec[0:1, :] += colsum(u * xhat)


def cross_backward(idx, lens, b1, g1, x0, gain_c, q, kv, wo, wq):
    tp = len(wo)
    rows, d = b1.shape
    ext = kv.shape[0]
    return pl.pallas_call(
        functools.partial(cross_backward_body, tp),
        out_shape=(
            shape((rows, d), BF),
            shape((ext, 2 * d), BF),
            shape((rows, d), BF),
            shape((PB, d), F32),
            shape((8, d), F32),
        ),
        in_specs=[SM, SM] + [VM] * 6 + [ANY] * (2 * tp),
        out_specs=[VM] * 5,
        scratch_shapes=[
            pltpu.VMEM((d, d), BF),
            pltpu.VMEM((d, d), BF),
            pltpu.VMEM((rows, d), BF),
            pltpu.VMEM((rows, d), F32),
            pltpu.VMEM((ext, 2 * d), F32),
            pltpu.SemaphoreType.DMA((2,)),
        ],
        compiler_params=params(),
        name="cross_backward",
    )(idx, lens, b1, g1, x0, gain_c, q, kv, *wo, *wq)


def tn_into(out, at, left, right, extra):
    tile = 256
    lead, lo, n = at

    @pl.loop(0, left.shape[1] // tile)
    def _(i):
        s = rows_at(i, tile)
        y = tn(left[:, s], right())
        if extra is not None:
            y = y + extra[lead, s, lo : lo + n].astype(F32)
        out[lead, s, lo : lo + n] = y.astype(BF)


def self_weights_body(tp, odd, ns, dqkv, o, b2, *refs):
    extra, out = (None, refs[0]) if odd else (refs[0], refs[1])
    w = ns.shape[1] // tp
    for j in range(tp // 2):
        p = 2 * j + (1 if odd else 0)
        tn_into(out, (j, 0, 3 * w), ns, lambda: dqkv[:, p * 3 * w : (p + 1) * 3 * w], extra)
        tn_into(out, (j, 3 * w, w), b2, lambda: o[:, p * w : (p + 1) * w], extra)


def self_weights(tp, odd, ns, dqkv, o, b2, came):
    d = ns.shape[1]
    ins = [ns, dqkv, o, b2] + list(came)
    return pl.pallas_call(
        functools.partial(self_weights_body, tp, odd),
        out_shape=shape((tp // 2, d, 4 * d // tp), BF),
        in_specs=[VM] * len(ins),
        out_specs=VM,
        compiler_params=params(),
        name="self_weights",
    )(*ins)


def cross_weights_body(tp, odd, nc, dq, o, b1, dkv, points, *refs):
    came, refs = refs[:tp], refs[tp:]
    extra, refs = (None, refs) if odd else (refs[0], refs[1:])
    out, ext_b, sem = refs
    half = ext_b.shape[0] // 2
    copies = row_copies(came, ext_b, sem) + [
        pltpu.make_async_copy(points.at[pl.ds(0, half), :], ext_b.at[pl.ds(half, half), :], sem)
    ]
    begin(copies)
    w = nc.shape[1] // tp
    for j in range(tp // 2):
        p = 2 * j + (1 if odd else 0)
        tn_into(out, (j, 0, w), nc, lambda: dq[:, p * w : (p + 1) * w], extra)
        tn_into(out, (j, 3 * w, w), b1, lambda: o[:, p * w : (p + 1) * w], extra)
    finish(copies)
    for j in range(tp // 2):
        p = 2 * j + (1 if odd else 0)
        tn_into(out, (j, w, 2 * w), ext_b, lambda: dkv[:, p * 2 * w : (p + 1) * 2 * w], extra)


def cross_weights(tp, odd, nc, dq, o, b1, dkv, points, came_points, came):
    d = nc.shape[1]
    ins = [nc, dq, o, b1, dkv, points] + list(came_points) + list(came)
    return pl.pallas_call(
        functools.partial(cross_weights_body, tp, odd),
        out_shape=shape((tp // 2, d, 4 * d // tp), BF),
        in_specs=[VM] * 5 + [ANY] * (1 + tp) + [VM] * len(came),
        out_specs=VM,
        scratch_shapes=[pltpu.VMEM((dkv.shape[0], d), BF), pltpu.SemaphoreType.DMA],
        compiler_params=params(),
        name="cross_weights",
    )(*ins)


def flip(x, axis, bit):
    n = lax.axis_size(axis)
    return lax.ppermute(x, axis, [(i, i ^ (1 << bit)) for i in range(n)])


def bits_of(axis):
    return (lax.axis_size(axis) - 1).bit_length()


def bit_at(axis, bit):
    return (lax.axis_index(axis) >> bit) & 1


def gather_pieces(own):
    have = {0: own}
    for bit in reversed(range(bits_of("tp"))):
        for p in list(have):
            have[p | (1 << bit)] = flip(have[p], "tp", bit)
    return [have[p] for p in range(len(have))]


def in_order(pieces):
    x = jnp.stack(pieces)
    for bit in range(bits_of("tp")):
        y = x.reshape((-1, 2, 1 << bit) + x.shape[1:])
        x = jnp.where(bit_at("tp", bit) == 1, y[:, ::-1], y).reshape(x.shape)
    return x


def add(*xs):
    return functools.reduce(jnp.add, [x.astype(F32) for x in xs]).astype(BF)


def halves(x, axis, bit):
    n = x.shape[0] // 2
    mine = bit_at(axis, bit)
    return (
        lax.dynamic_slice_in_dim(x, mine * n, n, 0),
        lax.dynamic_slice_in_dim(x, (1 - mine) * n, n, 0),
    )


def sum_half(x, axis, bit):
    keep, send = halves(x, axis, bit)
    return keep, flip(send, axis, bit)


def both(x, axis, bit):
    other = flip(x, axis, bit)
    low = bit_at(axis, bit) == 0
    return jnp.where(low, jnp.concatenate([x, other]), jnp.concatenate([other, x]))


def sum_over_grp(x):
    order = list(range(bits_of("grp")))
    for bit in order:
        x = add(*sum_half(x, "grp", bit))
    for bit in reversed(order):
        x = both(x, "grp", bit)
    return x.astype(F32)


def sum_pieces(even):
    have = {2 * j: even[j] for j in range(even.shape[0])}
    for bit in reversed(range(1, bits_of("tp"))):
        send = [p for p in have if p >> bit & 1]
        for p in send:
            got = flip(have[p], "tp", bit)
            have[p ^ (1 << bit)] = add(have[p ^ (1 << bit)], got)
        have = {p: v for p, v in have.items() if not p >> bit & 1}
    return have[0]


def sum_small(x):
    for bit in reversed(range(bits_of("tp"))):
        keep, got = sum_half(x, "tp", bit)
        x = keep + got
    x = x[0]
    for bit in range(bits_of("grp")):
        x = x + flip(x, "grp", bit)
    return x


def to_groups(x, per):
    lat, groups, w = x.shape
    n = groups // per
    tp = lax.axis_size("tp")
    y = jnp.transpose(x.reshape(lat, n, per, w), (1, 2, 0, 3))
    y = lax.all_to_all(y, ("grp", "tp"), split_axis=0, concat_axis=0, tiled=True)
    y = jnp.transpose(y.reshape(n // tp, tp, per, lat, w), (2, 0, 3, 1, 4))
    return y.reshape(per * lat * (n // tp), tp * w)


def from_groups(x, per):
    tp = lax.axis_size("tp")
    n = lax.axis_size("grp") * tp
    rows, d = x.shape
    lat, w = rows // per // (n // tp), d // tp
    y = jnp.transpose(x.reshape(per, n // tp, lat, tp, w), (1, 3, 0, 2, 4)).reshape(n, per, lat, w)
    y = lax.all_to_all(y, ("grp", "tp"), split_axis=0, concat_axis=0, tiled=True)
    return jnp.transpose(y, (2, 0, 1, 3)).reshape(lat, n * per, w)


def per_device(
    latents,
    skip_latents,
    points,
    neighbours,
    block_lengths,
    latent_embed,
    gain_cross,
    query_cross,
    key_cross,
    value_cross,
    output_cross,
    bias_cross,
    gain_self,
    query_self,
    key_self,
    value_self,
    output_self,
    bias_self,
    gain_mlp,
    hidden_weight,
    hidden_bias,
    output_weight,
    output_bias,
    cotangent,
):
    tp, grp = lax.axis_size("tp"), lax.axis_size("grp")
    t, i = lax.axis_index("tp"), lax.axis_index("grp")
    d = query_cross.shape[0]
    w = latent_embed.shape[1]
    lat_rows = latent_embed.shape[0]
    ff = hidden_weight.shape[1]
    groups_here = neighbours.shape[0]
    groups = groups_here * grp
    per = groups_here // tp
    blocks_here = points.shape[0] // PB
    all_blocks = blocks_here * grp
    half_rows = points.shape[0] // 2

    small = jnp.concatenate(
        [
            latent_embed,
            bias_cross[None],
            bias_self[None],
            output_bias[None],
            hidden_bias.reshape(ff // w, w),
        ]
    )
    small_pieces = gather_pieces(small)
    small_all = in_order(small_pieces)
    by_rows = jnp.transpose(small_all, (1, 0, 2)).reshape(small.shape[0], d)
    embed = by_rows[:lat_rows]
    bias_c, bias_s, bias_o = (by_rows[lat_rows + k : lat_rows + k + 1] for k in range(3))
    hid_bias = jnp.stack([piece[lat_rows + 3 :].reshape(ff) for piece in small_pieces[:2]])

    wkv = gather_pieces(jnp.concatenate([key_cross, value_cross], axis=1))
    wq = gather_pieces(query_cross)
    woc = gather_pieces(output_cross)
    wqkv = gather_pieces(jnp.concatenate([query_self, key_self, value_self], axis=1))
    wos = gather_pieces(output_self)
    whid = [hidden_weight, flip(hidden_weight, "tp", 0)]
    wout = [output_weight, flip(output_weight, "tp", 0)]

    share = half_rows // tp
    sent = lax.dynamic_slice_in_dim(points, half_rows + t * share, share, 0)
    first = lax.ppermute(sent, "grp", [(k, (k + 1) % grp) for k in range(grp)])
    came_points = gather_pieces(first)
    near = lax.dynamic_slice_in_dim(neighbours, t * per, per, 0).reshape(per * NB)
    block = (near - (i * blocks_here - blocks_here // 2)) % all_blocks
    share_blocks = share // PB
    moved = ((block // share_blocks) ^ t) * share_blocks + block % share_blocks
    idx = jnp.where(block < blocks_here // 2, moved, block).astype(jnp.int32)
    lens = block_lengths[near]

    gain_c, gain_s, gain_m = gain_cross[None], gain_self[None], gain_mlp[None]
    rows = per * lat_rows
    x0 = (
        to_groups(latents, per).astype(F32).reshape(per, lat_rows, d) + embed[None]
    ).reshape(rows, d)
    kv, q, oc, x1, nc, ns = cross_forward(
        idx, lens, x0, gain_c, gain_s, bias_c, came_points, points, wkv, wq, woc
    )
    qkv, os, x2, nm = self_forward(ns, x1, gain_m, bias_s, wqkv, wos)
    cot = to_groups(cotangent, per)

    steps = list(range(2, tp, 2))

    def swap(x, k):
        return lax.ppermute(x, "tp", [(j, j ^ k) for j in range(tp)])

    other_cot = [swap(cot, k) for k in steps]
    other_nm = [swap(nm, k) for k in steps]
    acts, gbs, hbgs = [], [], []
    act, gb, out, gnm, hbg = feed(nm, cot, hid_bias, whid, wout, F32)
    acts.append(act)
    gbs.append(gb)
    hbgs.append(hbg)
    back_out, back_gnm = [], []
    for k, n_k, c_k in zip(steps, other_nm, other_cot):
        act, gb, o_k, g_k, hbg = feed(n_k, c_k, hid_bias, whid, wout, BF)
        acts.append(act)
        gbs.append(gb)
        hbgs.append(hbg)
        back_gnm.append(swap(g_k, k))
        back_out.append(swap(o_k, k))
    nms, cots = [nm] + other_nm, [cot] + other_cot
    sent_o, sent_h = feed_weights(1, acts, cots, nms, gbs, [])
    got = [flip(sent_o, "tp", 0), flip(sent_h, "tp", 0)]
    own_o, own_h = feed_weights(0, acts, cots, nms, gbs, got)
    output_weight_grad = sum_over_grp(own_o)
    hidden_weight_grad = sum_over_grp(own_h)

    x3 = functools.reduce(jnp.add, [r.astype(F32) for r in back_out], x2 + out + bias_o)
    block_out = from_groups(x3.astype(BF), per).astype(F32) + skip_latents.astype(F32)
    squares = jnp.sum(jnp.square(block_out), axis=(0, 2))

    b2, dqkv, g1, b1, vec_s = self_backward(
        cot, gnm, back_gnm, x2, x1, gain_m, gain_s, qkv, wos, wqkv
    )
    odd = self_weights(tp, True, ns, dqkv, os, b2, [])
    even = self_weights(tp, False, ns, dqkv, os, b2, [flip(odd, "tp", 0)])
    self_grads = sum_over_grp(sum_pieces(even))

    dq, dkv, g0, emb, vec_c = cross_backward(idx, lens, b1, g1, x0, gain_c, q, kv, woc, wq)
    odd = cross_weights(tp, True, nc, dq, oc, b1, dkv, points, came_points, [])
    even = cross_weights(
        tp, False, nc, dq, oc, b1, dkv, points, came_points, [flip(odd, "tp", 0)]
    )
    cross_grads = sum_over_grp(sum_pieces(even))
    latents_grad = from_groups(g0, per).astype(F32)

    by_share = jnp.transpose(
        jnp.concatenate([emb, vec_s[:5], vec_c[:1]]).reshape(lat_rows + 6, tp, w), (1, 0, 2)
    )
    hb_all = functools.reduce(jnp.add, hbgs).reshape(2, ff // w, w)
    place = lax.broadcasted_iota(jnp.int32, (tp, 1, 1), 0)
    hb_share = jnp.where(place == t, hb_all[0][None], 0.0) + jnp.where(
        place == (t ^ 1), hb_all[1][None], 0.0
    )
    norm_rows = -(-groups // w)
    sq_rows = jnp.pad(squares, (0, norm_rows * w - groups)).reshape(1, norm_rows, w)
    packed = jnp.concatenate(
        [by_share, hb_share, jnp.broadcast_to(sq_rows, (tp, norm_rows, w))], axis=1
    )
    pad = -packed.shape[1] % 8
    packed = jnp.pad(packed, ((0, 0), (0, pad), (0, 0)))
    total = sum_small(packed)
    embed_grad = total[:lat_rows]
    (
        output_bias_grad,
        gain_mlp_grad,
        bias_self_grad,
        gain_self_grad,
        bias_cross_grad,
        gain_cross_grad,
    ) = (total[lat_rows + k] for k in range(6))
    at = lat_rows + 6
    hidden_bias_grad = total[at : at + ff // w].reshape(ff)
    at += ff // w
    square_sums = total[at : at + norm_rows].reshape(norm_rows * w)[:groups]
    group_norms = jnp.sqrt(square_sums / (lat_rows * d))

    def four(u):
        return u[:, :w], u[:, w : 2 * w], u[:, 2 * w : 3 * w], u[:, 3 * w :].T

    query_cross_grad, key_cross_grad, value_cross_grad, output_cross_grad = four(cross_grads)
    query_self_grad, key_self_grad, value_self_grad, output_self_grad = four(self_grads)
    return (
        block_out,
        group_norms,
        latents_grad,
        embed_grad,
        gain_cross_grad,
        query_cross_grad,
        key_cross_grad,
        value_cross_grad,
        output_cross_grad,
        bias_cross_grad,
        gain_self_grad,
        query_self_grad,
        key_self_grad,
        value_self_grad,
        output_self_grad,
        bias_self_grad,
        gain_mlp_grad,
        hidden_weight_grad,
        hidden_bias_grad,
        output_weight_grad,
        output_bias_grad,
    )


def solution(mesh):
    lay = P("grp", None, "tp")
    cols, rows, part = P(None, "tp"), P("tp", None), P("tp")
    attn = (P(), cols, cols, cols, rows, part)
    return jax.shard_map(
        per_device,
        mesh=mesh,
        in_specs=(lay, lay, P("grp", None), P("grp", None), P(), cols)
        + attn
        + attn
        + (P(), cols, part, rows, part, lay),
        out_specs=(lay, P(), lay, cols)
        + (part, cols, cols, cols, rows, part)
        + (part, cols, cols, cols, rows, part)
        + (part, cols, part, rows, part),
        check_vma=False,
    )
```

```python
import functools

import jax
import jax.numpy as jnp
from jax import lax
from jax.experimental import pallas as pl
from jax.experimental.pallas import tpu as pltpu
from jax.sharding import PartitionSpec as P

HD = 128
PB = 128
NB = 4
EPS = 1e-05
NEG = -1e30
SCALE = HD ** (-0.5)
BF = jnp.bfloat16
F32 = jnp.float32
VMEM_BYTES = 58 * 2**20
GRP = ("z", "x")

ANY = pl.BlockSpec(memory_space=pl.ANY)
VM = pl.BlockSpec(memory_space=pltpu.VMEM)
SM = pl.BlockSpec(memory_space=pltpu.SMEM)


def shape(dims, kind):
    return jax.ShapeDtypeStruct(dims, kind)


def params():
    return pltpu.CompilerParams(vmem_limit_bytes=VMEM_BYTES)


def cost(us):
    return pl.CostEstimate(flops=int(us * 1.1e9), bytes_accessed=int(us * 1e6), transcendentals=0)


def nn(left, right):
    return lax.dot_general(left, right, (((1,), (0,)), ((), ())), preferred_element_type=F32)


def nt(left, right):
    return lax.dot_general(left, right, (((1,), (1,)), ((), ())), preferred_element_type=F32)


def tn(left, right):
    return lax.dot_general(left, right, (((0,), (0,)), ((), ())), preferred_element_type=F32)


def rows_at(i, n):
    return pl.ds(pl.multiple_of(i * n, n), n)


def normalise(x):
    d = x - jnp.mean(x, axis=1, keepdims=True)
    r = lax.rsqrt(jnp.mean(d * d, axis=1, keepdims=True) + EPS)
    return d * r, r


def norm_back(u, xhat, r, gain):
    w = u * gain
    a = jnp.mean(w, axis=1, keepdims=True)
    b = jnp.mean(w * xhat, axis=1, keepdims=True)
    return r * (w - a - xhat * b)


def colsum(x):
    return jnp.sum(x, axis=0, keepdims=True)


def begin(copies):
    for c in copies:
        c.start()


def finish(copies):
    for c in copies:
        c.wait()


def row_copies(pieces, buf, sem):
    n = pieces[0].shape[0]
    return [pltpu.make_async_copy(s, buf.at[pl.ds(p * n, n), :], sem) for p, s in enumerate(pieces)]


def pack_parts(refs, tp, place):
    if len(refs) == tp:
        return [(p, None, r) for p, r in enumerate(refs)]
    parts = [(0, None, refs[0]), (1, None, refs[1])]
    for p in range(2, tp):
        parts.append((p, place[0], refs[2 * p - 2]))
        parts.append((p, 1 - place[0], refs[2 * p - 1]))
    return parts


def col_copies(parts, at, n, buf, sem):
    out = []
    for p, h, r in parts:
        to = pl.ds(p * n, n)
        k = r.shape[0]
        dst = buf.at[:, to] if h is None else buf.at[rows_at(h, k), to]
        out.append(pltpu.make_async_copy(r.at[:, pl.ds(at, n)], dst, sem))
    return out


def block_copies(parts, at, w, buf, sem):
    out = []
    for p, h, r in parts:
        count = r.shape[0] // w
        for k in range(count):
            col = k * w if h is None else pl.multiple_of((h * count + k) * w, 128)
            src = r.at[pl.ds(k * w, w), pl.ds(at, w)]
            out.append(pltpu.make_async_copy(src, buf.at[pl.ds(p * w, w), pl.ds(col, w)], sem))
    return out


def softmax_parts(s, axis):
    e = jnp.exp((s - jnp.max(s, axis=axis, keepdims=True)) * SCALE)
    return e * (1.0 / jnp.sum(e, axis=axis, keepdims=True))


def pack_body(counts, *refs):
    outs, at = refs[-len(counts) :], 0
    for n, out in zip(counts, outs):
        col, rows = 0, out.shape[0]
        for r in refs[at : at + n]:
            if r.shape[0] == rows:
                out[:, col : col + r.shape[1]] = r[...]
                col += r.shape[1]
            else:
                w = r.shape[0]
                for k in range(rows // w):
                    out[k * w : (k + 1) * w, col : col + w] = r[:, k * w : (k + 1) * w]
                col += w
        at += n


def packed(groups, late=()):
    counts = [len(g) for g in groups]
    ins = [x for g in groups for x in g]
    rows = groups[0][0].shape[0]
    outs = []
    for g in groups:
        cols = sum(x.shape[1] if x.shape[0] == rows else x.shape[0] for x in g)
        outs.append(shape((rows, cols), g[0].dtype))
    n = len(ins)
    return pl.pallas_call(
        lambda *refs: pack_body(counts, *refs[:n], *refs[n + len(late) :]),
        out_shape=outs,
        in_specs=[VM] * n + [ANY] * len(late),
        out_specs=[VM] * len(outs),
        compiler_params=pltpu.CompilerParams(vmem_limit_bytes=12 * 2**20),
        cost_estimate=cost(2),
        name="packed",
    )(*ins, *late)


def part_body(n, at, x, *refs):
    out, sem = refs[-2:]
    copy = pltpu.make_async_copy(x.at[pl.ds(pl.multiple_of(at[0] * n, n), n), :], out, sem)
    copy.start()
    copy.wait()


def part_of(x, at, n, late=()):
    return pl.pallas_call(
        functools.partial(part_body, n),
        out_shape=shape((n, x.shape[1]), x.dtype),
        in_specs=[SM] + [ANY] * (1 + len(late)),
        out_specs=VM,
        scratch_shapes=[pltpu.SemaphoreType.DMA],
        cost_estimate=cost(1),
        name="part_of",
    )(at, x, *late)


def share_copies(places, parts, bufs, sem):
    out = []
    for r, x in zip(parts, (places[0], 1 - places[0])):
        c = bufs[0].shape[0] // (2 * r.shape[0])
        for z in range(r.shape[0]):
            for j, buf in enumerate(bufs):
                src = r.at[z, pl.ds(j * c, c), :]
                out.append(pltpu.make_async_copy(src, buf.at[rows_at(2 * z + x, c), :], sem))
    return out


def final_body(places, own, other, *refs):
    q, k, v, o, qo_b, kv_b, sem = refs[-7:]
    copies = share_copies(places, (own, other), (qo_b, kv_b), sem)
    begin(copies)
    finish(copies)
    w = o.shape[0]
    q[...] = qo_b[0:w, :].astype(F32).T
    o[...] = qo_b[w : 2 * w, :].astype(F32)
    k[...] = kv_b[0:w, :].astype(F32).T
    v[...] = kv_b[w : 2 * w, :].astype(F32).T


def final(places, w, own, other, late=()):
    d = own.shape[2]
    tall, flat = shape((d, w), F32), shape((w, d), F32)
    return pl.pallas_call(
        final_body,
        out_shape=(tall, tall, tall, flat),
        in_specs=[SM] + [ANY] * (2 + len(late)),
        out_specs=[VM] * 4,
        scratch_shapes=[pltpu.VMEM((2 * w, d), BF)] * 2 + [pltpu.SemaphoreType.DMA],
        compiler_params=params(),
        cost_estimate=cost(5),
        name="final",
    )(places, own, other, *late)


def final_feed_body(places, own, other, out, hid, out_b, hid_b, sem):
    copies = share_copies(places, (own, other), (out_b, hid_b), sem)
    begin(copies)
    finish(copies)
    out[...] = out_b[...].astype(F32)
    hid[...] = hid_b[...].astype(F32).T


def final_feed(places, own, other):
    nz, c, d = own.shape
    ff = nz * c
    return pl.pallas_call(
        final_feed_body,
        out_shape=(shape((ff, d), F32), shape((d, ff), F32)),
        in_specs=[SM] + [ANY] * 2,
        out_specs=[VM] * 2,
        scratch_shapes=[pltpu.VMEM((ff, d), BF)] * 2 + [pltpu.SemaphoreType.DMA],
        compiler_params=params(),
        cost_estimate=cost(6),
        name="final_feed",
    )(places, own, other)


def keys_body(tp, points, came0, came1, *refs):
    packs, (kv, kv_b, ext_b, wkv_b, sems) = refs[:tp], refs[-5:]
    ext, d = ext_b.shape
    half = ext // 2
    near_c = [pltpu.make_async_copy(points.at[pl.ds(0, half), :], ext_b.at[pl.ds(half, half), :], sems.at[0])]
    far_c = row_copies([came0, came1], ext_b, sems.at[1])
    w_c = col_copies(pack_parts(packs, tp, None), 0, packs[0].shape[1], wkv_b, sems.at[2])
    for c in (w_c, near_c, far_c):
        begin(c)
    finish(w_c)
    span = 512

    def out_copy(i):
        s = rows_at(i, span)
        return pltpu.make_async_copy(kv_b.at[s, :], kv.at[s, :], sems.at[3])

    def work(i):
        s = rows_at(i, span)
        kv_b[s, :] = nn(ext_b[s, :], wkv_b[...]).astype(BF)
        out_copy(i).start()

    finish(near_c)
    pl.loop(half // span, ext // span)(work)
    finish(far_c)
    pl.loop(0, half // span)(work)

    @pl.loop(0, ext // span)
    def _(i):
        out_copy(i).wait()


def keys_values(points, came, packs, late):
    tp = len(packs)
    ext, d = points.shape
    return pl.pallas_call(
        functools.partial(keys_body, tp),
        out_shape=shape((ext, 2 * d), BF),
        in_specs=[ANY] * (3 + tp + len(late)),
        out_specs=ANY,
        scratch_shapes=[
            pltpu.VMEM((ext, 2 * d), BF),
            pltpu.VMEM((ext, d), BF),
            pltpu.VMEM((d, 2 * d), BF),
            pltpu.SemaphoreType.DMA((4,)),
        ],
        compiler_params=params(),
        cost_estimate=cost(14),
        name="keys_values",
    )(points, *came, *packs, *late)


def cross_forward_body(tp, idx, lens, x0, gain_c, gain_s, bias, kv, *refs):
    parts = pack_parts(refs[:tp], tp, None)
    (q, o, x1, nc, ns, kv_b, wq_b, wo_b, acc, sems) = refs[-10:]
    rows, d = x0.shape
    w = d // tp
    wq_c = col_copies(parts, 0, w, wq_b, sems.at[0])
    wo_c = block_copies(parts, w, w, wo_b, sems.at[1])
    kv_c = [pltpu.make_async_copy(kv, kv_b, sems.at[2])]
    for c in (wq_c, kv_c, wo_c):
        begin(c)

    @pl.loop(0, rows // PB)
    def _(i):
        s = rows_at(i, PB)
        xhat, _ = normalise(x0[s, :])
        nc[s, :] = (xhat * gain_c[...]).astype(BF)

    finish(wq_c)
    q[...] = nn(nc[...], wq_b[...]).astype(BF)
    finish(kv_c)

    @pl.loop(0, rows // PB)
    def _(g):
        s = rows_at(g, PB)
        at = [rows_at(idx[g * NB + n], PB) for n in range(NB)]
        lane = lax.broadcasted_iota(jnp.int32, (1, PB), 1)
        live = jnp.concatenate([(lane < lens[g * NB + n]).astype(jnp.int32) for n in range(NB)], axis=1) > 0
        for p in range(tp):
            for h in range(w // HD):
                c = p * w + h * HD
                k0 = p * 2 * w + h * HD
                k = jnp.concatenate([kv_b[a, k0 : k0 + HD] for a in at], axis=0)
                v = jnp.concatenate([kv_b[a, k0 + w : k0 + w + HD] for a in at], axis=0)
                pr = softmax_parts(jnp.where(live, nt(q[s, c : c + HD], k), NEG), 1)
                o[s, c : c + HD] = nn(pr.astype(BF), v).astype(BF)

    finish(wo_c)
    acc[...] = nn(o[...], wo_b[...])

    @pl.loop(0, rows // PB)
    def _(i):
        s = rows_at(i, PB)
        y = x0[s, :] + acc[s, :] + bias[...]
        x1[s, :] = y
        xhat, _ = normalise(y)
        ns[s, :] = (xhat * gain_s[...]).astype(BF)


def cross_forward(idx, lens, x0, gain_c, gain_s, bias, kv, packs):
    tp = len(packs)
    rows, d = x0.shape
    ext = kv.shape[0]
    return pl.pallas_call(
        functools.partial(cross_forward_body, tp),
        out_shape=(
            shape((rows, d), BF),
            shape((rows, d), BF),
            shape((rows, d), F32),
            shape((rows, d), BF),
            shape((rows, d), BF),
        ),
        in_specs=[SM] * 2 + [VM] * 4 + [ANY] * (1 + tp),
        out_specs=[VM] * 5,
        scratch_shapes=[
            pltpu.VMEM((ext, 2 * d), BF),
            pltpu.VMEM((d, d), BF),
            pltpu.VMEM((d, d), BF),
            pltpu.VMEM((rows, d), F32),
            pltpu.SemaphoreType.DMA((3,)),
        ],
        compiler_params=params(),
        cost_estimate=cost(20),
        name="cross_forward",
    )(idx, lens, x0, gain_c, gain_s, bias, kv, *packs)


def self_forward_body(tp, ns, x1, gain_m, bias, *refs):
    n = tp
    parts = pack_parts(refs[:n], tp, None)
    qkv, o, x2, nm, wqkv_b, wo_b, acc, sems = refs[-8:]
    rows, d = x1.shape
    w = d // tp
    wqkv_c = col_copies(parts, 0, 3 * w, wqkv_b, sems.at[0])
    wo_c = block_copies(parts, 3 * w, w, wo_b, sems.at[1])
    begin(wqkv_c)
    begin(wo_c)
    finish(wqkv_c)
    qkv[...] = nn(ns[...], wqkv_b[...]).astype(BF)

    @pl.loop(0, rows // PB)
    def _(g):
        s = rows_at(g, PB)
        for p in range(tp):
            for h in range(w // HD):
                c = p * w + h * HD
                k0 = p * 3 * w + h * HD
                pr = softmax_parts(nt(qkv[s, k0 : k0 + HD], qkv[s, k0 + w : k0 + w + HD]), 1)
                v = qkv[s, k0 + 2 * w : k0 + 2 * w + HD]
                o[s, c : c + HD] = nn(pr.astype(BF), v).astype(BF)

    finish(wo_c)
    acc[...] = nn(o[...], wo_b[...])

    @pl.loop(0, rows // PB)
    def _(i):
        s = rows_at(i, PB)
        y = x1[s, :] + acc[s, :] + bias[...]
        x2[s, :] = y
        xhat, _ = normalise(y)
        nm[s, :] = (xhat * gain_m[...]).astype(BF)


def self_forward(ns, x1, gain_m, bias, pack, late):
    rows, d = x1.shape
    tp = len(pack)
    return pl.pallas_call(
        functools.partial(self_forward_body, tp),
        out_shape=(
            shape((rows, 3 * d), BF),
            shape((rows, d), BF),
            shape((rows, d), F32),
            shape((rows, d), BF),
        ),
        in_specs=[VM] * 4 + [ANY] * (len(pack) + len(late)),
        out_specs=[VM] * 4,
        scratch_shapes=[
            pltpu.VMEM((d, 3 * d), BF),
            pltpu.VMEM((d, d), BF),
            pltpu.VMEM((rows, d), F32),
            pltpu.SemaphoreType.DMA((2,)),
        ],
        compiler_params=params(),
        cost_estimate=cost(22),
        name="self_forward",
    )(ns, x1, gain_m, bias, *pack, *late)


ROOT = 0.7978845608028654
CUBE = 0.044715


def feed_body(nm, cot, hb, wh0, wh1, wo0, wo1, *refs):
    act, gb, out, gnm, hbg = refs[-5:]
    rows, d = nm.shape
    ff = wh0.shape[1]
    span = min(512, ff)
    for p, (wh, wo) in enumerate(((wh0, wo0), (wh1, wo1))):
        for j in range(ff // span):
            s = slice(j * span, (j + 1) * span)
            x = nn(nm[...], wh[:, s]) + hb[p : p + 1, s]
            ga = nt(cot[...], wo[s, :])
            sq = x * x
            t = jnp.tanh(ROOT * x * (1.0 + CUBE * sq))
            half = 0.5 * (1.0 + t)
            act[p, :, s] = (x * half).astype(BF)
            slope = half + 0.5 * x * (1.0 - t * t) * (ROOT + (3.0 * ROOT * CUBE) * sq)
            g = (ga * slope).astype(BF)
            gb[p, :, s] = g
            hbg[p : p + 1, s] = colsum(g.astype(F32))
    gnm[...] = (nt(gb[0], wh0[...]) + nt(gb[1], wh1[...])).astype(gnm.dtype)
    out[...] = (nn(act[0], wo0[...]) + nn(act[1], wo1[...])).astype(out.dtype)


def feed(nm, cot, hb, wh, wo, kind, late=()):
    rows, d = nm.shape
    ff = wh[0].shape[1]
    return pl.pallas_call(
        feed_body,
        out_shape=(
            shape((2, rows, ff), BF),
            shape((2, rows, ff), BF),
            shape((rows, d), kind),
            shape((rows, d), kind),
            shape((2, ff), F32),
        ),
        in_specs=[VM] * 7 + [ANY] * len(late),
        out_specs=[VM] * 5,
        compiler_params=params(),
        cost_estimate=cost(15),
        name="feed",
    )(nm, cot, hb, *wh, *wo, *late)


def feed_weights_body(sets, *refs):
    lefts, rights, rest = refs[:sets], refs[sets : 2 * sets], refs[2 * sets :]
    out = rest[-1]
    came = rest[0] if len(rest) == 2 else None
    tile = 256

    @pl.loop(0, out.shape[0] // tile)
    def _(i):
        s = rows_at(i, tile)
        y = functools.reduce(jnp.add, [tn(a[0, :, s], c[...]) for a, c in zip(lefts, rights)])
        if came is not None:
            y = y + came[s, :].astype(F32)
        out[s, :] = y.astype(BF)


def feed_weights(p, lefts, rights, came):
    sets = len(lefts)

    def spec(x):
        if x.ndim == 3:
            return pl.BlockSpec((1,) + x.shape[1:], lambda i: (p, 0, 0))
        return pl.BlockSpec(x.shape, lambda i: (0, 0))

    dims = (lefts[0].shape[-1], rights[0].shape[-1])
    ins = list(lefts) + list(rights) + list(came)
    return pl.pallas_call(
        functools.partial(feed_weights_body, sets),
        grid=(1,),
        out_shape=shape(dims, BF),
        in_specs=[spec(x) for x in ins],
        out_specs=pl.BlockSpec(dims, lambda i: (0, 0)),
        compiler_params=params(),
        cost_estimate=cost(6),
        name="feed_weights",
    )(*ins)


def self_backward_body(tp, others, cot, gnm, x2, x1, gain_m, gain_s, qkv, *refs):
    gots, refs = refs[:others], refs[others:]
    n = tp
    parts = pack_parts(refs[:n], tp, None)
    b2, dqkv, g1, b1, vec, wo_b, wqkv_b, g2, gso, gns, sems = refs[-11:]
    rows, d = cot.shape
    w = d // tp
    wqkv_c = col_copies(parts, 0, 3 * w, wqkv_b, sems.at[0])
    wo_c = block_copies(parts, 3 * w, w, wo_b, sems.at[1])
    begin(wo_c)
    begin(wqkv_c)
    vec[...] = jnp.zeros_like(vec)

    @pl.loop(0, rows // PB)
    def _(i):
        s = rows_at(i, PB)
        u = functools.reduce(jnp.add, [r[s, :].astype(F32) for r in gots], gnm[s, :])
        xhat, r = normalise(x2[s, :])
        g3 = cot[s, :].astype(F32)
        y = g3 + norm_back(u, xhat, r, gain_m[...])
        g2[s, :] = y
        b2[s, :] = y.astype(BF)
        vec[0:1, :] += colsum(g3)
        vec[1:2, :] += colsum(u * xhat)
        vec[2:3, :] += colsum(y)

    finish(wo_c)
    gso[...] = nt(b2[...], wo_b[...]).astype(BF)

    @pl.loop(0, rows // PB)
    def _(g):
        s = rows_at(g, PB)
        for p in range(tp):
            for h in range(w // HD):
                c = p * w + h * HD
                k0 = p * 3 * w + h * HD
                k1, k2 = k0 + w, k0 + 2 * w
                q, k, v = qkv[s, k0 : k0 + HD], qkv[s, k1 : k1 + HD], qkv[s, k2 : k2 + HD]
                pr = softmax_parts(nt(k, q), 0)
                do = gso[s, c : c + HD]
                dp = nt(v, do)
                ds = (pr * (dp - jnp.sum(dp * pr, axis=0, keepdims=True))).astype(BF)
                dqkv[s, k0 : k0 + HD] = (tn(ds, k) * SCALE).astype(BF)
                dqkv[s, k1 : k1 + HD] = (nn(ds, q) * SCALE).astype(BF)
                dqkv[s, k2 : k2 + HD] = nn(pr.astype(BF), do).astype(BF)

    finish(wqkv_c)
    gns[...] = nt(dqkv[...], wqkv_b[...])

    @pl.loop(0, rows // PB)
    def _(i):
        s = rows_at(i, PB)
        u = gns[s, :]
        xhat, r = normalise(x1[s, :])
        y = g2[s, :] + norm_back(u, xhat, r, gain_s[...])
        g1[s, :] = y
        b1[s, :] = y.astype(BF)
        vec[3:4, :] += colsum(u * xhat)
        vec[4:5, :] += colsum(y)


def self_backward(cot, gnm, gots, x2, x1, gain_m, gain_s, qkv, pack, after):
    tp = len(pack)
    rows, d = cot.shape
    return pl.pallas_call(
        functools.partial(self_backward_body, tp, len(gots)),
        out_shape=(
            shape((rows, d), BF),
            shape((rows, 3 * d), BF),
            shape((rows, d), F32),
            shape((rows, d), BF),
            shape((8, d), F32),
        ),
        in_specs=[VM] * (7 + len(gots)) + [ANY] * (len(pack) + len(after)),
        out_specs=[VM] * 5,
        scratch_shapes=[
            pltpu.VMEM((d, d), BF),
            pltpu.VMEM((d, 3 * d), BF),
            pltpu.VMEM((rows, d), F32),
            pltpu.VMEM((rows, d), BF),
            pltpu.VMEM((rows, d), F32),
            pltpu.SemaphoreType.DMA((2,)),
        ],
        compiler_params=params(),
        cost_estimate=cost(27),
        name="self_backward",
    )(cot, gnm, x2, x1, gain_m, gain_s, qkv, *gots, *pack, *after)


def cross_backward_body(tp, idx, lens, b1, g1, x0, gain_c, q, kv, *refs):
    n = tp
    parts = pack_parts(refs[:n], tp, None)
    dq, dkv, g0, emb, vec, wo_b, wq_b, gco, gnc, dacc, kv_b, sems = refs[-12:]
    rows, d = b1.shape
    w = d // tp
    wq_c = col_copies(parts, 0, w, wq_b, sems.at[0])
    wo_c = block_copies(parts, w, w, wo_b, sems.at[1])
    kv_c = [pltpu.make_async_copy(kv, kv_b, sems.at[2])]
    begin(wo_c)
    begin(kv_c)
    begin(wq_c)
    vec[...] = jnp.zeros_like(vec)
    emb[...] = jnp.zeros_like(emb)
    ext = kv.shape[0]

    @pl.loop(0, ext // PB)
    def _(i):
        dacc[rows_at(i, PB), :] = jnp.zeros((PB, dacc.shape[1]), F32)

    finish(wo_c)
    gco[...] = nt(b1[...], wo_b[...]).astype(BF)
    finish(kv_c)

    @pl.loop(0, rows // PB)
    def _(g):
        s = rows_at(g, PB)
        at = [rows_at(idx[g * NB + n], PB) for n in range(NB)]
        row = lax.broadcasted_iota(jnp.int32, (PB, PB), 0)
        live = jnp.concatenate([(row < lens[g * NB + n]).astype(jnp.int32) for n in range(NB)], axis=0) > 0
        for p in range(tp):
            for h in range(w // HD):
                c = p * w + h * HD
                k0 = p * 2 * w + h * HD
                v0 = k0 + w
                k = jnp.concatenate([kv_b[a, k0 : k0 + HD] for a in at], axis=0)
                v = jnp.concatenate([kv_b[a, v0 : v0 + HD] for a in at], axis=0)
                qh = q[s, c : c + HD]
                do = gco[s, c : c + HD]
                pr = softmax_parts(jnp.where(live, nt(k, qh), NEG), 0)
                dp = nt(v, do)
                ds = (pr * (dp - jnp.sum(dp * pr, axis=0, keepdims=True))).astype(BF)
                dq[s, c : c + HD] = (tn(ds, k) * SCALE).astype(BF)
                dk = nn(ds, qh)
                dv = nn(pr.astype(BF), do)
                for j, a in enumerate(at):
                    dacc[a, k0 : k0 + HD] += dk[j * PB : (j + 1) * PB, :]
                    dacc[a, v0 : v0 + HD] += dv[j * PB : (j + 1) * PB, :]

    @pl.loop(0, ext // PB)
    def _(i):
        s = rows_at(i, PB)
        for p in range(tp):
            k0 = p * 2 * w
            dkv[s, k0 : k0 + w] = (dacc[s, k0 : k0 + w] * SCALE).astype(BF)
            dkv[s, k0 + w : k0 + 2 * w] = dacc[s, k0 + w : k0 + 2 * w].astype(BF)

    finish(wq_c)
    gnc[...] = nt(dq[...], wq_b[...])

    @pl.loop(0, rows // PB)
    def _(i):
        s = rows_at(i, PB)
        u = gnc[s, :]
        xhat, r = normalise(x0[s, :])
        y = g1[s, :] + norm_back(u, xhat, r, gain_c[...])
        g0[s, :] = y.astype(BF)
        emb[...] += y
        vec[0:1, :] += colsum(u * xhat)


def cross_backward(idx, lens, b1, g1, x0, gain_c, q, kv, pack, after):
    tp = len(pack)
    rows, d = b1.shape
    ext = kv.shape[0]
    return pl.pallas_call(
        functools.partial(cross_backward_body, tp),
        out_shape=(
            shape((rows, d), BF),
            shape((ext, 2 * d), BF),
            shape((rows, d), BF),
            shape((PB, d), F32),
            shape((8, d), F32),
        ),
        in_specs=[SM] * 2 + [VM] * 5 + [ANY] * (1 + len(pack) + len(after)),
        out_specs=[VM] * 5,
        scratch_shapes=[
            pltpu.VMEM((d, d), BF),
            pltpu.VMEM((d, d), BF),
            pltpu.VMEM((rows, d), BF),
            pltpu.VMEM((rows, d), F32),
            pltpu.VMEM((ext, 2 * d), F32),
            pltpu.VMEM((ext, 2 * d), BF),
            pltpu.SemaphoreType.DMA((3,)),
        ],
        compiler_params=params(),
        cost_estimate=cost(35),
        name="cross_backward",
    )(idx, lens, b1, g1, x0, gain_c, q, kv, *pack, *after)


def tn_into(out, lo, left, right, extra):
    n = left.shape[1]
    tile = min(256, n)
    for k in range(n // tile):
        r = slice(lo + k * tile, lo + (k + 1) * tile)
        y = tn(left[:, k * tile : (k + 1) * tile], right[...])
        if extra is not None:
            y = y + extra[r, :].astype(F32)
        out[r, :] = y.astype(BF)


def two(ref):
    n = ref.shape[0] // 2
    return ref.at[pl.ds(0, n), :], ref.at[pl.ds(n, n), :]


def self_weights_body(ns, dqkv, o, b2, *refs):
    ea, eb = two(refs[0]) if len(refs) > 1 else (None, None)
    a, b = two(refs[-1])
    w = o.shape[1]
    tn_into(a, 0, dqkv.at[:, pl.ds(0, w)], ns, ea)
    tn_into(b, 0, dqkv.at[:, pl.ds(w, 2 * w)], ns, eb)
    tn_into(a, w, o, b2, ea)


def column_block(x, p, n):
    return pl.BlockSpec((x.shape[0], n), lambda i: (0, p))


def whole_block(x):
    return pl.BlockSpec(x.shape, lambda i: (0, 0))


def self_weights(p, w, ns, dqkv, o, b2, came, late):
    d = ns.shape[1]
    return pl.pallas_call(
        lambda *refs: self_weights_body(*refs[: 4 + len(came)], refs[-1]),
        grid=(1,),
        out_shape=shape((4 * w, d), BF),
        in_specs=[whole_block(ns), column_block(dqkv, p, 3 * w), column_block(o, p, w), whole_block(b2)]
        + [whole_block(x) for x in came]
        + [ANY] * len(late),
        out_specs=pl.BlockSpec((4 * w, d), lambda i: (0, 0)),
        compiler_params=params(),
        cost_estimate=cost(4),
        name="self_weights",
    )(ns, dqkv, o, b2, *came, *late)


def cross_weights_body(nc, dq, o, b1, dkv, points, came0, came1, *refs):
    ext_b, sem = refs[-2:]
    came, outs = (refs[:1], refs[1:-2]) if len(refs) == 5 else ((), refs[:-2])
    ea, eb = two(came[0]) if came else (None, None)
    a, b = outs if len(outs) == 2 else two(outs[0])
    half = ext_b.shape[0] // 2
    copies = row_copies([came0, came1], ext_b, sem) + [
        pltpu.make_async_copy(points.at[pl.ds(0, half), :], ext_b.at[pl.ds(half, half), :], sem)
    ]
    begin(copies)
    w = o.shape[1]
    tn_into(a, 0, dq, nc, ea)
    tn_into(a, w, o, b1, ea)
    finish(copies)
    tn_into(b, 0, dkv, ext_b, eb)


def cross_weights(p, w, nc, dq, o, b1, dkv, points, came_points, came, late):
    d = nc.shape[1]
    rows = [4 * w] if p % 2 else [2 * w] * 2
    n, k = 8 + len(came), 2 + len(rows)
    return pl.pallas_call(
        lambda *refs: cross_weights_body(*refs[:n], *refs[-k:]),
        grid=(1,),
        out_shape=[shape((r, d), BF) for r in rows],
        in_specs=[
            whole_block(nc),
            column_block(dq, p, w),
            column_block(o, p, w),
            whole_block(b1),
            column_block(dkv, p, 2 * w),
        ]
        + [ANY] * 3
        + [whole_block(x) for x in came]
        + [ANY] * len(late),
        out_specs=[pl.BlockSpec((r, d), lambda i: (0, 0)) for r in rows],
        scratch_shapes=[pltpu.VMEM((dkv.shape[0], d), BF), pltpu.SemaphoreType.DMA],
        compiler_params=params(),
        cost_estimate=cost(8),
        name="cross_weights",
    )(nc, dq, o, b1, dkv, points, *came_points, *came, *late)


def flip(x, axis, bit):
    n = lax.axis_size(axis)
    return lax.ppermute(x, axis, [(i, i ^ (1 << bit)) for i in range(n)])


def bits_of(axis):
    return (lax.axis_size(axis) - 1).bit_length()


def bit_at(axis, bit):
    return (lax.axis_index(axis) >> bit) & 1


def gather_pieces(own, *late):
    have = {0: own}
    for bit in reversed(range(bits_of("tp"))):
        for p in list(have):
            x = have[p] if bit > 0 or p == 0 or not late else after(have[p], *late)
            have[p | (1 << bit)] = flip(x, "tp", bit)
    return [have[p] for p in range(len(have))]


def in_order(pieces):
    x = jnp.stack(pieces)
    for bit in range(bits_of("tp")):
        y = x.reshape((-1, 2, 1 << bit) + x.shape[1:])
        x = jnp.where(bit_at("tp", bit) == 1, y[:, ::-1], y).reshape(x.shape)
    return x


def add(*xs, late=()):
    return after(functools.reduce(jnp.add, [x.astype(F32) for x in xs]).astype(BF), *late)


def after(x, *deps):
    ok = True
    for v in deps:
        first = v[(0,) * v.ndim]
        ok = jnp.logical_and(ok, first == first)
    return jnp.where(ok, x, jnp.zeros_like(x))


def over_tp(have, bit, late=()):
    out = {p: v for p, v in have.items() if not p >> bit & 1}
    for p, v in have.items():
        if p >> bit & 1:
            q = p ^ (1 << bit)
            out[q] = add(out[q], flip(v, "tp", bit), late=late)
    return out


def over_y(have, late=()):
    for k in reversed(range(1, bits_of("tp"))):
        have = over_tp(have, k, late)
    return have


def flip_x(v):
    return lax.ppermute(v, "x", [(0, 1), (1, 0)])


def over_x(v, late=()):
    nz = lax.axis_size("z")
    v = v.reshape((nz, 2, v.shape[0] // (2 * nz)) + v.shape[1:])
    x = lax.axis_index("x")
    keep = lax.dynamic_index_in_dim(v, x, 1, keepdims=False)
    return add(keep, flip_x(lax.dynamic_index_in_dim(v, 1 - x, 1, keepdims=False)), late=late)


def sum_z(v):
    return lax.psum(v, "z")


def to_groups(x, per):
    lat, groups, w = x.shape
    n = groups // per
    tp = lax.axis_size("tp")
    y = jnp.transpose(x.reshape(lat, n, per, w), (1, 2, 0, 3))
    y = lax.all_to_all(y, ("z", "x", "tp"), split_axis=0, concat_axis=0, tiled=True)
    y = jnp.transpose(y.reshape(n // tp, tp, per, lat, w), (2, 0, 3, 1, 4))
    return y.reshape(per * lat * (n // tp), tp * w)


def from_groups(x, per):
    tp = lax.axis_size("tp")
    n = lax.axis_size(GRP) * tp
    rows, d = x.shape
    lat, w = rows // per // (n // tp), d // tp
    y = jnp.transpose(x.reshape(per, n // tp, lat, tp, w), (1, 3, 0, 2, 4)).reshape(n, per, lat, w)
    y = lax.all_to_all(y, ("z", "x", "tp"), split_axis=0, concat_axis=0, tiled=True)
    return jnp.transpose(y, (2, 0, 1, 3)).reshape(lat, n * per, w)


def per_device(
    latents,
    skip_latents,
    points,
    neighbours,
    block_lengths,
    latent_embed,
    gain_cross,
    query_cross,
    key_cross,
    value_cross,
    output_cross,
    bias_cross,
    gain_self,
    query_self,
    key_self,
    value_self,
    output_self,
    bias_self,
    gain_mlp,
    hidden_weight,
    hidden_bias,
    output_weight,
    output_bias,
    cotangent,
):
    tp, grp = lax.axis_size("tp"), lax.axis_size(GRP)
    t, i = lax.axis_index("tp"), lax.axis_index(GRP)
    d = query_cross.shape[0]
    w = latent_embed.shape[1]
    lat_rows = latent_embed.shape[0]
    ff = hidden_weight.shape[1]
    groups_here = neighbours.shape[0]
    groups = groups_here * grp
    per = groups_here // tp
    blocks_here = points.shape[0] // PB
    all_blocks = blocks_here * grp
    half_rows = points.shape[0] // 2

    kv_own = packed([[key_cross, value_cross]])[0]
    share = half_rows // 2
    core = bit_at("tp", 0)
    sent = part_of(points, (2 + core).astype(jnp.int32).reshape(1), share, [kv_own])
    first = lax.ppermute(sent, GRP, [(k, (k + 1) % grp) for k in range(grp)])
    came_points = [first, flip(first, "tp", 0)]
    near = lax.dynamic_slice_in_dim(neighbours, t * per, per, 0).reshape(per * NB)
    block = (near - (i * blocks_here - blocks_here // 2)) % all_blocks
    share_blocks = share // PB
    moved = ((block // share_blocks) ^ core) * share_blocks + block % share_blocks
    idx = jnp.where(block < blocks_here // 2, moved, block).astype(jnp.int32)
    lens = block_lengths[near]

    kv_pack = gather_pieces(kv_own)
    qo_own = packed([[query_cross, output_cross]], [kv_own])[0]
    qo_pack = gather_pieces(qo_own)

    small = jnp.concatenate(
        [
            after(latent_embed, kv_own),
            bias_cross[None],
            bias_self[None],
            output_bias[None],
            hidden_bias.reshape(ff // w, w),
        ]
    )
    small_pieces = gather_pieces(small)
    small_all = in_order(small_pieces)
    by_rows = jnp.transpose(small_all, (1, 0, 2)).reshape(small.shape[0], d)
    embed = by_rows[:lat_rows]
    bias_c, bias_s, bias_o = (by_rows[lat_rows + k : lat_rows + k + 1] for k in range(3))
    hid_bias = jnp.stack([piece[lat_rows + 3 :].reshape(ff) for piece in small_pieces[:2]])

    whid = [hidden_weight, flip(hidden_weight, "tp", 0)]
    wout = [output_weight, flip(output_weight, "tp", 0)]

    gain_c, gain_s, gain_m = gain_cross[None], gain_self[None], gain_mlp[None]
    rows = per * lat_rows
    x0 = (
        to_groups(after(latents, kv_own), per).astype(F32).reshape(per, lat_rows, d) + embed[None]
    ).reshape(rows, d)
    self_own = packed([[query_self, key_self, value_self, output_self]], [qo_pack[2]])[0]
    kv = keys_values(points, came_points, kv_pack, [x0, self_own])
    q, oc, x1, nc, ns = cross_forward(idx, lens, x0, gain_c, gain_s, bias_c, kv, qo_pack)
    self_pack = gather_pieces(self_own, x1)
    cot = after(to_groups(after(cotangent, x0), per), x1)
    qkv, os, x2, nm = self_forward(ns, x1, gain_m, bias_s, self_pack, [cot])

    steps = list(range(2, tp, 2))

    def swap(x, k):
        return lax.ppermute(x, "tp", [(j, j ^ k) for j in range(tp)])

    other_cot = [swap(cot, k) for k in steps]
    other_nm = [swap(nm, k) for k in steps]
    acts, gbs, hbgs = [], [], []
    act, gb, out, gnm, hbg = feed(nm, cot, hid_bias, whid, wout, F32, other_cot)
    acts.append(act)
    gbs.append(gb)
    hbgs.append(hbg)
    back_out, back_gnm = [], []
    for k, n_k, c_k in zip(steps, other_nm, other_cot):
        act, gb, o_k, g_k, hbg = feed(n_k, c_k, hid_bias, whid, wout, BF)
        acts.append(act)
        gbs.append(gb)
        hbgs.append(hbg)
        back_gnm.append(swap(g_k, k))
        back_out.append(o_k)
    nms, cots = [nm] + other_nm, [cot] + other_cot
    sent_o = feed_weights(1, acts, cots, [])
    sent_h = feed_weights(1, gbs, nms, [])
    own_o = feed_weights(0, acts, cots, [flip(sent_o, "tp", 0)])
    own_h = feed_weights(0, gbs, nms, [flip(sent_h, "tp", 0)])

    b2, dqkv, g1, b1, vec_s = self_backward(
        cot, gnm, back_gnm, x2, x1, gain_m, gain_s, qkv, self_pack, [own_o, own_h]
    )

    def pieces(weights, waits):
        got, out, late = {}, {}, []
        for p in reversed(range(1, tp, 2)):
            x = weights(p, [], waits(p, late) + late)
            late = [x]
            got[p - 1] = flip(x, "tp", 0)
        for p in reversed(range(0, tp, 2)):
            out[p] = weights(p, [got[p]], waits(p, late) + late)
            late = [out[p][0] if isinstance(out[p], (list, tuple)) else out[p]]
        return out

    x3 = x2 + out + bias_o
    for k, o_k in zip(steps, back_out):
        x3 = x3 + swap(after(o_k, own_h), k).astype(F32)
    leaving = after(x3.astype(BF), b2)
    sum_o, sum_h = over_x(own_o, [b2]), over_x(own_h, [b2])
    sum_f = jnp.concatenate([sum_o, sum_h], axis=1)
    selfs = pieces(
        lambda p, came, late: self_weights(p, w, ns, dqkv, os, b2, came, late),
        lambda p, late: [sum_f, leaving] if p == tp - 1 else [],
    )
    last = selfs[0]
    feed_z = sum_z(sum_f)
    restored = from_groups(after(leaving, selfs[tp - 2]), per)

    dq, dkv, g0, emb, vec_c = cross_backward(
        idx, lens, b1, g1, x0, gain_c, q, kv, qo_pack, [leaving, *selfs.values()]
    )
    stage = {}

    def norms_and_small(late):
        block_out = after(restored, *late).astype(F32) + skip_latents.astype(F32)
        squares = jnp.sum(jnp.square(block_out), axis=(0, 2))
        by_share = jnp.transpose(
            jnp.concatenate([emb, vec_s[:5], vec_c[:1]]).reshape(lat_rows + 6, tp, w), (1, 0, 2)
        )
        hb_all = functools.reduce(jnp.add, hbgs).reshape(2, ff // w, w)
        owner = lax.broadcasted_iota(jnp.int32, (tp, 1, 1), 0)
        hb_share = jnp.where(owner == t, hb_all[0][None], 0.0) + jnp.where(
            owner == (t ^ 1), hb_all[1][None], 0.0
        )
        sq_rows = jnp.pad(squares, (0, norm_rows * w - groups)).reshape(1, norm_rows, w)
        x = jnp.concatenate(
            [by_share, hb_share, jnp.broadcast_to(sq_rows, (tp, norm_rows, w))], axis=1
        )
        x = jnp.pad(x, ((0, 0), (0, -x.shape[1] % 8), (0, 0)))
        for bit in reversed(range(bits_of("tp"))):
            n = x.shape[0] // 2
            mine = bit_at("tp", bit)
            keep = lax.dynamic_slice_in_dim(x, mine * n, n, 0)
            x = keep + flip(lax.dynamic_slice_in_dim(x, (1 - mine) * n, n, 0), "tp", bit)
        x = x[0].reshape(-1)
        places_rows = 2 * lax.axis_size("z") * 8
        rows_all = -(-x.shape[0] // (d * places_rows)) * places_rows
        return block_out, jnp.pad(x, (0, rows_all * d - x.shape[0])).reshape(rows_all, d).astype(BF)

    norm_rows = -(-groups // w)

    def waits(p, late):
        if p == tp - 1:
            stage["self"] = over_y(selfs, [emb])[0]
            return [stage["self"], restored]
        if p == tp - 3:
            return []
        if p == tp - 2:
            n = stage["self"].shape[0] // 2
            stage["self"] = [over_x(stage["self"][:n], late), over_x(stage["self"][n:], late)]
            return stage["self"] + [feed_z]
        if p == 0:
            stage["self"] = after(jnp.concatenate(stage["self"], axis=1), *late)
            stage["out"], stage["small"] = norms_and_small(late)
            return [stage["small"]]
        return []

    def cross_piece(p, came, late):
        x = cross_weights(p, w, nc, dq, oc, b1, dkv, points, came_points, came, late)
        return x[0] if p % 2 else x

    cross = pieces(cross_piece, waits)
    late = [cross[0][0]]
    self_z = sum_z(stage["self"])
    cross_a = over_y({p: v[0] for p, v in cross.items()})[0]
    cross_b = over_y({p: over_x(v[1], [feed_z]) for p, v in cross.items()})[0]
    little = over_x(stage["small"])
    cross_z = jnp.concatenate([over_x(cross_a, [self_z]), cross_b, little], axis=1)
    feed_z, self_z = after(feed_z, cross_z), after(self_z, cross_z)
    self_x, feed_x = flip_x(self_z), flip_x(feed_z)
    returned = from_groups(after(g0, cross_z), per)
    cross_z = after(sum_z(cross_z), self_x)
    cross_x = flip_x(cross_z)
    n = little.shape[1]
    low = lax.axis_index("x") == 0
    own_n, other_n = cross_z[:, -n:], cross_x[:, -n:]
    total = jnp.where(low, jnp.stack([own_n, other_n], 1), jnp.stack([other_n, own_n], 1))
    total = total.astype(F32).reshape(-1)
    total = total[: total.shape[0] // w * w].reshape(-1, w)
    places = lax.axis_index("x").astype(jnp.int32).reshape(1)
    output_weight_grad, hidden_weight_grad = final_feed(places, feed_z, feed_x)
    query_self_grad, key_self_grad, value_self_grad, output_self_grad = final(
        places, w, self_z, self_x
    )
    block_out = stage["out"]
    latents_grad = returned.astype(F32)

    query_cross_grad, key_cross_grad, value_cross_grad, output_cross_grad = final(
        places, w, cross_z, cross_x, [output_weight_grad, hidden_weight_grad, output_self_grad]
    )
    embed_grad = total[:lat_rows]
    (
        output_bias_grad,
        gain_mlp_grad,
        bias_self_grad,
        gain_self_grad,
        bias_cross_grad,
        gain_cross_grad,
    ) = (total[lat_rows + k] for k in range(6))
    at = lat_rows + 6
    hidden_bias_grad = total[at : at + ff // w].reshape(ff)
    at += ff // w
    square_sums = total[at : at + norm_rows].reshape(norm_rows * w)[:groups]
    group_norms = jnp.sqrt(square_sums / (lat_rows * d))

    return (
        block_out,
        group_norms,
        latents_grad,
        embed_grad,
        gain_cross_grad,
        query_cross_grad,
        key_cross_grad,
        value_cross_grad,
        output_cross_grad,
        bias_cross_grad,
        gain_self_grad,
        query_self_grad,
        key_self_grad,
        value_self_grad,
        output_self_grad,
        bias_self_grad,
        gain_mlp_grad,
        hidden_weight_grad,
        hidden_bias_grad,
        output_weight_grad,
        output_bias_grad,
    )


def solution(mesh):
    grp, tp = mesh.shape["grp"], mesh.shape["tp"]
    own = jax.sharding.Mesh(mesh.devices.reshape(grp // 2, 2, tp), GRP + ("tp",))
    lay = P(GRP, None, "tp")
    cols, rows, part = P(None, "tp"), P("tp", None), P("tp")
    attn = (P(), cols, cols, cols, rows, part)
    return jax.shard_map(
        per_device,
        mesh=own,
        in_specs=(lay, lay, P(GRP, None), P(GRP, None), P(), cols)
        + attn
        + attn
        + (P(), cols, part, rows, part, lay),
        out_specs=(lay, P(), lay, cols)
        + (part, cols, cols, cols, rows, part)
        + (part, cols, cols, cols, rows, part)
        + (part, cols, part, rows, part),
        check_vma=False,
    )
```

```python
import functools

import jax
import jax.numpy as jnp
from jax import lax
from jax.experimental import pallas as pl
from jax.experimental.pallas import tpu as pltpu
from jax.sharding import PartitionSpec as P

HD = 128
PB = 128
NB = 4
EPS = 1e-05
NEG = -1e30
SCALE = HD ** (-0.5)
BF = jnp.bfloat16
F32 = jnp.float32
GRP = ("z", "x")

ANY = pl.BlockSpec(memory_space=pl.ANY)
VM = pl.BlockSpec(memory_space=pltpu.VMEM)
SM = pl.BlockSpec(memory_space=pltpu.SMEM)


def shape(dims, kind):
    return jax.ShapeDtypeStruct(dims, kind)


def params(mib):
    return pltpu.CompilerParams(vmem_limit_bytes=mib * 2**20)


def cost(us):
    return pl.CostEstimate(flops=int(us * 1.1e9), bytes_accessed=int(us * 1e6), transcendentals=0)


def nn(left, right):
    return lax.dot_general(left, right, (((1,), (0,)), ((), ())), preferred_element_type=F32)


def nt(left, right):
    return lax.dot_general(left, right, (((1,), (1,)), ((), ())), preferred_element_type=F32)


def tn(left, right):
    return lax.dot_general(left, right, (((0,), (0,)), ((), ())), preferred_element_type=F32)


def rows_at(i, n):
    return pl.ds(pl.multiple_of(i * n, n), n)


def normalise(x):
    d = x - jnp.mean(x, axis=1, keepdims=True)
    r = lax.rsqrt(jnp.mean(d * d, axis=1, keepdims=True) + EPS)
    return d * r, r


def norm_back(u, xhat, r, gain):
    w = u * gain
    a = jnp.mean(w, axis=1, keepdims=True)
    b = jnp.mean(w * xhat, axis=1, keepdims=True)
    return r * (w - a - xhat * b)


def colsum(x):
    return jnp.sum(x, axis=0, keepdims=True)


def begin(copies):
    for c in copies:
        c.start()


def finish(copies):
    for c in copies:
        c.wait()


def row_copies(pieces, buf, sem):
    n = pieces[0].shape[0]
    return [pltpu.make_async_copy(s, buf.at[pl.ds(p * n, n), :], sem) for p, s in enumerate(pieces)]


def pack_parts(refs, tp, place):
    if len(refs) == tp:
        return [(p, None, r) for p, r in enumerate(refs)]
    parts = [(0, None, refs[0]), (1, None, refs[1])]
    for p in range(2, tp):
        parts.append((p, place[0], refs[2 * p - 2]))
        parts.append((p, 1 - place[0], refs[2 * p - 1]))
    return parts


def col_copies(parts, at, n, buf, sem):
    out = []
    for p, h, r in parts:
        to = pl.ds(p * n, n)
        k = r.shape[0]
        dst = buf.at[:, to] if h is None else buf.at[rows_at(h, k), to]
        out.append(pltpu.make_async_copy(r.at[:, pl.ds(at, n)], dst, sem))
    return out


def block_copies(parts, at, w, buf, sem):
    out = []
    for p, h, r in parts:
        count = r.shape[0] // w
        for k in range(count):
            col = k * w if h is None else pl.multiple_of((h * count + k) * w, 128)
            src = r.at[pl.ds(k * w, w), pl.ds(at, w)]
            out.append(pltpu.make_async_copy(src, buf.at[pl.ds(p * w, w), pl.ds(col, w)], sem))
    return out


def softmax_parts(s, axis):
    e = jnp.exp((s - jnp.max(s, axis=axis, keepdims=True)) * SCALE)
    return e * (1.0 / jnp.sum(e, axis=axis, keepdims=True))


def pack_body(counts, *refs):
    outs, at = refs[-len(counts) :], 0
    for n, out in zip(counts, outs):
        col, rows = 0, out.shape[0]
        for r in refs[at : at + n]:
            if r.shape[0] == rows:
                out[:, col : col + r.shape[1]] = r[...]
                col += r.shape[1]
            else:
                w = r.shape[0]
                for k in range(rows // w):
                    out[k * w : (k + 1) * w, col : col + w] = r[:, k * w : (k + 1) * w]
                col += w
        at += n


def packed(groups, late=()):
    counts = [len(g) for g in groups]
    ins = [x for g in groups for x in g]
    rows = groups[0][0].shape[0]
    outs = []
    for g in groups:
        cols = sum(x.shape[1] if x.shape[0] == rows else x.shape[0] for x in g)
        outs.append(shape((rows, cols), g[0].dtype))
    n = len(ins)
    return pl.pallas_call(
        lambda *refs: pack_body(counts, *refs[:n], *refs[n + len(late) :]),
        out_shape=outs,
        in_specs=[VM] * n + [ANY] * len(late),
        out_specs=[VM] * len(outs),
        compiler_params=params(12),
        cost_estimate=cost(2),
        name="packed",
    )(*ins, *late)


def part_body(n, at, x, *refs):
    out, sem = refs[-2:]
    copy = pltpu.make_async_copy(x.at[pl.ds(pl.multiple_of(at[0] * n, n), n), :], out, sem)
    copy.start()
    copy.wait()


def part_of(x, at, n, late=()):
    return pl.pallas_call(
        functools.partial(part_body, n),
        out_shape=shape((n, x.shape[1]), x.dtype),
        in_specs=[SM] + [ANY] * (1 + len(late)),
        out_specs=VM,
        scratch_shapes=[pltpu.SemaphoreType.DMA],
        cost_estimate=cost(1),
        name="part_of",
    )(at, x, *late)


def share_copies(places, parts, bufs, sem):
    out = []
    for r, x in zip(parts, (places[0], 1 - places[0])):
        c = bufs[0].shape[0] // (2 * r.shape[0])
        for z in range(r.shape[0]):
            for j, buf in enumerate(bufs):
                src = r.at[z, pl.ds(j * c, c), :]
                out.append(pltpu.make_async_copy(src, buf.at[rows_at(2 * z + x, c), :], sem))
    return out


def final_body(places, own, other, *refs):
    q, k, v, o, qo_b, kv_b, sem = refs[-7:]
    copies = share_copies(places, (own, other), (qo_b, kv_b), sem)
    begin(copies)
    finish(copies)
    w = o.shape[0]
    q[...] = qo_b[0:w, :].astype(F32).T
    o[...] = qo_b[w : 2 * w, :].astype(F32)
    k[...] = kv_b[0:w, :].astype(F32).T
    v[...] = kv_b[w : 2 * w, :].astype(F32).T


def final(places, w, own, other, late=()):
    d = own.shape[2]
    tall, flat = shape((d, w), F32), shape((w, d), F32)
    return pl.pallas_call(
        final_body,
        out_shape=(tall, tall, tall, flat),
        in_specs=[SM] + [ANY] * (2 + len(late)),
        out_specs=[VM] * 4,
        scratch_shapes=[pltpu.VMEM((2 * w, d), BF)] * 2 + [pltpu.SemaphoreType.DMA],
        compiler_params=params(58),
        cost_estimate=cost(5),
        name="final",
    )(places, own, other, *late)


def final_feed_body(places, own, other_o, other_h, out, hid, out_b, hid_b, sem):
    c = other_o.shape[1]
    copies = []
    for z in range(own.shape[0]):
        here, there = rows_at(2 * z + places[0], c), rows_at(2 * z + 1 - places[0], c)
        for k, (other, buf) in enumerate(((other_o, out_b), (other_h, hid_b))):
            src = own.at[z, pl.ds(k * c, c), :]
            copies.append(pltpu.make_async_copy(src, buf.at[here, :], sem))
            copies.append(pltpu.make_async_copy(other.at[z], buf.at[there, :], sem))
    begin(copies)
    finish(copies)
    out[...] = out_b[...].astype(F32)
    hid[...] = hid_b[...].astype(F32).T


def final_feed(places, own, other_o, other_h):
    nz, c, d = own.shape
    ff = nz * c
    return pl.pallas_call(
        final_feed_body,
        out_shape=(shape((ff, d), F32), shape((d, ff), F32)),
        in_specs=[SM] + [ANY] * 3,
        out_specs=[VM] * 2,
        scratch_shapes=[pltpu.VMEM((ff, d), BF)] * 2 + [pltpu.SemaphoreType.DMA],
        compiler_params=params(58),
        cost_estimate=cost(6),
        name="final_feed",
    )(places, own, other_o, other_h)


def keys_body(tp, points, came0, came1, *refs):
    packs, (kv, kv_b, ext_b, wkv_b, sems) = refs[:tp], refs[-5:]
    ext, d = ext_b.shape
    half = ext // 2
    near_c = [pltpu.make_async_copy(points.at[pl.ds(0, half), :], ext_b.at[pl.ds(half, half), :], sems.at[0])]
    far_c = row_copies([came0, came1], ext_b, sems.at[1])
    w_c = col_copies(pack_parts(packs, tp, None), 0, packs[0].shape[1], wkv_b, sems.at[2])
    for c in (w_c, near_c, far_c):
        begin(c)
    finish(w_c)
    span = 512

    def out_copy(i):
        s = rows_at(i, span)
        return pltpu.make_async_copy(kv_b.at[s, :], kv.at[s, :], sems.at[3])

    def work(i):
        s = rows_at(i, span)
        kv_b[s, :] = nn(ext_b[s, :], wkv_b[...]).astype(BF)
        out_copy(i).start()

    finish(near_c)
    pl.loop(half // span, ext // span)(work)
    finish(far_c)
    pl.loop(0, half // span)(work)

    @pl.loop(0, ext // span)
    def _(i):
        out_copy(i).wait()


def keys_values(points, came, packs, late):
    tp = len(packs)
    ext, d = points.shape
    return pl.pallas_call(
        functools.partial(keys_body, tp),
        out_shape=shape((ext, 2 * d), BF),
        in_specs=[ANY] * (3 + tp + len(late)),
        out_specs=ANY,
        scratch_shapes=[
            pltpu.VMEM((ext, 2 * d), BF),
            pltpu.VMEM((ext, d), BF),
            pltpu.VMEM((d, 2 * d), BF),
            pltpu.SemaphoreType.DMA((4,)),
        ],
        compiler_params=params(58),
        cost_estimate=cost(14),
        name="keys_values",
    )(points, *came, *packs, *late)


def cross_forward_body(tp, idx, lens, x0, gain_c, gain_s, bias, kv, *refs):
    parts = pack_parts(refs[:tp], tp, None)
    (q, o, x1, nc, ns, kv_b, wq_b, wo_b, acc, sems) = refs[-10:]
    rows, d = x0.shape
    w = d // tp
    wq_c = col_copies(parts, 0, w, wq_b, sems.at[0])
    wo_c = block_copies(parts, w, w, wo_b, sems.at[1])
    kv_c = [pltpu.make_async_copy(kv, kv_b, sems.at[2])]
    for c in (wq_c, kv_c, wo_c):
        begin(c)

    @pl.loop(0, rows // PB)
    def _(i):
        s = rows_at(i, PB)
        xhat, _ = normalise(x0[s, :])
        nc[s, :] = (xhat * gain_c[...]).astype(BF)

    finish(wq_c)
    q[...] = nn(nc[...], wq_b[...]).astype(BF)
    finish(kv_c)

    @pl.loop(0, rows // PB)
    def _(g):
        s = rows_at(g, PB)
        at = [rows_at(idx[g * NB + n], PB) for n in range(NB)]
        lane = lax.broadcasted_iota(jnp.int32, (1, PB), 1)
        live = jnp.concatenate([(lane < lens[g * NB + n]).astype(jnp.int32) for n in range(NB)], axis=1) > 0
        for p in range(tp):
            for h in range(w // HD):
                c = p * w + h * HD
                k0 = p * 2 * w + h * HD
                k = jnp.concatenate([kv_b[a, k0 : k0 + HD] for a in at], axis=0)
                v = jnp.concatenate([kv_b[a, k0 + w : k0 + w + HD] for a in at], axis=0)
                pr = softmax_parts(jnp.where(live, nt(q[s, c : c + HD], k), NEG), 1)
                o[s, c : c + HD] = nn(pr.astype(BF), v).astype(BF)

    finish(wo_c)
    acc[...] = nn(o[...], wo_b[...])

    @pl.loop(0, rows // PB)
    def _(i):
        s = rows_at(i, PB)
        y = x0[s, :] + acc[s, :] + bias[...]
        x1[s, :] = y
        xhat, _ = normalise(y)
        ns[s, :] = (xhat * gain_s[...]).astype(BF)


def cross_forward(idx, lens, x0, gain_c, gain_s, bias, kv, packs):
    tp = len(packs)
    rows, d = x0.shape
    ext = kv.shape[0]
    return pl.pallas_call(
        functools.partial(cross_forward_body, tp),
        out_shape=(
            shape((rows, d), BF),
            shape((rows, d), BF),
            shape((rows, d), F32),
            shape((rows, d), BF),
            shape((rows, d), BF),
        ),
        in_specs=[SM] * 2 + [VM] * 4 + [ANY] * (1 + tp),
        out_specs=[VM] * 5,
        scratch_shapes=[
            pltpu.VMEM((ext, 2 * d), BF),
            pltpu.VMEM((d, d), BF),
            pltpu.VMEM((d, d), BF),
            pltpu.VMEM((rows, d), F32),
            pltpu.SemaphoreType.DMA((3,)),
        ],
        compiler_params=params(58),
        cost_estimate=cost(20),
        name="cross_forward",
    )(idx, lens, x0, gain_c, gain_s, bias, kv, *packs)


def self_forward_body(tp, ns, x1, gain_m, bias, *refs):
    n = tp
    parts = pack_parts(refs[:n], tp, None)
    qkv, o, x2, nm, wqkv_b, wo_b, acc, sems = refs[-8:]
    rows, d = x1.shape
    w = d // tp
    wqkv_c = col_copies(parts, 0, 3 * w, wqkv_b, sems.at[0])
    wo_c = block_copies(parts, 3 * w, w, wo_b, sems.at[1])
    begin(wqkv_c)
    begin(wo_c)
    finish(wqkv_c)
    qkv[...] = nn(ns[...], wqkv_b[...]).astype(BF)

    @pl.loop(0, rows // PB)
    def _(g):
        s = rows_at(g, PB)
        for p in range(tp):
            for h in range(w // HD):
                c = p * w + h * HD
                k0 = p * 3 * w + h * HD
                pr = softmax_parts(nt(qkv[s, k0 : k0 + HD], qkv[s, k0 + w : k0 + w + HD]), 1)
                v = qkv[s, k0 + 2 * w : k0 + 2 * w + HD]
                o[s, c : c + HD] = nn(pr.astype(BF), v).astype(BF)

    finish(wo_c)
    acc[...] = nn(o[...], wo_b[...])

    @pl.loop(0, rows // PB)
    def _(i):
        s = rows_at(i, PB)
        y = x1[s, :] + acc[s, :] + bias[...]
        x2[s, :] = y
        xhat, _ = normalise(y)
        nm[s, :] = (xhat * gain_m[...]).astype(BF)


def self_forward(ns, x1, gain_m, bias, pack, late):
    rows, d = x1.shape
    tp = len(pack)
    return pl.pallas_call(
        functools.partial(self_forward_body, tp),
        out_shape=(
            shape((rows, 3 * d), BF),
            shape((rows, d), BF),
            shape((rows, d), F32),
            shape((rows, d), BF),
        ),
        in_specs=[VM] * 4 + [ANY] * (len(pack) + len(late)),
        out_specs=[VM] * 4,
        scratch_shapes=[
            pltpu.VMEM((d, 3 * d), BF),
            pltpu.VMEM((d, d), BF),
            pltpu.VMEM((rows, d), F32),
            pltpu.SemaphoreType.DMA((2,)),
        ],
        compiler_params=params(32),
        cost_estimate=cost(22),
        name="self_forward",
    )(ns, x1, gain_m, bias, *pack, *late)


ROOT = 0.7978845608028654
CUBE = 0.044715


def feed_body(nm, cot, hb, wh0, wh1, wo0, wo1, *refs):
    act, gb, out, gnm, hbg = refs[-5:]
    rows, d = nm.shape
    ff = wh0.shape[1]
    span = min(512, ff)
    for p, (wh, wo) in enumerate(((wh0, wo0), (wh1, wo1))):
        for j in range(ff // span):
            s = slice(j * span, (j + 1) * span)
            x = nn(nm[...], wh[:, s]) + hb[p : p + 1, s]
            ga = nt(cot[...], wo[s, :])
            sq = x * x
            t = jnp.tanh(ROOT * x * (1.0 + CUBE * sq))
            half = 0.5 * (1.0 + t)
            act[p, :, s] = (x * half).astype(BF)
            slope = half + 0.5 * x * (1.0 - t * t) * (ROOT + (3.0 * ROOT * CUBE) * sq)
            g = (ga * slope).astype(BF)
            gb[p, :, s] = g
            hbg[p : p + 1, s] = colsum(g.astype(F32))
    gnm[...] = (nt(gb[0], wh0[...]) + nt(gb[1], wh1[...])).astype(gnm.dtype)
    out[...] = (nn(act[0], wo0[...]) + nn(act[1], wo1[...])).astype(out.dtype)


def feed(nm, cot, hb, wh, wo, kind, late=()):
    rows, d = nm.shape
    ff = wh[0].shape[1]
    return pl.pallas_call(
        feed_body,
        out_shape=(
            shape((2, rows, ff), BF),
            shape((2, rows, ff), BF),
            shape((rows, d), kind),
            shape((rows, d), kind),
            shape((2, ff), F32),
        ),
        in_specs=[VM] * 7 + [ANY] * len(late),
        out_specs=[VM] * 5,
        compiler_params=params(32),
        cost_estimate=cost(15),
        name="feed",
    )(nm, cot, hb, *wh, *wo, *late)


def feed_weights_body(sets, *refs):
    lefts, rights, rest = refs[:sets], refs[sets : 2 * sets], refs[2 * sets :]
    out = rest[-1]
    came = rest[0] if len(rest) == 2 else None
    tile = 256

    @pl.loop(0, out.shape[0] // tile)
    def _(i):
        s = rows_at(i, tile)
        y = functools.reduce(jnp.add, [tn(a[0, :, s], c[...]) for a, c in zip(lefts, rights)])
        if came is not None:
            y = y + came[s, :].astype(F32)
        out[s, :] = y.astype(BF)


def feed_weights(p, lefts, rights, came):
    sets = len(lefts)

    def spec(x):
        if x.ndim == 3:
            return pl.BlockSpec((1,) + x.shape[1:], lambda i: (p, 0, 0))
        return pl.BlockSpec(x.shape, lambda i: (0, 0))

    dims = (lefts[0].shape[-1], rights[0].shape[-1])
    ins = list(lefts) + list(rights) + list(came)
    return pl.pallas_call(
        functools.partial(feed_weights_body, sets),
        grid=(1,),
        out_shape=shape(dims, BF),
        in_specs=[spec(x) for x in ins],
        out_specs=pl.BlockSpec(dims, lambda i: (0, 0)),
        compiler_params=params(16),
        cost_estimate=cost(6),
        name="feed_weights",
    )(*ins)


def self_backward_body(tp, others, cot, gnm, x2, x1, gain_m, gain_s, qkv, *refs):
    gots, refs = refs[:others], refs[others:]
    n = tp
    parts = pack_parts(refs[:n], tp, None)
    b2, dqkv, g1, b1, vec, wo_b, wqkv_b, g2, gso, gns, sems = refs[-11:]
    rows, d = cot.shape
    w = d // tp
    wqkv_c = col_copies(parts, 0, 3 * w, wqkv_b, sems.at[0])
    wo_c = block_copies(parts, 3 * w, w, wo_b, sems.at[1])
    begin(wo_c)
    begin(wqkv_c)
    vec[...] = jnp.zeros_like(vec)

    @pl.loop(0, rows // PB)
    def _(i):
        s = rows_at(i, PB)
        u = functools.reduce(jnp.add, [r[s, :].astype(F32) for r in gots], gnm[s, :])
        xhat, r = normalise(x2[s, :])
        g3 = cot[s, :].astype(F32)
        y = g3 + norm_back(u, xhat, r, gain_m[...])
        g2[s, :] = y
        b2[s, :] = y.astype(BF)
        vec[0:1, :] += colsum(g3)
        vec[1:2, :] += colsum(u * xhat)
        vec[2:3, :] += colsum(y)

    finish(wo_c)
    gso[...] = nt(b2[...], wo_b[...]).astype(BF)

    @pl.loop(0, rows // PB)
    def _(g):
        s = rows_at(g, PB)
        for p in range(tp):
            for h in range(w // HD):
                c = p * w + h * HD
                k0 = p * 3 * w + h * HD
                k1, k2 = k0 + w, k0 + 2 * w
                q, k, v = qkv[s, k0 : k0 + HD], qkv[s, k1 : k1 + HD], qkv[s, k2 : k2 + HD]
                pr = softmax_parts(nt(k, q), 0)
                do = gso[s, c : c + HD]
                dp = nt(v, do)
                ds = (pr * (dp - jnp.sum(dp * pr, axis=0, keepdims=True))).astype(BF)
                dqkv[s, k0 : k0 + HD] = (tn(ds, k) * SCALE).astype(BF)
                dqkv[s, k1 : k1 + HD] = (nn(ds, q) * SCALE).astype(BF)
                dqkv[s, k2 : k2 + HD] = nn(pr.astype(BF), do).astype(BF)

    finish(wqkv_c)
    gns[...] = nt(dqkv[...], wqkv_b[...])

    @pl.loop(0, rows // PB)
    def _(i):
        s = rows_at(i, PB)
        u = gns[s, :]
        xhat, r = normalise(x1[s, :])
        y = g2[s, :] + norm_back(u, xhat, r, gain_s[...])
        g1[s, :] = y
        b1[s, :] = y.astype(BF)
        vec[3:4, :] += colsum(u * xhat)
        vec[4:5, :] += colsum(y)


def self_backward(cot, gnm, gots, x2, x1, gain_m, gain_s, qkv, pack, after):
    tp = len(pack)
    rows, d = cot.shape
    return pl.pallas_call(
        functools.partial(self_backward_body, tp, len(gots)),
        out_shape=(
            shape((rows, d), BF),
            shape((rows, 3 * d), BF),
            shape((rows, d), F32),
            shape((rows, d), BF),
            shape((8, d), F32),
        ),
        in_specs=[VM] * (7 + len(gots)) + [ANY] * (len(pack) + len(after)),
        out_specs=[VM] * 5,
        scratch_shapes=[
            pltpu.VMEM((d, d), BF),
            pltpu.VMEM((d, 3 * d), BF),
            pltpu.VMEM((rows, d), F32),
            pltpu.VMEM((rows, d), BF),
            pltpu.VMEM((rows, d), F32),
            pltpu.SemaphoreType.DMA((2,)),
        ],
        compiler_params=params(44),
        cost_estimate=cost(27),
        name="self_backward",
    )(cot, gnm, x2, x1, gain_m, gain_s, qkv, *gots, *pack, *after)


def cross_backward_body(tp, idx, lens, b1, g1, x0, gain_c, q, kv, *refs):
    n = tp
    parts = pack_parts(refs[:n], tp, None)
    dq, dkv, g0, emb, vec, wo_b, wq_b, gco, gnc, dacc, kv_b, sems = refs[-12:]
    rows, d = b1.shape
    w = d // tp
    wq_c = col_copies(parts, 0, w, wq_b, sems.at[0])
    wo_c = block_copies(parts, w, w, wo_b, sems.at[1])
    kv_c = [pltpu.make_async_copy(kv, kv_b, sems.at[2])]
    begin(wo_c)
    begin(kv_c)
    begin(wq_c)
    vec[...] = jnp.zeros_like(vec)
    emb[...] = jnp.zeros_like(emb)
    ext = kv.shape[0]

    @pl.loop(0, ext // PB)
    def _(i):
        dacc[rows_at(i, PB), :] = jnp.zeros((PB, dacc.shape[1]), F32)

    finish(wo_c)
    gco[...] = nt(b1[...], wo_b[...]).astype(BF)
    finish(kv_c)

    @pl.loop(0, rows // PB)
    def _(g):
        s = rows_at(g, PB)
        at = [rows_at(idx[g * NB + n], PB) for n in range(NB)]
        row = lax.broadcasted_iota(jnp.int32, (PB, PB), 0)
        live = jnp.concatenate([(row < lens[g * NB + n]).astype(jnp.int32) for n in range(NB)], axis=0) > 0
        for p in range(tp):
            for h in range(w // HD):
                c = p * w + h * HD
                k0 = p * 2 * w + h * HD
                v0 = k0 + w
                k = jnp.concatenate([kv_b[a, k0 : k0 + HD] for a in at], axis=0)
                v = jnp.concatenate([kv_b[a, v0 : v0 + HD] for a in at], axis=0)
                qh = q[s, c : c + HD]
                do = gco[s, c : c + HD]
                pr = softmax_parts(jnp.where(live, nt(k, qh), NEG), 0)
                dp = nt(v, do)
                ds = (pr * (dp - jnp.sum(dp * pr, axis=0, keepdims=True))).astype(BF)
                dq[s, c : c + HD] = (tn(ds, k) * SCALE).astype(BF)
                dk = nn(ds, qh)
                dv = nn(pr.astype(BF), do)
                for j, a in enumerate(at):
                    dacc[a, k0 : k0 + HD] += dk[j * PB : (j + 1) * PB, :]
                    dacc[a, v0 : v0 + HD] += dv[j * PB : (j + 1) * PB, :]

    @pl.loop(0, ext // PB)
    def _(i):
        s = rows_at(i, PB)
        for p in range(tp):
            k0 = p * 2 * w
            dkv[s, k0 : k0 + w] = (dacc[s, k0 : k0 + w] * SCALE).astype(BF)
            dkv[s, k0 + w : k0 + 2 * w] = dacc[s, k0 + w : k0 + 2 * w].astype(BF)

    finish(wq_c)
    gnc[...] = nt(dq[...], wq_b[...])

    @pl.loop(0, rows // PB)
    def _(i):
        s = rows_at(i, PB)
        u = gnc[s, :]
        xhat, r = normalise(x0[s, :])
        y = g1[s, :] + norm_back(u, xhat, r, gain_c[...])
        g0[s, :] = y.astype(BF)
        emb[...] += y
        vec[0:1, :] += colsum(u * xhat)


def cross_backward(idx, lens, b1, g1, x0, gain_c, q, kv, pack, after):
    tp = len(pack)
    rows, d = b1.shape
    ext = kv.shape[0]
    return pl.pallas_call(
        functools.partial(cross_backward_body, tp),
        out_shape=(
            shape((rows, d), BF),
            shape((ext, 2 * d), BF),
            shape((rows, d), BF),
            shape((PB, d), F32),
            shape((8, d), F32),
        ),
        in_specs=[SM] * 2 + [VM] * 5 + [ANY] * (1 + len(pack) + len(after)),
        out_specs=[VM] * 5,
        scratch_shapes=[
            pltpu.VMEM((d, d), BF),
            pltpu.VMEM((d, d), BF),
            pltpu.VMEM((rows, d), BF),
            pltpu.VMEM((rows, d), F32),
            pltpu.VMEM((ext, 2 * d), F32),
            pltpu.VMEM((ext, 2 * d), BF),
            pltpu.SemaphoreType.DMA((3,)),
        ],
        compiler_params=params(58),
        cost_estimate=cost(35),
        name="cross_backward",
    )(idx, lens, b1, g1, x0, gain_c, q, kv, *pack, *after)


def tn_into(out, lo, left, right, extra):
    n = left.shape[1]
    tile = min(256, n)
    for k in range(n // tile):
        r = slice(lo + k * tile, lo + (k + 1) * tile)
        y = tn(left[:, k * tile : (k + 1) * tile], right[...])
        if extra is not None:
            y = y + extra[r, :].astype(F32)
        out[r, :] = y.astype(BF)


def two(ref):
    n = ref.shape[0] // 2
    return ref.at[pl.ds(0, n), :], ref.at[pl.ds(n, n), :]


def self_weights_body(ns, dqkv, o, b2, *refs):
    ea, eb = two(refs[0]) if len(refs) > 1 else (None, None)
    a, b = two(refs[-1])
    w = o.shape[1]
    tn_into(a, 0, dqkv.at[:, pl.ds(0, w)], ns, ea)
    tn_into(b, 0, dqkv.at[:, pl.ds(w, 2 * w)], ns, eb)
    tn_into(a, w, o, b2, ea)


def column_block(x, p, n):
    return pl.BlockSpec((x.shape[0], n), lambda i: (0, p))


def whole_block(x):
    return pl.BlockSpec(x.shape, lambda i: (0, 0))


def self_weights(p, w, ns, dqkv, o, b2, came, late):
    d = ns.shape[1]
    return pl.pallas_call(
        lambda *refs: self_weights_body(*refs[: 4 + len(came)], refs[-1]),
        grid=(1,),
        out_shape=shape((4 * w, d), BF),
        in_specs=[whole_block(ns), column_block(dqkv, p, 3 * w), column_block(o, p, w), whole_block(b2)]
        + [whole_block(x) for x in came]
        + [ANY] * len(late),
        out_specs=pl.BlockSpec((4 * w, d), lambda i: (0, 0)),
        compiler_params=params(58),
        cost_estimate=cost(4),
        name="self_weights",
    )(ns, dqkv, o, b2, *came, *late)


def cross_weights_body(nc, dq, o, b1, dkv, points, came0, came1, *refs):
    ext_b, sem = refs[-2:]
    came, outs = (refs[:1], refs[1:-2]) if len(refs) == 5 else ((), refs[:-2])
    ea, eb = two(came[0]) if came else (None, None)
    a, b = outs if len(outs) == 2 else two(outs[0])
    half = ext_b.shape[0] // 2
    copies = row_copies([came0, came1], ext_b, sem) + [
        pltpu.make_async_copy(points.at[pl.ds(0, half), :], ext_b.at[pl.ds(half, half), :], sem)
    ]
    begin(copies)
    w = o.shape[1]
    tn_into(a, 0, dq, nc, ea)
    tn_into(a, w, o, b1, ea)
    finish(copies)
    tn_into(b, 0, dkv, ext_b, eb)


def cross_weights(p, w, nc, dq, o, b1, dkv, points, came_points, came, late):
    d = nc.shape[1]
    rows = [4 * w] if p % 2 else [2 * w] * 2
    n, k = 8 + len(came), 2 + len(rows)
    return pl.pallas_call(
        lambda *refs: cross_weights_body(*refs[:n], *refs[-k:]),
        grid=(1,),
        out_shape=[shape((r, d), BF) for r in rows],
        in_specs=[
            whole_block(nc),
            column_block(dq, p, w),
            column_block(o, p, w),
            whole_block(b1),
            column_block(dkv, p, 2 * w),
        ]
        + [ANY] * 3
        + [whole_block(x) for x in came]
        + [ANY] * len(late),
        out_specs=[pl.BlockSpec((r, d), lambda i: (0, 0)) for r in rows],
        scratch_shapes=[pltpu.VMEM((dkv.shape[0], d), BF), pltpu.SemaphoreType.DMA],
        compiler_params=params(58),
        cost_estimate=cost(8),
        name="cross_weights",
    )(nc, dq, o, b1, dkv, points, *came_points, *came, *late)


def flip(x, axis, bit):
    n = lax.axis_size(axis)
    return lax.ppermute(x, axis, [(i, i ^ (1 << bit)) for i in range(n)])


def bits_of(axis):
    return (lax.axis_size(axis) - 1).bit_length()


def bit_at(axis, bit):
    return (lax.axis_index(axis) >> bit) & 1


def gather_pieces(own, *late):
    have = {0: own}
    for bit in reversed(range(bits_of("tp"))):
        for p in list(have):
            x = have[p] if bit > 0 or p == 0 or not late else after(have[p], *late)
            have[p | (1 << bit)] = flip(x, "tp", bit)
    return [have[p] for p in range(len(have))]


def in_order(pieces):
    x = jnp.stack(pieces)
    for bit in range(bits_of("tp")):
        y = x.reshape((-1, 2, 1 << bit) + x.shape[1:])
        x = jnp.where(bit_at("tp", bit) == 1, y[:, ::-1], y).reshape(x.shape)
    return x


def add(*xs, late=()):
    return after(functools.reduce(jnp.add, [x.astype(F32) for x in xs]).astype(BF), *late)


def after(x, *deps):
    ok = True
    for v in deps:
        first = v[(0,) * v.ndim]
        ok = jnp.logical_and(ok, first == first)
    return jnp.where(ok, x, jnp.zeros_like(x))


def over_tp(have, bit, late=()):
    out = {p: v for p, v in have.items() if not p >> bit & 1}
    for p, v in have.items():
        if p >> bit & 1:
            q = p ^ (1 << bit)
            out[q] = add(out[q], flip(v, "tp", bit), late=late)
    return out


def over_y(have, late=()):
    for k in reversed(range(1, bits_of("tp"))):
        have = over_tp(have, k, late)
    return have


def flip_x(v):
    return lax.ppermute(v, "x", [(0, 1), (1, 0)])


def shares(v):
    nz = lax.axis_size("z")
    v = v.reshape((nz, 2, v.shape[0] // (2 * nz)) + v.shape[1:])
    x = lax.axis_index("x")
    keep = lax.dynamic_index_in_dim(v, x, 1, keepdims=False)
    return keep, lax.dynamic_index_in_dim(v, 1 - x, 1, keepdims=False)


def over_x(v, late=()):
    keep, send = shares(v)
    return add(keep, flip_x(send), late=late)


def sum_z(v):
    return lax.psum(v, "z")


def to_groups(x, per):
    lat, groups, w = x.shape
    n = groups // per
    tp = lax.axis_size("tp")
    y = jnp.transpose(x.reshape(lat, n, per, w), (1, 2, 0, 3))
    y = lax.all_to_all(y, ("z", "x", "tp"), split_axis=0, concat_axis=0, tiled=True)
    y = jnp.transpose(y.reshape(n // tp, tp, per, lat, w), (2, 0, 3, 1, 4))
    return y.reshape(per * lat * (n // tp), tp * w)


def from_groups(x, per):
    tp = lax.axis_size("tp")
    n = lax.axis_size(GRP) * tp
    rows, d = x.shape
    lat, w = rows // per // (n // tp), d // tp
    y = jnp.transpose(x.reshape(per, n // tp, lat, tp, w), (1, 3, 0, 2, 4)).reshape(n, per, lat, w)
    y = lax.all_to_all(y, ("z", "x", "tp"), split_axis=0, concat_axis=0, tiled=True)
    return jnp.transpose(y, (2, 0, 1, 3)).reshape(lat, n * per, w)


def per_device(
    latents,
    skip_latents,
    points,
    neighbours,
    block_lengths,
    latent_embed,
    gain_cross,
    query_cross,
    key_cross,
    value_cross,
    output_cross,
    bias_cross,
    gain_self,
    query_self,
    key_self,
    value_self,
    output_self,
    bias_self,
    gain_mlp,
    hidden_weight,
    hidden_bias,
    output_weight,
    output_bias,
    cotangent,
):
    tp, grp = lax.axis_size("tp"), lax.axis_size(GRP)
    t, i = lax.axis_index("tp"), lax.axis_index(GRP)
    d = query_cross.shape[0]
    w = latent_embed.shape[1]
    lat_rows = latent_embed.shape[0]
    ff = hidden_weight.shape[1]
    groups_here = neighbours.shape[0]
    groups = groups_here * grp
    per = groups_here // tp
    blocks_here = points.shape[0] // PB
    all_blocks = blocks_here * grp
    half_rows = points.shape[0] // 2

    kv_own = packed([[key_cross, value_cross]])[0]
    share = half_rows // 2
    core = bit_at("tp", 0)
    sent = part_of(points, (2 + core).astype(jnp.int32).reshape(1), share)
    first = lax.ppermute(sent, GRP, [(k, (k + 1) % grp) for k in range(grp)])
    came_points = [first, flip(first, "tp", 0)]
    near = lax.dynamic_slice_in_dim(neighbours, t * per, per, 0).reshape(per * NB)
    block = (near - (i * blocks_here - blocks_here // 2)) % all_blocks
    share_blocks = share // PB
    moved = ((block // share_blocks) ^ core) * share_blocks + block % share_blocks
    idx = jnp.where(block < blocks_here // 2, moved, block).astype(jnp.int32)
    lens = block_lengths[near]

    kv_pack = gather_pieces(kv_own)
    qo_own = packed([[query_cross, output_cross]], [kv_own])[0]

    small = jnp.concatenate(
        [
            after(latent_embed, kv_own),
            bias_cross[None],
            bias_self[None],
            output_bias[None],
            hidden_bias.reshape(ff // w, w),
        ]
    )
    small_pieces = gather_pieces(small)
    small_all = in_order(small_pieces)
    by_rows = jnp.transpose(small_all, (1, 0, 2)).reshape(small.shape[0], d)
    embed = by_rows[:lat_rows]
    bias_c, bias_s, bias_o = (by_rows[lat_rows + k : lat_rows + k + 1] for k in range(3))
    hid_bias = jnp.stack([piece[lat_rows + 3 :].reshape(ff) for piece in small_pieces[:2]])

    whid = [hidden_weight, flip(hidden_weight, "tp", 0)]
    wout = [output_weight, flip(output_weight, "tp", 0)]

    gain_c, gain_s, gain_m = gain_cross[None], gain_self[None], gain_mlp[None]
    rows = per * lat_rows
    self_own = packed([[query_self, key_self, value_self, output_self]], [qo_own])[0]
    kv = keys_values(points, came_points, kv_pack, [self_own])
    x0 = (
        to_groups(after(latents, kv_own, sent), per).astype(F32).reshape(per, lat_rows, d) + embed[None]
    ).reshape(rows, d)
    x0 = after(x0, kv)
    qo_pack = gather_pieces(qo_own, kv)
    q, oc, x1, nc, ns = cross_forward(idx, lens, x0, gain_c, gain_s, bias_c, kv, qo_pack)
    self_pack = gather_pieces(self_own, x1)
    cot = after(to_groups(after(cotangent, x0), per), x1)
    qkv, os, x2, nm = self_forward(ns, x1, gain_m, bias_s, self_pack, [cot])

    steps = list(range(2, tp, 2))

    def swap(x, k):
        return lax.ppermute(x, "tp", [(j, j ^ k) for j in range(tp)])

    other_cot = [swap(cot, k) for k in steps]
    other_nm = [swap(nm, k) for k in steps]
    acts, gbs, hbgs = [], [], []
    act, gb, out, gnm, hbg = feed(nm, cot, hid_bias, whid, wout, F32, other_cot)
    acts.append(act)
    gbs.append(gb)
    hbgs.append(hbg)
    back_out, back_gnm = [], []
    for k, n_k, c_k in zip(steps, other_nm, other_cot):
        act, gb, o_k, g_k, hbg = feed(n_k, c_k, hid_bias, whid, wout, BF)
        acts.append(act)
        gbs.append(gb)
        hbgs.append(hbg)
        back_gnm.append(swap(g_k, k))
        back_out.append(o_k)
    nms, cots = [nm] + other_nm, [cot] + other_cot
    sent_o = feed_weights(1, acts, cots, [])
    sent_h = feed_weights(1, gbs, nms, [])
    own_o = feed_weights(0, acts, cots, [flip(sent_o, "tp", 0)])
    own_h = feed_weights(0, gbs, nms, [flip(sent_h, "tp", 0)])

    b2, dqkv, g1, b1, vec_s = self_backward(
        cot, gnm, back_gnm, x2, x1, gain_m, gain_s, qkv, self_pack, [own_o, own_h]
    )

    def pieces(weights, waits):
        got, out, late = {}, {}, []
        for p in reversed(range(1, tp, 2)):
            x = weights(p, [], waits(p, late) + late)
            late = [x]
            got[p - 1] = flip(x, "tp", 0)
        for p in reversed(range(0, tp, 2)):
            out[p] = weights(p, [got[p]], waits(p, late) + late)
            late = [out[p][0] if isinstance(out[p], (list, tuple)) else out[p]]
        return out

    x3 = x2 + out + bias_o
    for k, o_k in zip(steps, back_out):
        x3 = x3 + swap(after(o_k, own_h), k).astype(F32)
    leaving = after(x3.astype(BF), b2)
    sum_o, sum_h = over_x(own_o, [b2]), over_x(own_h, [b2])
    sum_f = jnp.concatenate([sum_o, sum_h], axis=1)
    selfs = pieces(
        lambda p, came, late: self_weights(p, w, ns, dqkv, os, b2, came, late),
        lambda p, late: [sum_f, leaving] if p == tp - 1 else [],
    )
    last = selfs[0]
    feed_z = sum_z(sum_f)
    restored = from_groups(after(leaving, selfs[tp - 2]), per)

    dq, dkv, g0, emb, vec_c = cross_backward(
        idx, lens, b1, g1, x0, gain_c, q, kv, qo_pack, [leaving, *selfs.values()]
    )
    stage = {}

    def norms_and_small(late):
        block_out = after(restored, *late).astype(F32) + skip_latents.astype(F32)
        squares = jnp.sum(jnp.square(block_out), axis=(0, 2))
        by_share = jnp.transpose(
            jnp.concatenate([emb, vec_s[:5], vec_c[:1]]).reshape(lat_rows + 6, tp, w), (1, 0, 2)
        )
        hb_all = functools.reduce(jnp.add, hbgs).reshape(2, ff // w, w)
        owner = lax.broadcasted_iota(jnp.int32, (tp, 1, 1), 0)
        hb_share = jnp.where(owner == t, hb_all[0][None], 0.0) + jnp.where(
            owner == (t ^ 1), hb_all[1][None], 0.0
        )
        sq_rows = jnp.pad(squares, (0, norm_rows * w - groups)).reshape(1, norm_rows, w)
        x = jnp.concatenate(
            [by_share, hb_share, jnp.broadcast_to(sq_rows, (tp, norm_rows, w))], axis=1
        )
        x = jnp.pad(x, ((0, 0), (0, -x.shape[1] % 8), (0, 0)))
        for bit in reversed(range(bits_of("tp"))):
            n = x.shape[0] // 2
            mine = bit_at("tp", bit)
            keep = lax.dynamic_slice_in_dim(x, mine * n, n, 0)
            x = keep + flip(lax.dynamic_slice_in_dim(x, (1 - mine) * n, n, 0), "tp", bit)
        x = x[0].reshape(-1)
        places_rows = 2 * lax.axis_size("z") * 8
        rows_all = -(-x.shape[0] // (d * places_rows)) * places_rows
        return block_out, jnp.pad(x, (0, rows_all * d - x.shape[0])).reshape(rows_all, d).astype(BF)

    norm_rows = -(-groups // w)

    def waits(p, late):
        if p == tp - 1:
            stage["self"] = over_y(selfs, [emb])[0]
            stage["returned"] = from_groups(after(g0, *late), per)
            return [stage["self"], restored]
        if p == tp - 3:
            return []
        if p == tp - 2:
            n = stage["self"].shape[0] // 2
            stage["self"] = [over_x(stage["self"][:n], late), over_x(stage["self"][n:], late)]
            stage["returned"] = from_groups(after(g0, *late), per)
            return stage["self"] + [feed_z]
        if p == 0:
            stage["self"] = after(jnp.concatenate(stage["self"], axis=1), *late)
            stage["out"], stage["small"] = norms_and_small(late)
            return [stage["small"], stage["returned"]]
        return []

    def cross_piece(p, came, late):
        x = cross_weights(p, w, nc, dq, oc, b1, dkv, points, came_points, came, late)
        return x[0] if p % 2 else x

    cross = pieces(cross_piece, waits)
    late = [cross[0][0]]
    self_z = sum_z(stage["self"])
    cross_a = over_y({p: v[0] for p, v in cross.items()})[0]
    cross_b = over_y({p: over_x(v[1], [feed_z]) for p, v in cross.items()})[0]
    little = over_x(stage["small"])
    keep, send = shares(cross_a)
    half = feed_z.shape[1] // 2
    feed_ox = flip_x(after(feed_z[:, :half], send))
    cross_z = jnp.concatenate([add(keep, flip_x(send)), cross_b, little], axis=1)
    cross_z = after(cross_z, self_z, feed_ox)
    feed_hx = flip_x(after(feed_z[:, half:], cross_z))
    self_x = flip_x(after(self_z, cross_z))
    cross_z = after(sum_z(cross_z), self_x)
    returned = stage["returned"]
    cross_x = flip_x(cross_z)
    n = little.shape[1]
    low = lax.axis_index("x") == 0
    own_n, other_n = cross_z[:, -n:], cross_x[:, -n:]
    total = jnp.where(low, jnp.stack([own_n, other_n], 1), jnp.stack([other_n, own_n], 1))
    total = total.astype(F32).reshape(-1)
    total = total[: total.shape[0] // w * w].reshape(-1, w)
    places = lax.axis_index("x").astype(jnp.int32).reshape(1)
    output_weight_grad, hidden_weight_grad = final_feed(places, feed_z, feed_ox, feed_hx)
    query_self_grad, key_self_grad, value_self_grad, output_self_grad = final(
        places, w, self_z, self_x
    )
    block_out = stage["out"]
    latents_grad = returned.astype(F32)

    query_cross_grad, key_cross_grad, value_cross_grad, output_cross_grad = final(
        places, w, cross_z, cross_x, [output_weight_grad, hidden_weight_grad, output_self_grad]
    )
    embed_grad = total[:lat_rows]
    (
        output_bias_grad,
        gain_mlp_grad,
        bias_self_grad,
        gain_self_grad,
        bias_cross_grad,
        gain_cross_grad,
    ) = (total[lat_rows + k] for k in range(6))
    at = lat_rows + 6
    hidden_bias_grad = total[at : at + ff // w].reshape(ff)
    at += ff // w
    square_sums = total[at : at + norm_rows].reshape(norm_rows * w)[:groups]
    group_norms = jnp.sqrt(square_sums / (lat_rows * d))

    return (
        block_out,
        group_norms,
        latents_grad,
        embed_grad,
        gain_cross_grad,
        query_cross_grad,
        key_cross_grad,
        value_cross_grad,
        output_cross_grad,
        bias_cross_grad,
        gain_self_grad,
        query_self_grad,
        key_self_grad,
        value_self_grad,
        output_self_grad,
        bias_self_grad,
        gain_mlp_grad,
        hidden_weight_grad,
        hidden_bias_grad,
        output_weight_grad,
        output_bias_grad,
    )


def solution(mesh):
    grp, tp = mesh.shape["grp"], mesh.shape["tp"]
    own = jax.sharding.Mesh(mesh.devices.reshape(grp // 2, 2, tp), GRP + ("tp",))
    lay = P(GRP, None, "tp")
    cols, rows, part = P(None, "tp"), P("tp", None), P("tp")
    attn = (P(), cols, cols, cols, rows, part)
    return jax.shard_map(
        per_device,
        mesh=own,
        in_specs=(lay, lay, P(GRP, None), P(GRP, None), P(), cols)
        + attn
        + attn
        + (P(), cols, part, rows, part, lay),
        out_specs=(lay, P(), lay, cols)
        + (part, cols, cols, cols, rows, part)
        + (part, cols, cols, cols, rows, part)
        + (part, cols, part, rows, part),
        check_vma=False,
    )
```

```python
import functools

import jax
import jax.numpy as jnp
from jax import lax
from jax.experimental import pallas as pl
from jax.experimental.pallas import tpu as pltpu
from jax.sharding import PartitionSpec as P

HD = 128
PB = 128
NB = 4
EPS = 1e-05
NEG = -1e30
SCALE = HD ** (-0.5)
BF = jnp.bfloat16
F32 = jnp.float32
GRP = ("z", "x")

ANY = pl.BlockSpec(memory_space=pl.ANY)
VM = pl.BlockSpec(memory_space=pltpu.VMEM)
SM = pl.BlockSpec(memory_space=pltpu.SMEM)


def shape(dims, kind):
    return jax.ShapeDtypeStruct(dims, kind)


def params(mib):
    return pltpu.CompilerParams(vmem_limit_bytes=mib * 2**20)


def cost(us):
    return pl.CostEstimate(flops=int(us * 1.1e9), bytes_accessed=int(us * 1e6), transcendentals=0)


def nn(left, right):
    return lax.dot_general(left, right, (((1,), (0,)), ((), ())), preferred_element_type=F32)


def nt(left, right):
    return lax.dot_general(left, right, (((1,), (1,)), ((), ())), preferred_element_type=F32)


def tn(left, right):
    return lax.dot_general(left, right, (((0,), (0,)), ((), ())), preferred_element_type=F32)


def rows_at(i, n):
    return pl.ds(pl.multiple_of(i * n, n), n)


def normalise(x):
    d = x - jnp.mean(x, axis=1, keepdims=True)
    r = lax.rsqrt(jnp.mean(d * d, axis=1, keepdims=True) + EPS)
    return d * r, r


def norm_back(u, xhat, r, gain):
    w = u * gain
    a = jnp.mean(w, axis=1, keepdims=True)
    b = jnp.mean(w * xhat, axis=1, keepdims=True)
    return r * (w - a - xhat * b)


def colsum(x):
    return jnp.sum(x, axis=0, keepdims=True)


def begin(copies):
    for c in copies:
        c.start()


def finish(copies):
    for c in copies:
        c.wait()


def row_copies(pieces, buf, sem):
    n = pieces[0].shape[0]
    return [pltpu.make_async_copy(s, buf.at[pl.ds(p * n, n), :], sem) for p, s in enumerate(pieces)]


def pack_parts(refs, tp, place):
    if len(refs) == tp:
        return [(p, None, r) for p, r in enumerate(refs)]
    parts = [(0, None, refs[0]), (1, None, refs[1])]
    for p in range(2, tp):
        parts.append((p, place[0], refs[2 * p - 2]))
        parts.append((p, 1 - place[0], refs[2 * p - 1]))
    return parts


def col_copies(parts, at, n, buf, sem):
    out = []
    for p, h, r in parts:
        to = pl.ds(p * n, n)
        k = r.shape[0]
        dst = buf.at[:, to] if h is None else buf.at[rows_at(h, k), to]
        out.append(pltpu.make_async_copy(r.at[:, pl.ds(at, n)], dst, sem))
    return out


def block_copies(parts, at, w, buf, sem):
    out = []
    for p, h, r in parts:
        count = r.shape[0] // w
        for k in range(count):
            col = k * w if h is None else pl.multiple_of((h * count + k) * w, 128)
            src = r.at[pl.ds(k * w, w), pl.ds(at, w)]
            out.append(pltpu.make_async_copy(src, buf.at[pl.ds(p * w, w), pl.ds(col, w)], sem))
    return out


def softmax_parts(s, axis):
    e = jnp.exp((s - jnp.max(s, axis=axis, keepdims=True)) * SCALE)
    return e * (1.0 / jnp.sum(e, axis=axis, keepdims=True))


def head_sets(tp, w, size):
    heads = [(p, h * HD) for p in range(tp) for h in range(w // HD)]
    return [heads[i : i + size] for i in range(0, len(heads), size)]


def pack_body(counts, *refs):
    outs, at = refs[-len(counts) :], 0
    for n, out in zip(counts, outs):
        col, rows = 0, out.shape[0]
        for r in refs[at : at + n]:
            if r.shape[0] == rows:
                out[:, col : col + r.shape[1]] = r[...]
                col += r.shape[1]
            else:
                w = r.shape[0]
                for k in range(rows // w):
                    out[k * w : (k + 1) * w, col : col + w] = r[:, k * w : (k + 1) * w]
                col += w
        at += n


def packed(groups, late=()):
    counts = [len(g) for g in groups]
    ins = [x for g in groups for x in g]
    rows = groups[0][0].shape[0]
    outs = []
    for g in groups:
        cols = sum(x.shape[1] if x.shape[0] == rows else x.shape[0] for x in g)
        outs.append(shape((rows, cols), g[0].dtype))
    n = len(ins)
    return pl.pallas_call(
        lambda *refs: pack_body(counts, *refs[:n], *refs[n + len(late) :]),
        out_shape=outs,
        in_specs=[VM] * n + [ANY] * len(late),
        out_specs=[VM] * len(outs),
        compiler_params=params(12),
        cost_estimate=cost(2),
        name="packed",
    )(*ins, *late)


def part_body(n, at, x, *refs):
    out, sem = refs[-2:]
    copy = pltpu.make_async_copy(x.at[pl.ds(pl.multiple_of(at[0] * n, n), n), :], out, sem)
    copy.start()
    copy.wait()


def part_of(x, at, n, late=()):
    return pl.pallas_call(
        functools.partial(part_body, n),
        out_shape=shape((n, x.shape[1]), x.dtype),
        in_specs=[SM] + [ANY] * (1 + len(late)),
        out_specs=VM,
        scratch_shapes=[pltpu.SemaphoreType.DMA],
        cost_estimate=cost(1),
        name="part_of",
    )(at, x, *late)


def share_copies(places, parts, bufs, sem):
    out = []
    for r, x in zip(parts, (places[0], 1 - places[0])):
        c = bufs[0].shape[0] // (2 * r.shape[0])
        for z in range(r.shape[0]):
            for j, buf in enumerate(bufs):
                src = r.at[z, pl.ds(j * c, c), :]
                out.append(pltpu.make_async_copy(src, buf.at[rows_at(2 * z + x, c), :], sem))
    return out


def final_body(places, own, other, *refs):
    q, k, v, o, qo_b, kv_b, sem = refs[-7:]
    copies = share_copies(places, (own, other), (qo_b, kv_b), sem)
    begin(copies)
    finish(copies)
    w = o.shape[0]
    q[...] = qo_b[0:w, :].astype(F32).T
    o[...] = qo_b[w : 2 * w, :].astype(F32)
    k[...] = kv_b[0:w, :].astype(F32).T
    v[...] = kv_b[w : 2 * w, :].astype(F32).T


def final(places, w, own, other, late=()):
    d = own.shape[2]
    tall, flat = shape((d, w), F32), shape((w, d), F32)
    return pl.pallas_call(
        final_body,
        out_shape=(tall, tall, tall, flat),
        in_specs=[SM] + [ANY] * (2 + len(late)),
        out_specs=[VM] * 4,
        scratch_shapes=[pltpu.VMEM((2 * w, d), BF)] * 2 + [pltpu.SemaphoreType.DMA],
        compiler_params=params(58),
        cost_estimate=cost(5),
        name="final",
    )(places, own, other, *late)


def final_feed_body(places, own, other_o, other_h, out, hid, out_b, hid_b, sem):
    c = other_o.shape[1]
    copies = []
    for z in range(own.shape[0]):
        here, there = rows_at(2 * z + places[0], c), rows_at(2 * z + 1 - places[0], c)
        for k, (other, buf) in enumerate(((other_o, out_b), (other_h, hid_b))):
            src = own.at[z, pl.ds(k * c, c), :]
            copies.append(pltpu.make_async_copy(src, buf.at[here, :], sem))
            copies.append(pltpu.make_async_copy(other.at[z], buf.at[there, :], sem))
    begin(copies)
    finish(copies)
    out[...] = out_b[...].astype(F32)
    hid[...] = hid_b[...].astype(F32).T


def final_feed(places, own, other_o, other_h):
    nz, c, d = own.shape
    ff = nz * c
    return pl.pallas_call(
        final_feed_body,
        out_shape=(shape((ff, d), F32), shape((d, ff), F32)),
        in_specs=[SM] + [ANY] * 3,
        out_specs=[VM] * 2,
        scratch_shapes=[pltpu.VMEM((ff, d), BF)] * 2 + [pltpu.SemaphoreType.DMA],
        compiler_params=params(58),
        cost_estimate=cost(6),
        name="final_feed",
    )(places, own, other_o, other_h)


def keys_body(tp, points, came0, came1, *refs):
    packs, (kv, kv_b, ext_b, wkv_b, sems) = refs[:tp], refs[-5:]
    ext, d = ext_b.shape
    half = ext // 2
    near_c = [pltpu.make_async_copy(points.at[pl.ds(0, half), :], ext_b.at[pl.ds(half, half), :], sems.at[0])]
    far_c = row_copies([came0, came1], ext_b, sems.at[1])
    w_c = col_copies(pack_parts(packs, tp, None), 0, packs[0].shape[1], wkv_b, sems.at[2])
    for c in (w_c, near_c, far_c):
        begin(c)
    finish(w_c)
    span = 512

    def out_copy(i):
        s = rows_at(i, span)
        return pltpu.make_async_copy(kv_b.at[s, :], kv.at[s, :], sems.at[3])

    def work(i):
        s = rows_at(i, span)
        kv_b[s, :] = nn(ext_b[s, :], wkv_b[...]).astype(BF)
        out_copy(i).start()

    finish(near_c)
    pl.loop(half // span, ext // span)(work)
    finish(far_c)
    pl.loop(0, half // span)(work)

    @pl.loop(0, ext // span)
    def _(i):
        out_copy(i).wait()


def keys_values(points, came, packs, late):
    tp = len(packs)
    ext, d = points.shape
    return pl.pallas_call(
        functools.partial(keys_body, tp),
        out_shape=shape((ext, 2 * d), BF),
        in_specs=[ANY] * (3 + tp + len(late)),
        out_specs=ANY,
        scratch_shapes=[
            pltpu.VMEM((ext, 2 * d), BF),
            pltpu.VMEM((ext, d), BF),
            pltpu.VMEM((d, 2 * d), BF),
            pltpu.SemaphoreType.DMA((4,)),
        ],
        compiler_params=params(58),
        cost_estimate=cost(14),
        name="keys_values",
    )(points, *came, *packs, *late)


def cross_forward_body(tp, idx, lens, x0, gain_c, gain_s, bias, kv, *refs):
    parts = pack_parts(refs[:tp], tp, None)
    (q, o, x1, nc, ns, kv_b, wq_b, wo_b, acc, sems) = refs[-10:]
    rows, d = x0.shape
    w = d // tp
    wq_c = col_copies(parts, 0, w, wq_b, sems.at[0])
    wo_c = block_copies(parts, w, w, wo_b, sems.at[1])
    kv_c = [pltpu.make_async_copy(kv, kv_b, sems.at[2])]
    for c in (wq_c, kv_c, wo_c):
        begin(c)

    @pl.loop(0, rows // PB)
    def _(i):
        s = rows_at(i, PB)
        xhat, _ = normalise(x0[s, :])
        nc[s, :] = (xhat * gain_c[...]).astype(BF)

    finish(wq_c)
    q[...] = nn(nc[...], wq_b[...]).astype(BF)
    finish(kv_c)

    @pl.loop(0, rows // PB)
    def _(g):
        s = rows_at(g, PB)
        at = [rows_at(idx[g * NB + n], PB) for n in range(NB)]
        lane = lax.broadcasted_iota(jnp.int32, (1, PB), 1)
        live = jnp.concatenate([(lane < lens[g * NB + n]).astype(jnp.int32) for n in range(NB)], axis=1) > 0
        for heads in head_sets(tp, w, 8):
            def part(lo):
                return [
                    jnp.concatenate([kv_b[a, p * 2 * w + lo + h : p * 2 * w + lo + h + HD] for a in at], axis=0)
                    for p, h in heads
                ]

            qs = [q[s, p * w + h : p * w + h + HD] for p, h in heads]
            ks, vs = part(0), part(w)
            ss = [jnp.where(live, nt(x, k), NEG) for x, k in zip(qs, ks)]
            ps = [softmax_parts(x, 1).astype(BF) for x in ss]
            outs = [nn(x, v).astype(BF) for x, v in zip(ps, vs)]
            for (p, h), x in zip(heads, outs):
                o[s, p * w + h : p * w + h + HD] = x

    finish(wo_c)
    acc[...] = nn(o[...], wo_b[...])

    @pl.loop(0, rows // PB)
    def _(i):
        s = rows_at(i, PB)
        y = x0[s, :] + acc[s, :] + bias[...]
        x1[s, :] = y
        xhat, _ = normalise(y)
        ns[s, :] = (xhat * gain_s[...]).astype(BF)


def cross_forward(idx, lens, x0, gain_c, gain_s, bias, kv, packs):
    tp = len(packs)
    rows, d = x0.shape
    ext = kv.shape[0]
    return pl.pallas_call(
        functools.partial(cross_forward_body, tp),
        out_shape=(
            shape((rows, d), BF),
            shape((rows, d), BF),
            shape((rows, d), F32),
            shape((rows, d), BF),
            shape((rows, d), BF),
        ),
        in_specs=[SM] * 2 + [VM] * 4 + [ANY] * (1 + tp),
        out_specs=[VM] * 5,
        scratch_shapes=[
            pltpu.VMEM((ext, 2 * d), BF),
            pltpu.VMEM((d, d), BF),
            pltpu.VMEM((d, d), BF),
            pltpu.VMEM((rows, d), F32),
            pltpu.SemaphoreType.DMA((3,)),
        ],
        compiler_params=params(58),
        cost_estimate=cost(20),
        name="cross_forward",
    )(idx, lens, x0, gain_c, gain_s, bias, kv, *packs)


def self_forward_body(tp, ns, x1, gain_m, bias, *refs):
    n = tp
    parts = pack_parts(refs[:n], tp, None)
    qkv, o, x2, nm, wqkv_b, wo_b, acc, sems = refs[-8:]
    rows, d = x1.shape
    w = d // tp
    wqkv_c = col_copies(parts, 0, 3 * w, wqkv_b, sems.at[0])
    wo_c = block_copies(parts, 3 * w, w, wo_b, sems.at[1])
    begin(wqkv_c)
    begin(wo_c)
    finish(wqkv_c)
    qkv[...] = nn(ns[...], wqkv_b[...]).astype(BF)

    @pl.loop(0, rows // PB)
    def _(g):
        s = rows_at(g, PB)
        for heads in head_sets(tp, w, 8):
            qs, ks, vs = (
                [qkv[s, p * 3 * w + lo + h : p * 3 * w + lo + h + HD] for p, h in heads]
                for lo in (0, w, 2 * w)
            )
            ss = [nt(x, k) for x, k in zip(qs, ks)]
            ps = [softmax_parts(x, 1).astype(BF) for x in ss]
            outs = [nn(x, v).astype(BF) for x, v in zip(ps, vs)]
            for (p, h), x in zip(heads, outs):
                o[s, p * w + h : p * w + h + HD] = x

    finish(wo_c)
    acc[...] = nn(o[...], wo_b[...])

    @pl.loop(0, rows // PB)
    def _(i):
        s = rows_at(i, PB)
        y = x1[s, :] + acc[s, :] + bias[...]
        x2[s, :] = y
        xhat, _ = normalise(y)
        nm[s, :] = (xhat * gain_m[...]).astype(BF)


def self_forward(ns, x1, gain_m, bias, pack, late):
    rows, d = x1.shape
    tp = len(pack)
    return pl.pallas_call(
        functools.partial(self_forward_body, tp),
        out_shape=(
            shape((rows, 3 * d), BF),
            shape((rows, d), BF),
            shape((rows, d), F32),
            shape((rows, d), BF),
        ),
        in_specs=[VM] * 4 + [ANY] * (len(pack) + len(late)),
        out_specs=[VM] * 4,
        scratch_shapes=[
            pltpu.VMEM((d, 3 * d), BF),
            pltpu.VMEM((d, d), BF),
            pltpu.VMEM((rows, d), F32),
            pltpu.SemaphoreType.DMA((2,)),
        ],
        compiler_params=params(32),
        cost_estimate=cost(22),
        name="self_forward",
    )(ns, x1, gain_m, bias, *pack, *late)


ROOT = 0.7978845608028654
CUBE = 0.044715


def feed_body(nm, cot, hb, wh0, wh1, wo0, wo1, *refs):
    act, gb, out, gnm, hbg = refs[-5:]
    rows, d = nm.shape
    ff = wh0.shape[1]
    span = min(512, ff)
    for p, (wh, wo) in enumerate(((wh0, wo0), (wh1, wo1))):
        for j in range(ff // span):
            s = slice(j * span, (j + 1) * span)
            x = nn(nm[...], wh[:, s]) + hb[p : p + 1, s]
            ga = nt(cot[...], wo[s, :])
            sq = x * x
            t = jnp.tanh(ROOT * x * (1.0 + CUBE * sq))
            half = 0.5 * (1.0 + t)
            act[p, :, s] = (x * half).astype(BF)
            slope = half + 0.5 * x * (1.0 - t * t) * (ROOT + (3.0 * ROOT * CUBE) * sq)
            g = (ga * slope).astype(BF)
            gb[p, :, s] = g
            hbg[p : p + 1, s] = colsum(g.astype(F32))
    gnm[...] = (nt(gb[0], wh0[...]) + nt(gb[1], wh1[...])).astype(gnm.dtype)
    out[...] = (nn(act[0], wo0[...]) + nn(act[1], wo1[...])).astype(out.dtype)


def feed(nm, cot, hb, wh, wo, kind, late=()):
    rows, d = nm.shape
    ff = wh[0].shape[1]
    return pl.pallas_call(
        feed_body,
        out_shape=(
            shape((2, rows, ff), BF),
            shape((2, rows, ff), BF),
            shape((rows, d), kind),
            shape((rows, d), kind),
            shape((2, ff), F32),
        ),
        in_specs=[VM] * 7 + [ANY] * len(late),
        out_specs=[VM] * 5,
        compiler_params=params(32),
        cost_estimate=cost(15),
        name="feed",
    )(nm, cot, hb, *wh, *wo, *late)


def feed_weights_body(sets, *refs):
    lefts, rights, rest = refs[:sets], refs[sets : 2 * sets], refs[2 * sets :]
    out = rest[-1]
    came = rest[0] if len(rest) == 2 else None
    tile = 256

    @pl.loop(0, out.shape[0] // tile)
    def _(i):
        s = rows_at(i, tile)
        y = functools.reduce(jnp.add, [tn(a[0, :, s], c[...]) for a, c in zip(lefts, rights)])
        if came is not None:
            y = y + came[s, :].astype(F32)
        out[s, :] = y.astype(BF)


def feed_weights(p, lefts, rights, came):
    sets = len(lefts)

    def spec(x):
        if x.ndim == 3:
            return pl.BlockSpec((1,) + x.shape[1:], lambda i: (p, 0, 0))
        return pl.BlockSpec(x.shape, lambda i: (0, 0))

    dims = (lefts[0].shape[-1], rights[0].shape[-1])
    ins = list(lefts) + list(rights) + list(came)
    return pl.pallas_call(
        functools.partial(feed_weights_body, sets),
        grid=(1,),
        out_shape=shape(dims, BF),
        in_specs=[spec(x) for x in ins],
        out_specs=pl.BlockSpec(dims, lambda i: (0, 0)),
        compiler_params=params(16),
        cost_estimate=cost(6),
        name="feed_weights",
    )(*ins)


def self_backward_body(tp, others, cot, gnm, x2, x1, gain_m, gain_s, qkv, *refs):
    gots, refs = refs[:others], refs[others:]
    n = tp
    parts = pack_parts(refs[:n], tp, None)
    b2, dqkv, g1, b1, vec, wo_b, wqkv_b, g2, gso, gns, sems = refs[-11:]
    rows, d = cot.shape
    w = d // tp
    wqkv_c = col_copies(parts, 0, 3 * w, wqkv_b, sems.at[0])
    wo_c = block_copies(parts, 3 * w, w, wo_b, sems.at[1])
    begin(wo_c)
    begin(wqkv_c)
    vec[...] = jnp.zeros_like(vec)

    @pl.loop(0, rows // PB)
    def _(i):
        s = rows_at(i, PB)
        u = functools.reduce(jnp.add, [r[s, :].astype(F32) for r in gots], gnm[s, :])
        xhat, r = normalise(x2[s, :])
        g3 = cot[s, :].astype(F32)
        y = g3 + norm_back(u, xhat, r, gain_m[...])
        g2[s, :] = y
        b2[s, :] = y.astype(BF)
        vec[0:1, :] += colsum(g3)
        vec[1:2, :] += colsum(u * xhat)
        vec[2:3, :] += colsum(y)

    finish(wo_c)
    gso[...] = nt(b2[...], wo_b[...]).astype(BF)

    @pl.loop(0, rows // PB)
    def _(g):
        s = rows_at(g, PB)
        for heads in head_sets(tp, w, 8):
            qs, ks, vs = (
                [qkv[s, p * 3 * w + lo + h : p * 3 * w + lo + h + HD] for p, h in heads]
                for lo in (0, w, 2 * w)
            )
            dos = [gso[s, p * w + h : p * w + h + HD] for p, h in heads]
            ss = [nt(k, x) for x, k in zip(qs, ks)]
            dps = [nt(v, x) for x, v in zip(dos, vs)]
            prs = [softmax_parts(x, 0) for x in ss]
            dss = [
                (x * (y - jnp.sum(y * x, axis=0, keepdims=True))).astype(BF) for x, y in zip(prs, dps)
            ]
            dqs = [(tn(x, k) * SCALE).astype(BF) for x, k in zip(dss, ks)]
            dks = [(nn(x, y) * SCALE).astype(BF) for x, y in zip(dss, qs)]
            dvs = [nn(x.astype(BF), y).astype(BF) for x, y in zip(prs, dos)]
            for lo, parts_out in ((0, dqs), (w, dks), (2 * w, dvs)):
                for (p, h), x in zip(heads, parts_out):
                    dqkv[s, p * 3 * w + lo + h : p * 3 * w + lo + h + HD] = x

    finish(wqkv_c)
    gns[...] = nt(dqkv[...], wqkv_b[...])

    @pl.loop(0, rows // PB)
    def _(i):
        s = rows_at(i, PB)
        u = gns[s, :]
        xhat, r = normalise(x1[s, :])
        y = g2[s, :] + norm_back(u, xhat, r, gain_s[...])
        g1[s, :] = y
        b1[s, :] = y.astype(BF)
        vec[3:4, :] += colsum(u * xhat)
        vec[4:5, :] += colsum(y)


def self_backward(cot, gnm, gots, x2, x1, gain_m, gain_s, qkv, pack, after):
    tp = len(pack)
    rows, d = cot.shape
    return pl.pallas_call(
        functools.partial(self_backward_body, tp, len(gots)),
        out_shape=(
            shape((rows, d), BF),
            shape((rows, 3 * d), BF),
            shape((rows, d), F32),
            shape((rows, d), BF),
            shape((8, d), F32),
        ),
        in_specs=[VM] * (7 + len(gots)) + [ANY] * (len(pack) + len(after)),
        out_specs=[VM] * 5,
        scratch_shapes=[
            pltpu.VMEM((d, d), BF),
            pltpu.VMEM((d, 3 * d), BF),
            pltpu.VMEM((rows, d), F32),
            pltpu.VMEM((rows, d), BF),
            pltpu.VMEM((rows, d), F32),
            pltpu.SemaphoreType.DMA((2,)),
        ],
        compiler_params=params(44),
        cost_estimate=cost(27),
        name="self_backward",
    )(cot, gnm, x2, x1, gain_m, gain_s, qkv, *gots, *pack, *after)


def cross_backward_body(tp, idx, lens, b1, g1, x0, gain_c, q, kv, *refs):
    n = tp
    parts = pack_parts(refs[:n], tp, None)
    dq, dkv, g0, emb, vec, wo_b, wq_b, gco, gnc, dacc, kv_b, sems = refs[-12:]
    rows, d = b1.shape
    w = d // tp
    wq_c = col_copies(parts, 0, w, wq_b, sems.at[0])
    wo_c = block_copies(parts, w, w, wo_b, sems.at[1])
    kv_c = [pltpu.make_async_copy(kv, kv_b, sems.at[2])]
    begin(wo_c)
    begin(kv_c)
    begin(wq_c)
    vec[...] = jnp.zeros_like(vec)
    emb[...] = jnp.zeros_like(emb)
    ext = kv.shape[0]

    @pl.loop(0, ext // PB)
    def _(i):
        dacc[rows_at(i, PB), :] = jnp.zeros((PB, dacc.shape[1]), F32)

    finish(wo_c)
    gco[...] = nt(b1[...], wo_b[...]).astype(BF)
    finish(kv_c)

    @pl.loop(0, rows // PB)
    def _(g):
        s = rows_at(g, PB)
        at = [rows_at(idx[g * NB + n], PB) for n in range(NB)]
        row = lax.broadcasted_iota(jnp.int32, (PB, PB), 0)
        live = jnp.concatenate([(row < lens[g * NB + n]).astype(jnp.int32) for n in range(NB)], axis=0) > 0
        for heads in head_sets(tp, w, 8):
            def part(lo):
                return [
                    jnp.concatenate([kv_b[a, p * 2 * w + lo + h : p * 2 * w + lo + h + HD] for a in at], axis=0)
                    for p, h in heads
                ]

            qs, dos = ([r[s, p * w + h : p * w + h + HD] for p, h in heads] for r in (q, gco))
            ks, vs = part(0), part(w)
            ss = [jnp.where(live, nt(k, x), NEG) for x, k in zip(qs, ks)]
            dps = [nt(v, x) for x, v in zip(dos, vs)]
            prs = [softmax_parts(x, 0) for x in ss]
            dss = [
                (x * (y - jnp.sum(y * x, axis=0, keepdims=True))).astype(BF) for x, y in zip(prs, dps)
            ]
            dqs = [(tn(x, k) * SCALE).astype(BF) for x, k in zip(dss, ks)]
            dks = [nn(x, y) for x, y in zip(dss, qs)]
            dvs = [nn(x.astype(BF), y) for x, y in zip(prs, dos)]
            for (p, h), x, y, z in zip(heads, dqs, dks, dvs):
                dq[s, p * w + h : p * w + h + HD] = x
                k0 = p * 2 * w + h
                for j, a in enumerate(at):
                    dacc[a, k0 : k0 + HD] += y[j * PB : (j + 1) * PB, :]
                    dacc[a, k0 + w : k0 + w + HD] += z[j * PB : (j + 1) * PB, :]

    @pl.loop(0, ext // PB)
    def _(i):
        s = rows_at(i, PB)
        for p in range(tp):
            k0 = p * 2 * w
            dkv[s, k0 : k0 + w] = (dacc[s, k0 : k0 + w] * SCALE).astype(BF)
            dkv[s, k0 + w : k0 + 2 * w] = dacc[s, k0 + w : k0 + 2 * w].astype(BF)

    finish(wq_c)
    gnc[...] = nt(dq[...], wq_b[...])

    @pl.loop(0, rows // PB)
    def _(i):
        s = rows_at(i, PB)
        u = gnc[s, :]
        xhat, r = normalise(x0[s, :])
        y = g1[s, :] + norm_back(u, xhat, r, gain_c[...])
        g0[s, :] = y.astype(BF)
        emb[...] += y
        vec[0:1, :] += colsum(u * xhat)


def cross_backward(idx, lens, b1, g1, x0, gain_c, q, kv, pack, after):
    tp = len(pack)
    rows, d = b1.shape
    ext = kv.shape[0]
    return pl.pallas_call(
        functools.partial(cross_backward_body, tp),
        out_shape=(
            shape((rows, d), BF),
            shape((ext, 2 * d), BF),
            shape((rows, d), BF),
            shape((PB, d), F32),
            shape((8, d), F32),
        ),
        in_specs=[SM] * 2 + [VM] * 5 + [ANY] * (1 + len(pack) + len(after)),
        out_specs=[VM] * 5,
        scratch_shapes=[
            pltpu.VMEM((d, d), BF),
            pltpu.VMEM((d, d), BF),
            pltpu.VMEM((rows, d), BF),
            pltpu.VMEM((rows, d), F32),
            pltpu.VMEM((ext, 2 * d), F32),
            pltpu.VMEM((ext, 2 * d), BF),
            pltpu.SemaphoreType.DMA((3,)),
        ],
        compiler_params=params(58),
        cost_estimate=cost(35),
        name="cross_backward",
    )(idx, lens, b1, g1, x0, gain_c, q, kv, *pack, *after)


def tn_into(out, lo, left, right, extra):
    n = left.shape[1]
    tile = min(256, n)
    for k in range(n // tile):
        r = slice(lo + k * tile, lo + (k + 1) * tile)
        y = tn(left[:, k * tile : (k + 1) * tile], right[...])
        if extra is not None:
            y = y + extra[r, :].astype(F32)
        out[r, :] = y.astype(BF)


def two(ref):
    n = ref.shape[0] // 2
    return ref.at[pl.ds(0, n), :], ref.at[pl.ds(n, n), :]


def self_weights_body(ns, dqkv, o, b2, *refs):
    ea, eb = two(refs[0]) if len(refs) > 1 else (None, None)
    a, b = two(refs[-1])
    w = o.shape[1]
    tn_into(a, 0, dqkv.at[:, pl.ds(0, w)], ns, ea)
    tn_into(b, 0, dqkv.at[:, pl.ds(w, 2 * w)], ns, eb)
    tn_into(a, w, o, b2, ea)


def column_block(x, p, n):
    return pl.BlockSpec((x.shape[0], n), lambda i: (0, p))


def whole_block(x):
    return pl.BlockSpec(x.shape, lambda i: (0, 0))


def self_weights(p, w, ns, dqkv, o, b2, came, late):
    d = ns.shape[1]
    return pl.pallas_call(
        lambda *refs: self_weights_body(*refs[: 4 + len(came)], refs[-1]),
        grid=(1,),
        out_shape=shape((4 * w, d), BF),
        in_specs=[whole_block(ns), column_block(dqkv, p, 3 * w), column_block(o, p, w), whole_block(b2)]
        + [whole_block(x) for x in came]
        + [ANY] * len(late),
        out_specs=pl.BlockSpec((4 * w, d), lambda i: (0, 0)),
        compiler_params=params(58),
        cost_estimate=cost(4),
        name="self_weights",
    )(ns, dqkv, o, b2, *came, *late)


def cross_weights_body(nc, dq, o, b1, dkv, points, came0, came1, *refs):
    ext_b, sem = refs[-2:]
    came, outs = (refs[:1], refs[1:-2]) if len(refs) == 5 else ((), refs[:-2])
    ea, eb = two(came[0]) if came else (None, None)
    a, b = outs if len(outs) == 2 else two(outs[0])
    half = ext_b.shape[0] // 2
    copies = row_copies([came0, came1], ext_b, sem) + [
        pltpu.make_async_copy(points.at[pl.ds(0, half), :], ext_b.at[pl.ds(half, half), :], sem)
    ]
    begin(copies)
    w = o.shape[1]
    tn_into(a, 0, dq, nc, ea)
    tn_into(a, w, o, b1, ea)
    finish(copies)
    tn_into(b, 0, dkv, ext_b, eb)


def cross_weights(p, w, nc, dq, o, b1, dkv, points, came_points, came, late):
    d = nc.shape[1]
    rows = [4 * w] if p % 2 else [2 * w] * 2
    n, k = 8 + len(came), 2 + len(rows)
    return pl.pallas_call(
        lambda *refs: cross_weights_body(*refs[:n], *refs[-k:]),
        grid=(1,),
        out_shape=[shape((r, d), BF) for r in rows],
        in_specs=[
            whole_block(nc),
            column_block(dq, p, w),
            column_block(o, p, w),
            whole_block(b1),
            column_block(dkv, p, 2 * w),
        ]
        + [ANY] * 3
        + [whole_block(x) for x in came]
        + [ANY] * len(late),
        out_specs=[pl.BlockSpec((r, d), lambda i: (0, 0)) for r in rows],
        scratch_shapes=[pltpu.VMEM((dkv.shape[0], d), BF), pltpu.SemaphoreType.DMA],
        compiler_params=params(58),
        cost_estimate=cost(8),
        name="cross_weights",
    )(nc, dq, o, b1, dkv, points, *came_points, *came, *late)


def flip(x, axis, bit):
    n = lax.axis_size(axis)
    return lax.ppermute(x, axis, [(i, i ^ (1 << bit)) for i in range(n)])


def bits_of(axis):
    return (lax.axis_size(axis) - 1).bit_length()


def bit_at(axis, bit):
    return (lax.axis_index(axis) >> bit) & 1


def gather_pieces(own, *late):
    have = {0: own}
    for bit in reversed(range(bits_of("tp"))):
        for p in list(have):
            x = have[p] if bit > 0 or p == 0 or not late else after(have[p], *late)
            have[p | (1 << bit)] = flip(x, "tp", bit)
    return [have[p] for p in range(len(have))]


def in_order(pieces):
    x = jnp.stack(pieces)
    for bit in range(bits_of("tp")):
        y = x.reshape((-1, 2, 1 << bit) + x.shape[1:])
        x = jnp.where(bit_at("tp", bit) == 1, y[:, ::-1], y).reshape(x.shape)
    return x


def add(*xs, late=()):
    return after(functools.reduce(jnp.add, [x.astype(F32) for x in xs]).astype(BF), *late)


def after(x, *deps):
    ok = True
    for v in deps:
        first = v[(0,) * v.ndim]
        ok = jnp.logical_and(ok, first == first)
    return jnp.where(ok, x, jnp.zeros_like(x))


def over_tp(have, bit, late=()):
    out = {p: v for p, v in have.items() if not p >> bit & 1}
    for p, v in have.items():
        if p >> bit & 1:
            q = p ^ (1 << bit)
            out[q] = add(out[q], flip(v, "tp", bit), late=late)
    return out


def over_y(have, late=()):
    for k in reversed(range(1, bits_of("tp"))):
        have = over_tp(have, k, late)
    return have


def flip_x(v):
    return lax.ppermute(v, "x", [(0, 1), (1, 0)])


def shares(v):
    nz = lax.axis_size("z")
    v = v.reshape((nz, 2, v.shape[0] // (2 * nz)) + v.shape[1:])
    x = lax.axis_index("x")
    keep = lax.dynamic_index_in_dim(v, x, 1, keepdims=False)
    return keep, lax.dynamic_index_in_dim(v, 1 - x, 1, keepdims=False)


def over_x(v, late=()):
    keep, send = shares(v)
    return add(keep, flip_x(send), late=late)


def sum_z(v):
    return lax.psum(v, "z")


def to_groups(x, per):
    lat, groups, w = x.shape
    n = groups // per
    tp = lax.axis_size("tp")
    y = jnp.transpose(x.reshape(lat, n, per, w), (1, 2, 0, 3))
    y = lax.all_to_all(y, ("z", "x", "tp"), split_axis=0, concat_axis=0, tiled=True)
    y = jnp.transpose(y.reshape(n // tp, tp, per, lat, w), (2, 0, 3, 1, 4))
    return y.reshape(per * lat * (n // tp), tp * w)


def from_groups(x, per):
    tp = lax.axis_size("tp")
    n = lax.axis_size(GRP) * tp
    rows, d = x.shape
    lat, w = rows // per // (n // tp), d // tp
    y = jnp.transpose(x.reshape(per, n // tp, lat, tp, w), (1, 3, 0, 2, 4)).reshape(n, per, lat, w)
    y = lax.all_to_all(y, ("z", "x", "tp"), split_axis=0, concat_axis=0, tiled=True)
    return jnp.transpose(y, (2, 0, 1, 3)).reshape(lat, n * per, w)


def per_device(
    latents,
    skip_latents,
    points,
    neighbours,
    block_lengths,
    latent_embed,
    gain_cross,
    query_cross,
    key_cross,
    value_cross,
    output_cross,
    bias_cross,
    gain_self,
    query_self,
    key_self,
    value_self,
    output_self,
    bias_self,
    gain_mlp,
    hidden_weight,
    hidden_bias,
    output_weight,
    output_bias,
    cotangent,
):
    tp, grp = lax.axis_size("tp"), lax.axis_size(GRP)
    t, i = lax.axis_index("tp"), lax.axis_index(GRP)
    d = query_cross.shape[0]
    w = latent_embed.shape[1]
    lat_rows = latent_embed.shape[0]
    ff = hidden_weight.shape[1]
    groups_here = neighbours.shape[0]
    groups = groups_here * grp
    per = groups_here // tp
    blocks_here = points.shape[0] // PB
    all_blocks = blocks_here * grp
    half_rows = points.shape[0] // 2

    kv_own = packed([[key_cross, value_cross]])[0]
    share = half_rows // 2
    core = bit_at("tp", 0)
    sent = part_of(points, (2 + core).astype(jnp.int32).reshape(1), share)
    first = lax.ppermute(sent, GRP, [(k, (k + 1) % grp) for k in range(grp)])
    came_points = [first, flip(first, "tp", 0)]
    near = lax.dynamic_slice_in_dim(neighbours, t * per, per, 0).reshape(per * NB)
    block = (near - (i * blocks_here - blocks_here // 2)) % all_blocks
    share_blocks = share // PB
    moved = ((block // share_blocks) ^ core) * share_blocks + block % share_blocks
    idx = jnp.where(block < blocks_here // 2, moved, block).astype(jnp.int32)
    lens = block_lengths[near]

    kv_pack = gather_pieces(kv_own)
    qo_own = packed([[query_cross, output_cross]], [kv_own])[0]

    small = jnp.concatenate(
        [
            after(latent_embed, kv_own),
            bias_cross[None],
            bias_self[None],
            output_bias[None],
            hidden_bias.reshape(ff // w, w),
        ]
    )
    small_pieces = gather_pieces(small)
    small_all = in_order(small_pieces)
    by_rows = jnp.transpose(small_all, (1, 0, 2)).reshape(small.shape[0], d)
    embed = by_rows[:lat_rows]
    bias_c, bias_s, bias_o = (by_rows[lat_rows + k : lat_rows + k + 1] for k in range(3))
    hid_bias = jnp.stack([piece[lat_rows + 3 :].reshape(ff) for piece in small_pieces[:2]])

    whid = [hidden_weight, flip(hidden_weight, "tp", 0)]
    wout = [output_weight, flip(output_weight, "tp", 0)]

    gain_c, gain_s, gain_m = gain_cross[None], gain_self[None], gain_mlp[None]
    rows = per * lat_rows
    self_own = packed([[query_self, key_self, value_self, output_self]], [qo_own])[0]
    kv = keys_values(points, came_points, kv_pack, [self_own])
    x0 = (
        to_groups(after(latents, kv_own, sent), per).astype(F32).reshape(per, lat_rows, d) + embed[None]
    ).reshape(rows, d)
    x0 = after(x0, kv)
    qo_pack = gather_pieces(qo_own, kv)
    q, oc, x1, nc, ns = cross_forward(idx, lens, x0, gain_c, gain_s, bias_c, kv, qo_pack)
    self_pack = gather_pieces(self_own, x1)
    cot = after(to_groups(after(cotangent, x0), per), x1)
    qkv, os, x2, nm = self_forward(ns, x1, gain_m, bias_s, self_pack, [cot])

    steps = list(range(2, tp, 2))

    def swap(x, k):
        return lax.ppermute(x, "tp", [(j, j ^ k) for j in range(tp)])

    other_cot = [swap(cot, k) for k in steps]
    other_nm = [swap(nm, k) for k in steps]
    acts, gbs, hbgs = [], [], []
    act, gb, out, gnm, hbg = feed(nm, cot, hid_bias, whid, wout, F32, other_cot)
    acts.append(act)
    gbs.append(gb)
    hbgs.append(hbg)
    back_out, back_gnm = [], []
    for k, n_k, c_k in zip(steps, other_nm, other_cot):
        act, gb, o_k, g_k, hbg = feed(n_k, c_k, hid_bias, whid, wout, BF)
        acts.append(act)
        gbs.append(gb)
        hbgs.append(hbg)
        back_gnm.append(swap(g_k, k))
        back_out.append(o_k)
    nms, cots = [nm] + other_nm, [cot] + other_cot
    sent_o = feed_weights(1, acts, cots, [])
    sent_h = feed_weights(1, gbs, nms, [])
    own_o = feed_weights(0, acts, cots, [flip(sent_o, "tp", 0)])
    own_h = feed_weights(0, gbs, nms, [flip(sent_h, "tp", 0)])

    b2, dqkv, g1, b1, vec_s = self_backward(
        cot, gnm, back_gnm, x2, x1, gain_m, gain_s, qkv, self_pack, [own_o, own_h]
    )

    def pieces(weights, waits):
        got, out, late = {}, {}, []
        for p in reversed(range(1, tp, 2)):
            x = weights(p, [], waits(p, late) + late)
            late = [x]
            got[p - 1] = flip(x, "tp", 0)
        for p in reversed(range(0, tp, 2)):
            out[p] = weights(p, [got[p]], waits(p, late) + late)
            late = [out[p][0] if isinstance(out[p], (list, tuple)) else out[p]]
        return out

    x3 = x2 + out + bias_o
    for k, o_k in zip(steps, back_out):
        x3 = x3 + swap(after(o_k, own_h), k).astype(F32)
    leaving = after(x3.astype(BF), b2)
    sum_o, sum_h = over_x(own_o, [b2]), over_x(own_h, [b2])
    sum_f = jnp.concatenate([sum_o, sum_h], axis=1)
    selfs = pieces(
        lambda p, came, late: self_weights(p, w, ns, dqkv, os, b2, came, late),
        lambda p, late: [sum_f, leaving] if p == tp - 1 else [],
    )
    last = selfs[0]
    feed_z = sum_z(sum_f)
    restored = from_groups(after(leaving, selfs[tp - 2]), per)

    dq, dkv, g0, emb, vec_c = cross_backward(
        idx, lens, b1, g1, x0, gain_c, q, kv, qo_pack, [leaving, *selfs.values()]
    )
    stage = {}

    def norms_and_small(late):
        block_out = after(restored, *late).astype(F32) + skip_latents.astype(F32)
        squares = jnp.sum(jnp.square(block_out), axis=(0, 2))
        by_share = jnp.transpose(
            jnp.concatenate([emb, vec_s[:5], vec_c[:1]]).reshape(lat_rows + 6, tp, w), (1, 0, 2)
        )
        hb_all = functools.reduce(jnp.add, hbgs).reshape(2, ff // w, w)
        owner = lax.broadcasted_iota(jnp.int32, (tp, 1, 1), 0)
        hb_share = jnp.where(owner == t, hb_all[0][None], 0.0) + jnp.where(
            owner == (t ^ 1), hb_all[1][None], 0.0
        )
        sq_rows = jnp.pad(squares, (0, norm_rows * w - groups)).reshape(1, norm_rows, w)
        x = jnp.concatenate(
            [by_share, hb_share, jnp.broadcast_to(sq_rows, (tp, norm_rows, w))], axis=1
        )
        x = jnp.pad(x, ((0, 0), (0, -x.shape[1] % 8), (0, 0)))
        for bit in reversed(range(bits_of("tp"))):
            n = x.shape[0] // 2
            mine = bit_at("tp", bit)
            keep = lax.dynamic_slice_in_dim(x, mine * n, n, 0)
            x = keep + flip(lax.dynamic_slice_in_dim(x, (1 - mine) * n, n, 0), "tp", bit)
        x = x[0].reshape(-1)
        places_rows = 2 * lax.axis_size("z") * 8
        rows_all = -(-x.shape[0] // (d * places_rows)) * places_rows
        return block_out, jnp.pad(x, (0, rows_all * d - x.shape[0])).reshape(rows_all, d).astype(BF)

    norm_rows = -(-groups // w)

    def waits(p, late):
        if p == tp - 1:
            stage["self"] = over_y(selfs, [emb])[0]
            stage["returned"] = from_groups(after(g0, *late), per)
            return [stage["self"], restored]
        if p == tp - 3:
            return []
        if p == tp - 2:
            n = stage["self"].shape[0] // 2
            stage["self"] = [over_x(stage["self"][:n], late), over_x(stage["self"][n:], late)]
            stage["returned"] = from_groups(after(g0, *late), per)
            return stage["self"] + [feed_z]
        if p == 0:
            stage["self"] = after(jnp.concatenate(stage["self"], axis=1), *late)
            stage["out"], stage["small"] = norms_and_small(late)
            return [stage["small"], stage["returned"]]
        return []

    def cross_piece(p, came, late):
        x = cross_weights(p, w, nc, dq, oc, b1, dkv, points, came_points, came, late)
        return x[0] if p % 2 else x

    cross = pieces(cross_piece, waits)
    late = [cross[0][0]]
    self_z = sum_z(stage["self"])
    cross_a = over_y({p: v[0] for p, v in cross.items()})[0]
    cross_b = over_y({p: over_x(v[1], [feed_z]) for p, v in cross.items()})[0]
    little = over_x(stage["small"])
    keep, send = shares(cross_a)
    half = feed_z.shape[1] // 2
    feed_ox = flip_x(after(feed_z[:, :half], send))
    cross_z = jnp.concatenate([add(keep, flip_x(send)), cross_b, little], axis=1)
    cross_z = after(cross_z, self_z, feed_ox)
    feed_hx = flip_x(after(feed_z[:, half:], cross_z))
    self_x = flip_x(after(self_z, cross_z))
    cross_z = after(sum_z(cross_z), self_x)
    returned = stage["returned"]
    cross_x = flip_x(cross_z)
    n = little.shape[1]
    low = lax.axis_index("x") == 0
    own_n, other_n = cross_z[:, -n:], cross_x[:, -n:]
    total = jnp.where(low, jnp.stack([own_n, other_n], 1), jnp.stack([other_n, own_n], 1))
    total = total.astype(F32).reshape(-1)
    total = total[: total.shape[0] // w * w].reshape(-1, w)
    places = lax.axis_index("x").astype(jnp.int32).reshape(1)
    output_weight_grad, hidden_weight_grad = final_feed(places, feed_z, feed_ox, feed_hx)
    query_self_grad, key_self_grad, value_self_grad, output_self_grad = final(
        places, w, self_z, self_x
    )
    block_out = stage["out"]
    latents_grad = returned.astype(F32)

    query_cross_grad, key_cross_grad, value_cross_grad, output_cross_grad = final(
        places, w, cross_z, cross_x, [output_weight_grad, hidden_weight_grad, output_self_grad]
    )
    embed_grad = total[:lat_rows]
    (
        output_bias_grad,
        gain_mlp_grad,
        bias_self_grad,
        gain_self_grad,
        bias_cross_grad,
        gain_cross_grad,
    ) = (total[lat_rows + k] for k in range(6))
    at = lat_rows + 6
    hidden_bias_grad = total[at : at + ff // w].reshape(ff)
    at += ff // w
    square_sums = total[at : at + norm_rows].reshape(norm_rows * w)[:groups]
    group_norms = jnp.sqrt(square_sums / (lat_rows * d))

    return (
        block_out,
        group_norms,
        latents_grad,
        embed_grad,
        gain_cross_grad,
        query_cross_grad,
        key_cross_grad,
        value_cross_grad,
        output_cross_grad,
        bias_cross_grad,
        gain_self_grad,
        query_self_grad,
        key_self_grad,
        value_self_grad,
        output_self_grad,
        bias_self_grad,
        gain_mlp_grad,
        hidden_weight_grad,
        hidden_bias_grad,
        output_weight_grad,
        output_bias_grad,
    )


def solution(mesh):
    grp, tp = mesh.shape["grp"], mesh.shape["tp"]
    own = jax.sharding.Mesh(mesh.devices.reshape(grp // 2, 2, tp), GRP + ("tp",))
    lay = P(GRP, None, "tp")
    cols, rows, part = P(None, "tp"), P("tp", None), P("tp")
    attn = (P(), cols, cols, cols, rows, part)
    return jax.shard_map(
        per_device,
        mesh=own,
        in_specs=(lay, lay, P(GRP, None), P(GRP, None), P(), cols)
        + attn
        + attn
        + (P(), cols, part, rows, part, lay),
        out_specs=(lay, P(), lay, cols)
        + (part, cols, cols, cols, rows, part)
        + (part, cols, cols, cols, rows, part)
        + (part, cols, part, rows, part),
        check_vma=False,
    )
```

```python
import functools

import jax
import jax.numpy as jnp
from jax import lax
from jax.experimental import pallas as pl
from jax.experimental.pallas import tpu as pltpu
from jax.sharding import PartitionSpec as P

HD = 128
PB = 128
NB = 4
EPS = 1e-05
NEG = -1e30
SCALE = HD ** (-0.5)
BF = jnp.bfloat16
F32 = jnp.float32
GRP = ("z", "x")

ANY = pl.BlockSpec(memory_space=pl.ANY)
VM = pl.BlockSpec(memory_space=pltpu.VMEM)
SM = pl.BlockSpec(memory_space=pltpu.SMEM)


def shape(dims, kind):
    return jax.ShapeDtypeStruct(dims, kind)


def params(mib):
    return pltpu.CompilerParams(vmem_limit_bytes=mib * 2**20)


def cost(us):
    return pl.CostEstimate(flops=int(us * 1.1e9), bytes_accessed=int(us * 1e6), transcendentals=0)


def nn(left, right):
    return lax.dot_general(left, right, (((1,), (0,)), ((), ())), preferred_element_type=F32)


def nt(left, right):
    return lax.dot_general(left, right, (((1,), (1,)), ((), ())), preferred_element_type=F32)


def tn(left, right):
    return lax.dot_general(left, right, (((0,), (0,)), ((), ())), preferred_element_type=F32)


def rows_at(i, n):
    return pl.ds(pl.multiple_of(i * n, n), n)


def normalise(x):
    d = x - jnp.mean(x, axis=1, keepdims=True)
    r = lax.rsqrt(jnp.mean(d * d, axis=1, keepdims=True) + EPS)
    return d * r, r


def norm_back(u, xhat, r, gain):
    w = u * gain
    a = jnp.mean(w, axis=1, keepdims=True)
    b = jnp.mean(w * xhat, axis=1, keepdims=True)
    return r * (w - a - xhat * b)


def colsum(x):
    return jnp.sum(x, axis=0, keepdims=True)


def begin(copies):
    for c in copies:
        c.start()


def finish(copies):
    for c in copies:
        c.wait()


def row_copies(pieces, buf, sem):
    n = pieces[0].shape[0]
    return [pltpu.make_async_copy(s, buf.at[pl.ds(p * n, n), :], sem) for p, s in enumerate(pieces)]


def pack_parts(refs, tp, place):
    if len(refs) == tp:
        return [(p, None, r) for p, r in enumerate(refs)]
    parts = [(0, None, refs[0]), (1, None, refs[1])]
    for p in range(2, tp):
        parts.append((p, place[0], refs[2 * p - 2]))
        parts.append((p, 1 - place[0], refs[2 * p - 1]))
    return parts


def col_copies(parts, at, n, buf, sem):
    out = []
    for p, h, r in parts:
        to = pl.ds(p * n, n)
        k = r.shape[0]
        dst = buf.at[:, to] if h is None else buf.at[rows_at(h, k), to]
        out.append(pltpu.make_async_copy(r.at[:, pl.ds(at, n)], dst, sem))
    return out


def block_copies(parts, at, w, buf, sem):
    out = []
    for p, h, r in parts:
        count = r.shape[0] // w
        for k in range(count):
            col = k * w if h is None else pl.multiple_of((h * count + k) * w, 128)
            src = r.at[pl.ds(k * w, w), pl.ds(at, w)]
            out.append(pltpu.make_async_copy(src, buf.at[pl.ds(p * w, w), pl.ds(col, w)], sem))
    return out


def softmax_parts(s, axis):
    e = jnp.exp((s - jnp.max(s, axis=axis, keepdims=True)) * SCALE)
    return e * (1.0 / jnp.sum(e, axis=axis, keepdims=True))


def head_sets(tp, w, size):
    heads = [(p, h * HD) for p in range(tp) for h in range(w // HD)]
    return [heads[i : i + size] for i in range(0, len(heads), size)]


def pack_body(counts, *refs):
    outs, at = refs[-len(counts) :], 0
    for n, out in zip(counts, outs):
        col, rows = 0, out.shape[0]
        for r in refs[at : at + n]:
            if r.shape[0] == rows:
                out[:, col : col + r.shape[1]] = r[...]
                col += r.shape[1]
            else:
                w = r.shape[0]
                for k in range(rows // w):
                    out[k * w : (k + 1) * w, col : col + w] = r[:, k * w : (k + 1) * w]
                col += w
        at += n


def packed(groups, late=()):
    counts = [len(g) for g in groups]
    ins = [x for g in groups for x in g]
    rows = groups[0][0].shape[0]
    outs = []
    for g in groups:
        cols = sum(x.shape[1] if x.shape[0] == rows else x.shape[0] for x in g)
        outs.append(shape((rows, cols), g[0].dtype))
    n = len(ins)
    return pl.pallas_call(
        lambda *refs: pack_body(counts, *refs[:n], *refs[n + len(late) :]),
        out_shape=outs,
        in_specs=[VM] * n + [ANY] * len(late),
        out_specs=[VM] * len(outs),
        compiler_params=params(12),
        cost_estimate=cost(2),
        name="packed",
    )(*ins, *late)


def part_body(n, at, x, *refs):
    out, sem = refs[-2:]
    copy = pltpu.make_async_copy(x.at[pl.ds(pl.multiple_of(at[0] * n, n), n), :], out, sem)
    copy.start()
    copy.wait()


def part_of(x, at, n, late=()):
    return pl.pallas_call(
        functools.partial(part_body, n),
        out_shape=shape((n, x.shape[1]), x.dtype),
        in_specs=[SM] + [ANY] * (1 + len(late)),
        out_specs=VM,
        scratch_shapes=[pltpu.SemaphoreType.DMA],
        cost_estimate=cost(1),
        name="part_of",
    )(at, x, *late)


def share_copies(places, parts, bufs, sem):
    out = []
    for r, x in zip(parts, (places[0], 1 - places[0])):
        c = bufs[0].shape[0] // (2 * r.shape[0])
        for z in range(r.shape[0]):
            for j, buf in enumerate(bufs):
                src = r.at[z, pl.ds(j * c, c), :]
                out.append(pltpu.make_async_copy(src, buf.at[rows_at(2 * z + x, c), :], sem))
    return out


def final_body(places, own, other, *refs):
    q, k, v, o, qo_b, kv_b, sem = refs[-7:]
    copies = share_copies(places, (own, other), (qo_b, kv_b), sem)
    begin(copies)
    finish(copies)
    w = o.shape[0]
    q[...] = qo_b[0:w, :].astype(F32).T
    o[...] = qo_b[w : 2 * w, :].astype(F32)
    k[...] = kv_b[0:w, :].astype(F32).T
    v[...] = kv_b[w : 2 * w, :].astype(F32).T


def final(places, w, own, other, late=()):
    d = own.shape[2]
    tall, flat = shape((d, w), F32), shape((w, d), F32)
    return pl.pallas_call(
        final_body,
        out_shape=(tall, tall, tall, flat),
        in_specs=[SM] + [ANY] * (2 + len(late)),
        out_specs=[VM] * 4,
        scratch_shapes=[pltpu.VMEM((2 * w, d), BF)] * 2 + [pltpu.SemaphoreType.DMA],
        compiler_params=params(58),
        cost_estimate=cost(5),
        name="final",
    )(places, own, other, *late)


def final_feed_body(places, own, other_o, other_h, out, hid, out_b, hid_b, sem):
    c = other_o.shape[1]
    copies = []
    for z in range(own.shape[0]):
        here, there = rows_at(2 * z + places[0], c), rows_at(2 * z + 1 - places[0], c)
        for k, (other, buf) in enumerate(((other_o, out_b), (other_h, hid_b))):
            src = own.at[z, pl.ds(k * c, c), :]
            copies.append(pltpu.make_async_copy(src, buf.at[here, :], sem))
            copies.append(pltpu.make_async_copy(other.at[z], buf.at[there, :], sem))
    begin(copies)
    finish(copies)
    out[...] = out_b[...].astype(F32)
    hid[...] = hid_b[...].astype(F32).T


def final_feed(places, own, other_o, other_h):
    nz, c, d = own.shape
    ff = nz * c
    return pl.pallas_call(
        final_feed_body,
        out_shape=(shape((ff, d), F32), shape((d, ff), F32)),
        in_specs=[SM] + [ANY] * 3,
        out_specs=[VM] * 2,
        scratch_shapes=[pltpu.VMEM((ff, d), BF)] * 2 + [pltpu.SemaphoreType.DMA],
        compiler_params=params(58),
        cost_estimate=cost(6),
        name="final_feed",
    )(places, own, other_o, other_h)


def keys_body(tp, points, came0, came1, *refs):
    packs, (kv, kv_b, ext_b, wkv_b, sems) = refs[:tp], refs[-5:]
    ext, d = ext_b.shape
    half = ext // 2
    near_c = [pltpu.make_async_copy(points.at[pl.ds(0, half), :], ext_b.at[pl.ds(half, half), :], sems.at[0])]
    far_c = row_copies([came0, came1], ext_b, sems.at[1])
    w_c = col_copies(pack_parts(packs, tp, None), 0, packs[0].shape[1], wkv_b, sems.at[2])
    for c in (w_c, near_c, far_c):
        begin(c)
    finish(w_c)
    span = 512

    def out_copy(i):
        s = rows_at(i, span)
        return pltpu.make_async_copy(kv_b.at[s, :], kv.at[s, :], sems.at[3])

    def work(i):
        s = rows_at(i, span)
        kv_b[s, :] = nn(ext_b[s, :], wkv_b[...]).astype(BF)
        out_copy(i).start()

    finish(near_c)
    pl.loop(half // span, ext // span)(work)
    finish(far_c)
    pl.loop(0, half // span)(work)

    @pl.loop(0, ext // span)
    def _(i):
        out_copy(i).wait()


def keys_values(points, came, packs, late):
    tp = len(packs)
    ext, d = points.shape
    return pl.pallas_call(
        functools.partial(keys_body, tp),
        out_shape=shape((ext, 2 * d), BF),
        in_specs=[ANY] * (3 + tp + len(late)),
        out_specs=ANY,
        scratch_shapes=[
            pltpu.VMEM((ext, 2 * d), BF),
            pltpu.VMEM((ext, d), BF),
            pltpu.VMEM((d, 2 * d), BF),
            pltpu.SemaphoreType.DMA((4,)),
        ],
        compiler_params=params(58),
        cost_estimate=cost(14),
        name="keys_values",
    )(points, *came, *packs, *late)


def cross_forward_body(tp, idx, lens, x0, gain_c, gain_s, bias, kv, *refs):
    parts = pack_parts(refs[:tp], tp, None)
    (q, o, x1, nc, ns, kv_b, wq_b, wo_b, acc, sems) = refs[-10:]
    rows, d = x0.shape
    w = d // tp
    wq_c = col_copies(parts, 0, w, wq_b, sems.at[0])
    wo_c = block_copies(parts, w, w, wo_b, sems.at[1])
    kv_c = [pltpu.make_async_copy(kv, kv_b, sems.at[2])]
    for c in (wq_c, kv_c, wo_c):
        begin(c)

    @pl.loop(0, rows // PB)
    def _(i):
        s = rows_at(i, PB)
        xhat, _ = normalise(x0[s, :])
        nc[s, :] = (xhat * gain_c[...]).astype(BF)

    finish(wq_c)
    q[...] = nn(nc[...], wq_b[...]).astype(BF)
    finish(kv_c)

    @pl.loop(0, rows // PB)
    def _(g):
        s = rows_at(g, PB)
        at = [rows_at(idx[g * NB + n], PB) for n in range(NB)]
        lane = lax.broadcasted_iota(jnp.int32, (1, PB), 1)
        live = jnp.concatenate([(lane < lens[g * NB + n]).astype(jnp.int32) for n in range(NB)], axis=1) > 0
        for heads in head_sets(tp, w, 8):
            def part(lo):
                return [
                    jnp.concatenate([kv_b[a, p * 2 * w + lo + h : p * 2 * w + lo + h + HD] for a in at], axis=0)
                    for p, h in heads
                ]

            qs = [q[s, p * w + h : p * w + h + HD] for p, h in heads]
            ks, vs = part(0), part(w)
            ss = [jnp.where(live, nt(x, k), NEG) for x, k in zip(qs, ks)]
            ps = [softmax_parts(x, 1).astype(BF) for x in ss]
            outs = [nn(x, v).astype(BF) for x, v in zip(ps, vs)]
            for (p, h), x in zip(heads, outs):
                o[s, p * w + h : p * w + h + HD] = x

    finish(wo_c)
    acc[...] = nn(o[...], wo_b[...])

    @pl.loop(0, rows // PB)
    def _(i):
        s = rows_at(i, PB)
        y = x0[s, :] + acc[s, :] + bias[...]
        x1[s, :] = y
        xhat, _ = normalise(y)
        ns[s, :] = (xhat * gain_s[...]).astype(BF)


def cross_forward(idx, lens, x0, gain_c, gain_s, bias, kv, packs):
    tp = len(packs)
    rows, d = x0.shape
    ext = kv.shape[0]
    return pl.pallas_call(
        functools.partial(cross_forward_body, tp),
        out_shape=(
            shape((rows, d), BF),
            shape((rows, d), BF),
            shape((rows, d), F32),
            shape((rows, d), BF),
            shape((rows, d), BF),
        ),
        in_specs=[SM] * 2 + [VM] * 4 + [ANY] * (1 + tp),
        out_specs=[VM] * 5,
        scratch_shapes=[
            pltpu.VMEM((ext, 2 * d), BF),
            pltpu.VMEM((d, d), BF),
            pltpu.VMEM((d, d), BF),
            pltpu.VMEM((rows, d), F32),
            pltpu.SemaphoreType.DMA((3,)),
        ],
        compiler_params=params(58),
        cost_estimate=cost(20),
        name="cross_forward",
    )(idx, lens, x0, gain_c, gain_s, bias, kv, *packs)


def self_forward_body(tp, ns, x1, gain_m, bias, *refs):
    n = tp
    parts = pack_parts(refs[:n], tp, None)
    qkv, o, x2, nm, wqkv_b, wo_b, acc, sems = refs[-8:]
    rows, d = x1.shape
    w = d // tp
    wqkv_c = col_copies(parts, 0, 3 * w, wqkv_b, sems.at[0])
    wo_c = block_copies(parts, 3 * w, w, wo_b, sems.at[1])
    begin(wqkv_c)
    begin(wo_c)
    finish(wqkv_c)
    qkv[...] = nn(ns[...], wqkv_b[...]).astype(BF)

    @pl.loop(0, rows // PB)
    def _(g):
        s = rows_at(g, PB)
        for heads in head_sets(tp, w, 8):
            qs, ks, vs = (
                [qkv[s, p * 3 * w + lo + h : p * 3 * w + lo + h + HD] for p, h in heads]
                for lo in (0, w, 2 * w)
            )
            ss = [nt(x, k) for x, k in zip(qs, ks)]
            ps = [softmax_parts(x, 1).astype(BF) for x in ss]
            outs = [nn(x, v).astype(BF) for x, v in zip(ps, vs)]
            for (p, h), x in zip(heads, outs):
                o[s, p * w + h : p * w + h + HD] = x

    finish(wo_c)
    acc[...] = nn(o[...], wo_b[...])

    @pl.loop(0, rows // PB)
    def _(i):
        s = rows_at(i, PB)
        y = x1[s, :] + acc[s, :] + bias[...]
        x2[s, :] = y
        xhat, _ = normalise(y)
        nm[s, :] = (xhat * gain_m[...]).astype(BF)


def self_forward(ns, x1, gain_m, bias, pack, late):
    rows, d = x1.shape
    tp = len(pack)
    return pl.pallas_call(
        functools.partial(self_forward_body, tp),
        out_shape=(
            shape((rows, 3 * d), BF),
            shape((rows, d), BF),
            shape((rows, d), F32),
            shape((rows, d), BF),
        ),
        in_specs=[VM] * 4 + [ANY] * (len(pack) + len(late)),
        out_specs=[VM] * 4,
        scratch_shapes=[
            pltpu.VMEM((d, 3 * d), BF),
            pltpu.VMEM((d, d), BF),
            pltpu.VMEM((rows, d), F32),
            pltpu.SemaphoreType.DMA((2,)),
        ],
        compiler_params=params(32),
        cost_estimate=cost(22),
        name="self_forward",
    )(ns, x1, gain_m, bias, *pack, *late)


ROOT = 0.7978845608028654
CUBE = 0.044715


def feed_body(nm, cot, hb, wh0, wh1, wo0, wo1, *refs):
    act, gb, out, gnm, hbg = refs[-5:]
    rows, d = nm.shape
    ff = wh0.shape[1]
    span = min(512, ff)
    for p, (wh, wo) in enumerate(((wh0, wo0), (wh1, wo1))):
        for j in range(ff // span):
            s = slice(j * span, (j + 1) * span)
            x = nn(nm[...], wh[:, s]) + hb[p : p + 1, s]
            ga = nt(cot[...], wo[s, :])
            sq = x * x
            t = jnp.tanh(ROOT * x * (1.0 + CUBE * sq))
            half = 0.5 * (1.0 + t)
            act[p, :, s] = (x * half).astype(BF)
            slope = half + 0.5 * x * (1.0 - t * t) * (ROOT + (3.0 * ROOT * CUBE) * sq)
            g = (ga * slope).astype(BF)
            gb[p, :, s] = g
            hbg[p : p + 1, s] = colsum(g.astype(F32))
    gnm[...] = (nt(gb[0], wh0[...]) + nt(gb[1], wh1[...])).astype(gnm.dtype)
    out[...] = (nn(act[0], wo0[...]) + nn(act[1], wo1[...])).astype(out.dtype)


def feed(nm, cot, hb, wh, wo, kind, late=()):
    rows, d = nm.shape
    ff = wh[0].shape[1]
    return pl.pallas_call(
        feed_body,
        out_shape=(
            shape((2, rows, ff), BF),
            shape((2, rows, ff), BF),
            shape((rows, d), kind),
            shape((rows, d), kind),
            shape((2, ff), F32),
        ),
        in_specs=[VM] * 7 + [ANY] * len(late),
        out_specs=[VM] * 5,
        compiler_params=params(32),
        cost_estimate=cost(15),
        name="feed",
    )(nm, cot, hb, *wh, *wo, *late)


def feed_weights_body(sets, *refs):
    lefts, rights, rest = refs[:sets], refs[sets : 2 * sets], refs[2 * sets :]
    out = rest[-1]
    came = rest[0] if len(rest) == 2 else None
    tile = 256

    @pl.loop(0, out.shape[0] // tile)
    def _(i):
        s = rows_at(i, tile)
        y = functools.reduce(jnp.add, [tn(a[0, :, s], c[...]) for a, c in zip(lefts, rights)])
        if came is not None:
            y = y + came[s, :].astype(F32)
        out[s, :] = y.astype(BF)


def feed_weights(p, lefts, rights, came):
    sets = len(lefts)

    def spec(x):
        if x.ndim == 3:
            return pl.BlockSpec((1,) + x.shape[1:], lambda i: (p, 0, 0))
        return pl.BlockSpec(x.shape, lambda i: (0, 0))

    dims = (lefts[0].shape[-1], rights[0].shape[-1])
    ins = list(lefts) + list(rights) + list(came)
    return pl.pallas_call(
        functools.partial(feed_weights_body, sets),
        grid=(1,),
        out_shape=shape(dims, BF),
        in_specs=[spec(x) for x in ins],
        out_specs=pl.BlockSpec(dims, lambda i: (0, 0)),
        compiler_params=params(16),
        cost_estimate=cost(6),
        name="feed_weights",
    )(*ins)


def self_backward_body(tp, others, cot, gnm, x2, x1, gain_m, gain_s, qkv, *refs):
    gots, refs = refs[:others], refs[others:]
    n = tp
    parts = pack_parts(refs[:n], tp, None)
    b2, dqkv, g1, b1, vec, wo_b, wqkv_b, g2, gso, gns, sems = refs[-11:]
    rows, d = cot.shape
    w = d // tp
    wqkv_c = col_copies(parts, 0, 3 * w, wqkv_b, sems.at[0])
    wo_c = block_copies(parts, 3 * w, w, wo_b, sems.at[1])
    begin(wo_c)
    begin(wqkv_c)
    vec[...] = jnp.zeros_like(vec)

    @pl.loop(0, rows // PB)
    def _(i):
        s = rows_at(i, PB)
        u = functools.reduce(jnp.add, [r[s, :].astype(F32) for r in gots], gnm[s, :])
        xhat, r = normalise(x2[s, :])
        g3 = cot[s, :].astype(F32)
        y = g3 + norm_back(u, xhat, r, gain_m[...])
        g2[s, :] = y
        b2[s, :] = y.astype(BF)
        vec[0:1, :] += colsum(g3)
        vec[1:2, :] += colsum(u * xhat)
        vec[2:3, :] += colsum(y)

    finish(wo_c)
    gso[...] = nt(b2[...], wo_b[...]).astype(BF)

    @pl.loop(0, rows // PB)
    def _(g):
        s = rows_at(g, PB)
        for heads in head_sets(tp, w, 8):
            qs, ks, vs = (
                [qkv[s, p * 3 * w + lo + h : p * 3 * w + lo + h + HD] for p, h in heads]
                for lo in (0, w, 2 * w)
            )
            dos = [gso[s, p * w + h : p * w + h + HD] for p, h in heads]
            ss = [nt(k, x) for x, k in zip(qs, ks)]
            dps = [nt(v, x) for x, v in zip(dos, vs)]
            prs = [softmax_parts(x, 0) for x in ss]
            dss = [
                (x * (y - jnp.sum(y * x, axis=0, keepdims=True))).astype(BF) for x, y in zip(prs, dps)
            ]
            dqs = [(tn(x, k) * SCALE).astype(BF) for x, k in zip(dss, ks)]
            dks = [(nn(x, y) * SCALE).astype(BF) for x, y in zip(dss, qs)]
            dvs = [nn(x.astype(BF), y).astype(BF) for x, y in zip(prs, dos)]
            for lo, parts_out in ((0, dqs), (w, dks), (2 * w, dvs)):
                for (p, h), x in zip(heads, parts_out):
                    dqkv[s, p * 3 * w + lo + h : p * 3 * w + lo + h + HD] = x

    finish(wqkv_c)
    gns[...] = nt(dqkv[...], wqkv_b[...])

    @pl.loop(0, rows // PB)
    def _(i):
        s = rows_at(i, PB)
        u = gns[s, :]
        xhat, r = normalise(x1[s, :])
        y = g2[s, :] + norm_back(u, xhat, r, gain_s[...])
        g1[s, :] = y
        b1[s, :] = y.astype(BF)
        vec[3:4, :] += colsum(u * xhat)
        vec[4:5, :] += colsum(y)


def self_backward(cot, gnm, gots, x2, x1, gain_m, gain_s, qkv, pack, after):
    tp = len(pack)
    rows, d = cot.shape
    return pl.pallas_call(
        functools.partial(self_backward_body, tp, len(gots)),
        out_shape=(
            shape((rows, d), BF),
            shape((rows, 3 * d), BF),
            shape((rows, d), F32),
            shape((rows, d), BF),
            shape((8, d), F32),
        ),
        in_specs=[VM] * (7 + len(gots)) + [ANY] * (len(pack) + len(after)),
        out_specs=[VM] * 5,
        scratch_shapes=[
            pltpu.VMEM((d, d), BF),
            pltpu.VMEM((d, 3 * d), BF),
            pltpu.VMEM((rows, d), F32),
            pltpu.VMEM((rows, d), BF),
            pltpu.VMEM((rows, d), F32),
            pltpu.SemaphoreType.DMA((2,)),
        ],
        compiler_params=params(44),
        cost_estimate=cost(27),
        name="self_backward",
    )(cot, gnm, x2, x1, gain_m, gain_s, qkv, *gots, *pack, *after)


def cross_backward_body(tp, idx, lens, b1, g1, x0, gain_c, q, kv, *refs):
    n = tp
    parts = pack_parts(refs[:n], tp, None)
    dq, dkv, g0, emb, vec, wo_b, wq_b, gco, gnc, dacc, kv_b, sems = refs[-12:]
    rows, d = b1.shape
    w = d // tp
    wq_c = col_copies(parts, 0, w, wq_b, sems.at[0])
    wo_c = block_copies(parts, w, w, wo_b, sems.at[1])
    kv_c = [pltpu.make_async_copy(kv, kv_b, sems.at[2])]
    begin(wo_c)
    begin(kv_c)
    begin(wq_c)
    vec[...] = jnp.zeros_like(vec)
    emb[...] = jnp.zeros_like(emb)
    ext = kv.shape[0]

    @pl.loop(0, ext // PB)
    def _(i):
        dacc[rows_at(i, PB), :] = jnp.zeros((PB, dacc.shape[1]), F32)

    finish(wo_c)
    gco[...] = nt(b1[...], wo_b[...]).astype(BF)
    finish(kv_c)

    @pl.loop(0, rows // PB)
    def _(g):
        s = rows_at(g, PB)
        at = [rows_at(idx[g * NB + n], PB) for n in range(NB)]
        row = lax.broadcasted_iota(jnp.int32, (PB, PB), 0)
        live = jnp.concatenate([(row < lens[g * NB + n]).astype(jnp.int32) for n in range(NB)], axis=0) > 0
        for heads in head_sets(tp, w, 8):
            def part(lo):
                return [
                    jnp.concatenate([kv_b[a, p * 2 * w + lo + h : p * 2 * w + lo + h + HD] for a in at], axis=0)
                    for p, h in heads
                ]

            qs, dos = ([r[s, p * w + h : p * w + h + HD] for p, h in heads] for r in (q, gco))
            ks, vs = part(0), part(w)
            ss = [jnp.where(live, nt(k, x), NEG) for x, k in zip(qs, ks)]
            dps = [nt(v, x) for x, v in zip(dos, vs)]
            prs = [softmax_parts(x, 0) for x in ss]
            dss = [
                (x * (y - jnp.sum(y * x, axis=0, keepdims=True))).astype(BF) for x, y in zip(prs, dps)
            ]
            dqs = [(tn(x, k) * SCALE).astype(BF) for x, k in zip(dss, ks)]
            dks = [nn(x, y) for x, y in zip(dss, qs)]
            dvs = [nn(x.astype(BF), y) for x, y in zip(prs, dos)]
            for (p, h), x, y, z in zip(heads, dqs, dks, dvs):
                dq[s, p * w + h : p * w + h + HD] = x
                k0 = p * 2 * w + h
                for j, a in enumerate(at):
                    dacc[a, k0 : k0 + HD] += y[j * PB : (j + 1) * PB, :]
                    dacc[a, k0 + w : k0 + w + HD] += z[j * PB : (j + 1) * PB, :]

    @pl.loop(0, ext // PB)
    def _(i):
        s = rows_at(i, PB)
        for p in range(tp):
            k0 = p * 2 * w
            dkv[s, k0 : k0 + w] = (dacc[s, k0 : k0 + w] * SCALE).astype(BF)
            dkv[s, k0 + w : k0 + 2 * w] = dacc[s, k0 + w : k0 + 2 * w].astype(BF)

    finish(wq_c)
    gnc[...] = nt(dq[...], wq_b[...])

    @pl.loop(0, rows // PB)
    def _(i):
        s = rows_at(i, PB)
        u = gnc[s, :]
        xhat, r = normalise(x0[s, :])
        y = g1[s, :] + norm_back(u, xhat, r, gain_c[...])
        g0[s, :] = y.astype(BF)
        emb[...] += y
        vec[0:1, :] += colsum(u * xhat)


def cross_backward(idx, lens, b1, g1, x0, gain_c, q, kv, pack, after):
    tp = len(pack)
    rows, d = b1.shape
    ext = kv.shape[0]
    return pl.pallas_call(
        functools.partial(cross_backward_body, tp),
        out_shape=(
            shape((rows, d), BF),
            shape((ext, 2 * d), BF),
            shape((rows, d), BF),
            shape((PB, d), F32),
            shape((8, d), F32),
        ),
        in_specs=[SM] * 2 + [VM] * 5 + [ANY] * (1 + len(pack) + len(after)),
        out_specs=[VM] * 5,
        scratch_shapes=[
            pltpu.VMEM((d, d), BF),
            pltpu.VMEM((d, d), BF),
            pltpu.VMEM((rows, d), BF),
            pltpu.VMEM((rows, d), F32),
            pltpu.VMEM((ext, 2 * d), F32),
            pltpu.VMEM((ext, 2 * d), BF),
            pltpu.SemaphoreType.DMA((3,)),
        ],
        compiler_params=params(58),
        cost_estimate=cost(35),
        name="cross_backward",
    )(idx, lens, b1, g1, x0, gain_c, q, kv, *pack, *after)


def tn_into(out, lo, left, right, extra):
    n = left.shape[1]
    tile = min(256, n)
    for k in range(n // tile):
        r = slice(lo + k * tile, lo + (k + 1) * tile)
        y = tn(left[:, k * tile : (k + 1) * tile], right[...])
        if extra is not None:
            y = y + extra[r, :].astype(F32)
        out[r, :] = y.astype(BF)


def two(ref):
    n = ref.shape[0] // 2
    return ref.at[pl.ds(0, n), :], ref.at[pl.ds(n, n), :]


def self_weights_body(ns, dqkv, o, b2, *refs):
    ea, eb = two(refs[0]) if len(refs) > 1 else (None, None)
    a, b = two(refs[-1])
    w = o.shape[1]
    tn_into(a, 0, dqkv.at[:, pl.ds(0, w)], ns, ea)
    tn_into(b, 0, dqkv.at[:, pl.ds(w, 2 * w)], ns, eb)
    tn_into(a, w, o, b2, ea)


def column_block(x, p, n):
    return pl.BlockSpec((x.shape[0], n), lambda i: (0, p))


def whole_block(x):
    return pl.BlockSpec(x.shape, lambda i: (0, 0))


def self_weights(p, w, ns, dqkv, o, b2, came, late):
    d = ns.shape[1]
    return pl.pallas_call(
        lambda *refs: self_weights_body(*refs[: 4 + len(came)], refs[-1]),
        grid=(1,),
        out_shape=shape((4 * w, d), BF),
        in_specs=[whole_block(ns), column_block(dqkv, p, 3 * w), column_block(o, p, w), whole_block(b2)]
        + [whole_block(x) for x in came]
        + [ANY] * len(late),
        out_specs=pl.BlockSpec((4 * w, d), lambda i: (0, 0)),
        compiler_params=params(58),
        cost_estimate=cost(4),
        name="self_weights",
    )(ns, dqkv, o, b2, *came, *late)


def cross_weights_body(nc, dq, o, b1, dkv, points, came0, came1, *refs):
    ext_b, sem = refs[-2:]
    came, outs = (refs[:1], refs[1:-2]) if len(refs) == 5 else ((), refs[:-2])
    ea, eb = two(came[0]) if came else (None, None)
    a, b = outs if len(outs) == 2 else two(outs[0])
    half = ext_b.shape[0] // 2
    copies = row_copies([came0, came1], ext_b, sem) + [
        pltpu.make_async_copy(points.at[pl.ds(0, half), :], ext_b.at[pl.ds(half, half), :], sem)
    ]
    begin(copies)
    w = o.shape[1]
    tn_into(a, 0, dq, nc, ea)
    tn_into(a, w, o, b1, ea)
    finish(copies)
    tn_into(b, 0, dkv, ext_b, eb)


def cross_weights(p, w, nc, dq, o, b1, dkv, points, came_points, came, late):
    d = nc.shape[1]
    rows = [4 * w] if p % 2 else [2 * w] * 2
    n, k = 8 + len(came), 2 + len(rows)
    return pl.pallas_call(
        lambda *refs: cross_weights_body(*refs[:n], *refs[-k:]),
        grid=(1,),
        out_shape=[shape((r, d), BF) for r in rows],
        in_specs=[
            whole_block(nc),
            column_block(dq, p, w),
            column_block(o, p, w),
            whole_block(b1),
            column_block(dkv, p, 2 * w),
        ]
        + [ANY] * 3
        + [whole_block(x) for x in came]
        + [ANY] * len(late),
        out_specs=[pl.BlockSpec((r, d), lambda i: (0, 0)) for r in rows],
        scratch_shapes=[pltpu.VMEM((dkv.shape[0], d), BF), pltpu.SemaphoreType.DMA],
        compiler_params=params(58),
        cost_estimate=cost(8),
        name="cross_weights",
    )(nc, dq, o, b1, dkv, points, *came_points, *came, *late)


def flip(x, axis, bit):
    n = lax.axis_size(axis)
    return lax.ppermute(x, axis, [(i, i ^ (1 << bit)) for i in range(n)])


def bits_of(axis):
    return (lax.axis_size(axis) - 1).bit_length()


def bit_at(axis, bit):
    return (lax.axis_index(axis) >> bit) & 1


def gather_pieces(own, *late):
    have = {0: own}
    for bit in reversed(range(bits_of("tp"))):
        for p in list(have):
            x = have[p] if bit > 0 or p == 0 or not late else after(have[p], *late)
            have[p | (1 << bit)] = flip(x, "tp", bit)
    return [have[p] for p in range(len(have))]


def in_order(pieces):
    x = jnp.stack(pieces)
    for bit in range(bits_of("tp")):
        y = x.reshape((-1, 2, 1 << bit) + x.shape[1:])
        x = jnp.where(bit_at("tp", bit) == 1, y[:, ::-1], y).reshape(x.shape)
    return x


def add(*xs, late=()):
    return after(functools.reduce(jnp.add, [x.astype(F32) for x in xs]).astype(BF), *late)


def after(x, *deps):
    ok = True
    for v in deps:
        first = v[(0,) * v.ndim]
        ok = jnp.logical_and(ok, first == first)
    return jnp.where(ok, x, jnp.zeros_like(x))


def over_tp(have, bit, late=()):
    out = {p: v for p, v in have.items() if not p >> bit & 1}
    for p, v in have.items():
        if p >> bit & 1:
            q = p ^ (1 << bit)
            out[q] = add(out[q], flip(v, "tp", bit), late=late)
    return out


def over_y(have, late=()):
    for k in reversed(range(1, bits_of("tp"))):
        have = over_tp(have, k, late)
    return have


def flip_x(v):
    return lax.ppermute(v, "x", [(0, 1), (1, 0)])


def shares(v):
    nz = lax.axis_size("z")
    v = v.reshape((nz, 2, v.shape[0] // (2 * nz)) + v.shape[1:])
    x = lax.axis_index("x")
    keep = lax.dynamic_index_in_dim(v, x, 1, keepdims=False)
    return keep, lax.dynamic_index_in_dim(v, 1 - x, 1, keepdims=False)


def over_x(v, late=()):
    keep, send = shares(v)
    return add(keep, flip_x(send), late=late)


def sum_z(v):
    return lax.psum(v, "z")


def to_groups(x, per):
    lat, groups, w = x.shape
    n = groups // per
    tp = lax.axis_size("tp")
    y = jnp.transpose(x.reshape(lat, n, per, w), (1, 2, 0, 3))
    y = lax.all_to_all(y, ("z", "x", "tp"), split_axis=0, concat_axis=0, tiled=True)
    y = jnp.transpose(y.reshape(n // tp, tp, per, lat, w), (2, 0, 3, 1, 4))
    return y.reshape(per * lat * (n // tp), tp * w)


def from_groups(x, per):
    tp = lax.axis_size("tp")
    n = lax.axis_size(GRP) * tp
    rows, d = x.shape
    lat, w = rows // per // (n // tp), d // tp
    y = jnp.transpose(x.reshape(per, n // tp, lat, tp, w), (1, 3, 0, 2, 4)).reshape(n, per, lat, w)
    y = lax.all_to_all(y, ("z", "x", "tp"), split_axis=0, concat_axis=0, tiled=True)
    return jnp.transpose(y, (2, 0, 1, 3)).reshape(lat, n * per, w)


def per_device(
    latents,
    skip_latents,
    points,
    neighbours,
    block_lengths,
    latent_embed,
    gain_cross,
    query_cross,
    key_cross,
    value_cross,
    output_cross,
    bias_cross,
    gain_self,
    query_self,
    key_self,
    value_self,
    output_self,
    bias_self,
    gain_mlp,
    hidden_weight,
    hidden_bias,
    output_weight,
    output_bias,
    cotangent,
):
    tp, grp = lax.axis_size("tp"), lax.axis_size(GRP)
    t, i = lax.axis_index("tp"), lax.axis_index(GRP)
    d = query_cross.shape[0]
    w = latent_embed.shape[1]
    lat_rows = latent_embed.shape[0]
    ff = hidden_weight.shape[1]
    groups_here = neighbours.shape[0]
    groups = groups_here * grp
    per = groups_here // tp
    blocks_here = points.shape[0] // PB
    all_blocks = blocks_here * grp
    half_rows = points.shape[0] // 2

    kv_own = packed([[key_cross, value_cross]])[0]
    share = half_rows // 2
    core = bit_at("tp", 0)
    sent = part_of(points, (2 + core).astype(jnp.int32).reshape(1), share)
    first = lax.ppermute(sent, GRP, [(k, (k + 1) % grp) for k in range(grp)])
    came_points = [first, flip(first, "tp", 0)]
    near = lax.dynamic_slice_in_dim(neighbours, t * per, per, 0).reshape(per * NB)
    block = (near - (i * blocks_here - blocks_here // 2)) % all_blocks
    share_blocks = share // PB
    moved = ((block // share_blocks) ^ core) * share_blocks + block % share_blocks
    idx = jnp.where(block < blocks_here // 2, moved, block).astype(jnp.int32)
    lens = block_lengths[near]

    kv_pack = gather_pieces(kv_own)
    qo_own = packed([[query_cross, output_cross]], [kv_own])[0]

    small = jnp.concatenate(
        [
            after(latent_embed, kv_own),
            bias_cross[None],
            bias_self[None],
            output_bias[None],
            hidden_bias.reshape(ff // w, w),
        ]
    )
    small_pieces = gather_pieces(small)
    small_all = in_order(small_pieces)
    by_rows = jnp.transpose(small_all, (1, 0, 2)).reshape(small.shape[0], d)
    embed = by_rows[:lat_rows]
    bias_c, bias_s, bias_o = (by_rows[lat_rows + k : lat_rows + k + 1] for k in range(3))
    hid_bias = jnp.stack([piece[lat_rows + 3 :].reshape(ff) for piece in small_pieces[:2]])

    whid = [hidden_weight, flip(hidden_weight, "tp", 0)]
    wout = [output_weight, flip(output_weight, "tp", 0)]

    gain_c, gain_s, gain_m = gain_cross[None], gain_self[None], gain_mlp[None]
    rows = per * lat_rows
    self_own = packed([[query_self, key_self, value_self, output_self]], [qo_own])[0]
    kv = keys_values(points, came_points, kv_pack, [self_own])
    x0 = (
        to_groups(after(latents, kv_own, sent), per).astype(F32).reshape(per, lat_rows, d) + embed[None]
    ).reshape(rows, d)
    x0 = after(x0, kv)
    qo_pack = gather_pieces(qo_own, kv)
    q, oc, x1, nc, ns = cross_forward(idx, lens, x0, gain_c, gain_s, bias_c, kv, qo_pack)
    self_pack = gather_pieces(self_own, x1)
    cot = after(to_groups(after(cotangent, x0), per), x1)
    qkv, os, x2, nm = self_forward(ns, x1, gain_m, bias_s, self_pack, [cot])

    steps = list(range(2, tp, 2))

    def swap(x, k):
        return lax.ppermute(x, "tp", [(j, j ^ k) for j in range(tp)])

    other_cot = [swap(cot, k) for k in steps]
    other_nm = [swap(nm, k) for k in steps]
    acts, gbs, hbgs = [], [], []
    act, gb, out, gnm, hbg = feed(nm, cot, hid_bias, whid, wout, F32, other_cot)
    acts.append(act)
    gbs.append(gb)
    hbgs.append(hbg)
    back_out, back_gnm = [], []
    for k, n_k, c_k in zip(steps, other_nm, other_cot):
        act, gb, o_k, g_k, hbg = feed(n_k, c_k, hid_bias, whid, wout, BF)
        acts.append(act)
        gbs.append(gb)
        hbgs.append(hbg)
        back_gnm.append(swap(g_k, k))
        back_out.append(o_k)
    nms, cots = [nm] + other_nm, [cot] + other_cot
    sent_o = feed_weights(1, acts, cots, [])
    sent_h = feed_weights(1, gbs, nms, [])
    own_o = feed_weights(0, acts, cots, [flip(sent_o, "tp", 0)])
    own_h = feed_weights(0, gbs, nms, [flip(sent_h, "tp", 0)])

    b2, dqkv, g1, b1, vec_s = self_backward(
        cot, gnm, back_gnm, x2, x1, gain_m, gain_s, qkv, self_pack, [own_o, own_h]
    )

    def pieces(weights, waits):
        got, out, late = {}, {}, []
        for p in reversed(range(1, tp, 2)):
            x = weights(p, [], waits(p, late) + late)
            late = [x]
            got[p - 1] = flip(x, "tp", 0)
        for p in reversed(range(0, tp, 2)):
            out[p] = weights(p, [got[p]], waits(p, late) + late)
            late = [out[p][0] if isinstance(out[p], (list, tuple)) else out[p]]
        return out

    x3 = x2 + out + bias_o
    for k, o_k in zip(steps, back_out):
        x3 = x3 + swap(after(o_k, own_h), k).astype(F32)
    leaving = after(x3.astype(BF), b2)
    sum_o, sum_h = over_x(own_o, [b2]), over_x(own_h, [b2])
    sum_f = jnp.concatenate([sum_o, sum_h], axis=1)
    selfs = pieces(
        lambda p, came, late: self_weights(p, w, ns, dqkv, os, b2, came, late),
        lambda p, late: [sum_f, leaving] if p == tp - 1 else [],
    )
    last = selfs[0]
    feed_z = sum_z(sum_f)
    restored = from_groups(after(leaving, selfs[tp - 2]), per)

    dq, dkv, g0, emb, vec_c = cross_backward(
        idx, lens, b1, g1, x0, gain_c, q, kv, qo_pack, [leaving, *selfs.values()]
    )
    stage = {}

    def norms_and_small(late):
        block_out = after(restored, *late).astype(F32) + skip_latents.astype(F32)
        squares = jnp.sum(jnp.square(block_out), axis=(0, 2))
        by_share = jnp.transpose(
            jnp.concatenate([emb, vec_s[:5], vec_c[:1]]).reshape(lat_rows + 6, tp, w), (1, 0, 2)
        )
        hb_all = functools.reduce(jnp.add, hbgs).reshape(2, ff // w, w)
        owner = lax.broadcasted_iota(jnp.int32, (tp, 1, 1), 0)
        hb_share = jnp.where(owner == t, hb_all[0][None], 0.0) + jnp.where(
            owner == (t ^ 1), hb_all[1][None], 0.0
        )
        sq_rows = jnp.pad(squares, (0, norm_rows * w - groups)).reshape(1, norm_rows, w)
        x = jnp.concatenate(
            [by_share, hb_share, jnp.broadcast_to(sq_rows, (tp, norm_rows, w))], axis=1
        )
        x = jnp.pad(x, ((0, 0), (0, -x.shape[1] % 8), (0, 0)))
        for bit in reversed(range(bits_of("tp"))):
            n = x.shape[0] // 2
            mine = bit_at("tp", bit)
            keep = lax.dynamic_slice_in_dim(x, mine * n, n, 0)
            x = keep + flip(lax.dynamic_slice_in_dim(x, (1 - mine) * n, n, 0), "tp", bit)
        x = x[0].reshape(-1)
        places_rows = 2 * lax.axis_size("z") * 8
        rows_all = -(-x.shape[0] // (d * places_rows)) * places_rows
        return block_out, jnp.pad(x, (0, rows_all * d - x.shape[0])).reshape(rows_all, d).astype(BF)

    norm_rows = -(-groups // w)

    def waits(p, late):
        if p == tp - 1:
            stage["self"] = over_y(selfs, [emb])[0]
            stage["returned"] = from_groups(after(g0, *late), per)
            return [stage["self"]]
        if p == tp - 3:
            return [restored]
        if p == tp - 2:
            n = stage["self"].shape[0] // 2
            stage["self"] = [over_x(stage["self"][:n], late), over_x(stage["self"][n:], late)]
            stage["returned"] = from_groups(after(g0, *late), per)
            return stage["self"] + [feed_z]
        if p == 0:
            stage["self"] = after(jnp.concatenate(stage["self"], axis=1), *late)
            stage["out"], stage["small"] = norms_and_small(late)
            return [stage["small"], stage["returned"]]
        return []

    def cross_piece(p, came, late):
        x = cross_weights(p, w, nc, dq, oc, b1, dkv, points, came_points, came, late)
        return x[0] if p % 2 else x

    cross = pieces(cross_piece, waits)
    late = [cross[0][0]]
    self_z = sum_z(stage["self"])
    cross_a = over_y({p: v[0] for p, v in cross.items()})[0]
    cross_b = over_y({p: over_x(v[1], [feed_z]) for p, v in cross.items()})[0]
    little = over_x(stage["small"])
    keep, send = shares(cross_a)
    half = feed_z.shape[1] // 2
    feed_ox = flip_x(after(feed_z[:, :half], send))
    cross_z = jnp.concatenate([add(keep, flip_x(send)), cross_b, little], axis=1)
    cross_z = after(cross_z, self_z, feed_ox)
    feed_hx = flip_x(after(feed_z[:, half:], cross_z))
    self_x = flip_x(after(self_z, cross_z))
    cross_z = after(sum_z(cross_z), self_x)
    returned = stage["returned"]
    cross_x = flip_x(cross_z)
    n = little.shape[1]
    low = lax.axis_index("x") == 0
    own_n, other_n = cross_z[:, -n:], cross_x[:, -n:]
    total = jnp.where(low, jnp.stack([own_n, other_n], 1), jnp.stack([other_n, own_n], 1))
    total = total.astype(F32).reshape(-1)
    total = total[: total.shape[0] // w * w].reshape(-1, w)
    places = lax.axis_index("x").astype(jnp.int32).reshape(1)
    output_weight_grad, hidden_weight_grad = final_feed(places, feed_z, feed_ox, feed_hx)
    query_self_grad, key_self_grad, value_self_grad, output_self_grad = final(
        places, w, self_z, self_x
    )
    block_out = stage["out"]
    latents_grad = returned.astype(F32)

    query_cross_grad, key_cross_grad, value_cross_grad, output_cross_grad = final(
        places, w, cross_z, cross_x, [output_weight_grad, hidden_weight_grad, output_self_grad]
    )
    embed_grad = total[:lat_rows]
    (
        output_bias_grad,
        gain_mlp_grad,
        bias_self_grad,
        gain_self_grad,
        bias_cross_grad,
        gain_cross_grad,
    ) = (total[lat_rows + k] for k in range(6))
    at = lat_rows + 6
    hidden_bias_grad = total[at : at + ff // w].reshape(ff)
    at += ff // w
    square_sums = total[at : at + norm_rows].reshape(norm_rows * w)[:groups]
    group_norms = jnp.sqrt(square_sums / (lat_rows * d))

    return (
        block_out,
        group_norms,
        latents_grad,
        embed_grad,
        gain_cross_grad,
        query_cross_grad,
        key_cross_grad,
        value_cross_grad,
        output_cross_grad,
        bias_cross_grad,
        gain_self_grad,
        query_self_grad,
        key_self_grad,
        value_self_grad,
        output_self_grad,
        bias_self_grad,
        gain_mlp_grad,
        hidden_weight_grad,
        hidden_bias_grad,
        output_weight_grad,
        output_bias_grad,
    )


def solution(mesh):
    grp, tp = mesh.shape["grp"], mesh.shape["tp"]
    own = jax.sharding.Mesh(mesh.devices.reshape(grp // 2, 2, tp), GRP + ("tp",))
    lay = P(GRP, None, "tp")
    cols, rows, part = P(None, "tp"), P("tp", None), P("tp")
    attn = (P(), cols, cols, cols, rows, part)
    return jax.shard_map(
        per_device,
        mesh=own,
        in_specs=(lay, lay, P(GRP, None), P(GRP, None), P(), cols)
        + attn
        + attn
        + (P(), cols, part, rows, part, lay),
        out_specs=(lay, P(), lay, cols)
        + (part, cols, cols, cols, rows, part)
        + (part, cols, cols, cols, rows, part)
        + (part, cols, part, rows, part),
        check_vma=False,
    )
```
